128 devices in a mesh: gx: 8 (over x, core), gy: 16 (over y, z).
Axes of the slice: x: 4, y: 4, z: 4, core: 2. Of those that a mesh axis runs over, the one named last changes fastest.
Arguments:
- right_side: float32 [2, 128, 128, 128], P(None, 'gx', 'gy'), may hold values from -6 to 6
- accumulation: float32 [4, 128, 128, 128], P(None, 'gx', 'gy'), may hold values from -0.3 to 0.5, as said below
- trans_x: float32 [2, 128, 128, 128], P(None, 'gx', 'gy'), may hold values from 0.05 to 0.5
- trans_y: float32 [2, 128, 128, 128], P(None, 'gx', 'gy'), may hold values from 5 to 50
- trans_z: float32 [2, 128, 128, 128], P(None, 'gx', 'gy'), may hold values from 0.05 to 0.5
- perf_cell: int32 [8, 16, 8, 32], P('gx', 'gy'), may hold values from 0 to 16383
- perf_well: int32 [8, 16, 8, 32], P('gx', 'gy'), may hold values from 0 to 15
- perf_weight: float32 [8, 16, 8, 32], P('gx', 'gy'), may hold values from 0.05 to 2
- perf_count: int32 [8, 16, 8], P('gx', 'gy'), may hold values from 8 to 32, as said below
- breaks: int32 [128, 128], P(('gx', 'gy')), may hold values 0 or 1
Outputs:
- adjoint: float32 [2, 128, 128, 128], P(None, 'gx', 'gy')
- residual: float32 [2, 128, 128, 128], P(None, 'gx', 'gy')
The draws below stay inside these ranges and needn't reach their ends.
Inputs may be any that keep to these rules, and one draw needn't show every extreme that they name: `accumulation`: entries 00 and 11 are positive; |entry 01| <= 0.6 entry 00 and |entry 10| <= 0.6 entry 11. `perf_count`: in every draw and every second-axis index, one owner receives 32 live slots from every device.
All inputs are finite; a program needn't handle non-finite values. No bound on the sum of `breaks` on one device may be relied on, other than what follows from the above.
Results may differ from the reference program's by a relative error of at most 0.00035.
Values sent between devices are 32-bit elements; how exact they have to be, the bound alone decides.
No kernel may reach another device: no remote copies, remote signals or barrier semaphores. Data moves between devices by JAX's collectives and lax.ppermute only.
A program may use at most 64 MiB of HBM per device.

```python
import math
import jax
import jax.numpy as jnp
from jax import lax

CX = 16
CY = 8
NZ = 128
SLOTS = 32
W_DEV = 16
NX = 128
NY = 128
N_GX = 8
N_GY = 16


def draw_accumulation(key, part):
    key = jax.random.fold_in(key, 7)
    first, second = jax.random.split(key)
    spread = jax.random.uniform(first, (2, NX, NY, NZ), jnp.float32)
    diagonal = 0.05 * jnp.exp(spread * jnp.log(10.0))
    cross = jax.random.uniform(second, (2, NX, NY, NZ), jnp.float32, -0.6, 0.6)
    return jnp.stack([diagonal[0], cross[0] * diagonal[0], cross[1] * diagonal[1], diagonal[1]]).astype(jnp.float32)


def draw_perf_count(key, part):
    key = jax.random.fold_in(key, 11)
    first, second = jax.random.split(key)
    base = jax.random.randint(first, (N_GX, N_GY, N_GX), SLOTS // 4, SLOTS // 2 + 1)
    heavy = jax.random.randint(second, (N_GY,), 0, N_GX)
    full = jnp.arange(N_GX)[None, None, :] == heavy[None, :, None]
    return jnp.where(full, SLOTS, base).astype(jnp.int32)


def place_ends(entries, own_key, smallest, high):
    longest = entries.shape.index(max(entries.shape))
    spots = []
    for shift in (0, 1):
        where = [jax.random.randint(jax.random.fold_in(own_key, axis), (), 0, length) for axis, length in enumerate(entries.shape)]
        where[longest] = (where[longest] + shift) % entries.shape[longest]
        spots.append(tuple(where))
    return entries.at[spots[0]].set(smallest).at[spots[1]].set(high)


def block_scale(rng, shape, cuts, least, high):
    factor_of, own = 1.0, jax.random.fold_in(rng, 6)
    for position, blocks in cuts:
        steps = jnp.exp(jax.random.uniform(jax.random.fold_in(own, position), (blocks,), jnp.float32, least / len(cuts), high / len(cuts)))
        factor_of = factor_of * jnp.repeat(steps, shape[position] // blocks).reshape([-1 if axis == position else 1 for axis in range(len(shape))])
    return factor_of


def gaussian(stream_key, shape, width, limit, cuts=(), held_as=jnp.bfloat16):
    values = width * jax.random.normal(stream_key, shape, jnp.float32)
    if cuts:
        values = values * block_scale(stream_key, shape, cuts, -0.22, 0.18)
    return jnp.clip(values, -limit, limit).astype(held_as)


def setup_inputs(seed: int = 0) -> dict:
    seeds = jax.random.split(jax.random.key(seed), 11)
    right_side = gaussian(seeds[0], (2, NX, NY, NZ), 1.0, 6.0, ((1, 8), (2, 16)), jnp.float32)
    accumulation = draw_accumulation(jax.random.fold_in(seeds[10], 71), 0)
    trans_x = jnp.clip(jnp.exp(math.log(0.5) - 2.3025851 * jax.random.uniform(seeds[2], (2, NX, NY, NZ), jnp.float32) ** block_scale(seeds[2], (2, NX, NY, NZ), ((1, 8), (2, 16)), -0.2, 0.2)), 0.05, 0.5)
    trans_y = jnp.clip(jnp.exp(math.log(50.0) - 2.3025851 * jax.random.uniform(seeds[3], (2, NX, NY, NZ), jnp.float32) ** block_scale(seeds[3], (2, NX, NY, NZ), ((1, 8), (2, 16)), -0.2, 0.2)), 5.0, 50.0)
    trans_z = jnp.clip(jnp.exp(math.log(0.5) - 2.3025851 * jax.random.uniform(seeds[4], (2, NX, NY, NZ), jnp.float32) ** block_scale(seeds[4], (2, NX, NY, NZ), ((1, 8), (2, 16)), -0.2, 0.2)), 0.05, 0.5)
    perf_cell = place_ends(jax.random.randint(seeds[5], (N_GX, N_GY, N_GX, SLOTS), 0, CX * CY * NZ), jax.random.fold_in(seeds[5], 1), 0, (CX * CY * NZ) - 1).astype(jnp.int32)
    perf_well = place_ends(jax.random.randint(seeds[6], (N_GX, N_GY, N_GX, SLOTS), 0, W_DEV), jax.random.fold_in(seeds[6], 1), 0, W_DEV - 1).astype(jnp.int32)
    perf_weight = jnp.clip(jnp.exp(math.log(2.0) - 3.6888794 * jax.random.uniform(seeds[7], (N_GX, N_GY, N_GX, SLOTS), jnp.float32) ** block_scale(seeds[7], (N_GX, N_GY, N_GX, SLOTS), ((0, 8), (1, 16)), -0.2, 0.2)), 0.05, 2.0)
    perf_count = draw_perf_count(jax.random.fold_in(seeds[10], 71), 0)
    breaks = place_ends((jax.random.randint(seeds[9], (NX, NY), 0, 256) < 1).astype(jnp.int32), jax.random.fold_in(seeds[9], 1), 0, 1)
    return dict(right_side=right_side, accumulation=accumulation, trans_x=trans_x, trans_y=trans_y, trans_z=trans_z, perf_cell=perf_cell, perf_well=perf_well, perf_weight=perf_weight, perf_count=perf_count, breaks=breaks)


def shift_down(a, s):
    return jnp.concatenate([jnp.zeros_like(a[..., :s, :]), a[..., :-s, :]], axis=-2)


def shift_up(a, s):
    return jnp.concatenate([a[..., s:, :], jnp.zeros_like(a[..., :s, :])], axis=-2)


def mul_block(p, q):
    return jnp.stack([jnp.stack([p[0, 0] * q[0, 0] + p[0, 1] * q[1, 0], p[0, 0] * q[0, 1] + p[0, 1] * q[1, 1]]),
                      jnp.stack([p[1, 0] * q[0, 0] + p[1, 1] * q[1, 0], p[1, 0] * q[0, 1] + p[1, 1] * q[1, 1]])])


def apply_block(p, v):
    return jnp.stack([p[0, 0] * v[0] + p[0, 1] * v[1], p[1, 0] * v[0] + p[1, 1] * v[1]])


def invert_block(p):
    determ = p[0, 0] * p[1, 1] - p[0, 1] * p[1, 0]
    return jnp.stack([jnp.stack([p[1, 1], -p[0, 1]]), jnp.stack([-p[1, 0], p[0, 0]])]) / determ


def diag_block(d):
    zero = jnp.zeros_like(d[0])
    return jnp.stack([jnp.stack([d[0], zero]), jnp.stack([zero, d[1]])])


def line_solve(center, lower, upper, rhs):
    below = diag_block(lower)
    above = diag_block(upper)
    length = rhs.shape[-2]
    stride = 1
    while stride < length:
        inverse = invert_block(center)
        alpha = -mul_block(below, shift_down(inverse, stride))
        gamma = -mul_block(above, shift_up(inverse, stride))
        center = center + mul_block(alpha, shift_down(above, stride)) + mul_block(gamma, shift_up(below, stride))
        new_below = mul_block(alpha, shift_down(below, stride))
        new_above = mul_block(gamma, shift_up(above, stride))
        rhs = rhs + apply_block(alpha, shift_down(rhs, stride)) + apply_block(gamma, shift_up(rhs, stride))
        below, above = new_below, new_above
        stride = stride * 2
    return apply_block(invert_block(center), rhs)


def well_term(pressure, perf_cell, perf_well, perf_weight, perf_count):
    tiles = pressure.reshape(N_GX, CX, N_GY, CY, NZ).transpose(0, 2, 1, 3, 4).reshape(N_GX, N_GY, CX * CY * NZ)
    cells = perf_cell.reshape(N_GX, N_GY, N_GX * SLOTS)
    values = jnp.take_along_axis(tiles, cells, axis=2).reshape(N_GX, N_GY, N_GX, SLOTS)
    live = (jnp.arange(SLOTS)[None, None, None, :] < perf_count[..., None]).astype(jnp.float32)
    weights = perf_weight * live
    onehot = (perf_well[..., None] == jnp.arange(W_DEV)[None, None, None, None, :]).astype(jnp.float32)
    hp = lax.Precision.HIGHEST
    sums = jnp.einsum('sgdk,sgdkw->gdw', weights * values, onehot, precision=hp)
    totals = jnp.maximum(jnp.einsum('sgdk,sgdkw->gdw', weights, onehot, precision=hp), 1.0)
    rates = sums / totals
    slot_rate = jnp.einsum('sgdkw,gdw->sgdk', onehot, rates, precision=hp)
    added = (weights * slot_rate).reshape(N_GX, N_GY, N_GX * SLOTS)
    source = jnp.arange(N_GX)[:, None, None]
    column = jnp.arange(N_GY)[None, :, None]
    tiles_add = jnp.zeros((N_GX, N_GY, CX * CY * NZ), jnp.float32).at[source, column, cells].add(added)
    return tiles_add.reshape(N_GX, N_GY, CX, CY, NZ).transpose(0, 2, 1, 3, 4).reshape(NX, NY, NZ)


def reference(right_side, accumulation, trans_x, trans_y, trans_z, perf_cell, perf_well, perf_weight, perf_count, breaks):
    tx = trans_x * (jnp.arange(NX) < NX - 1).astype(jnp.float32)[None, :, None, None]
    ty = trans_y * (jnp.arange(NY) < NY - 1).astype(jnp.float32)[None, None, :, None]
    tz = trans_z * (jnp.arange(NZ) < NZ - 1).astype(jnp.float32)[None, None, None, :]
    lx = jnp.concatenate([jnp.zeros_like(tx[:, :1]), tx[:, :-1]], axis=1)
    ly = jnp.concatenate([jnp.zeros_like(ty[:, :, :1]), ty[:, :, :-1]], axis=2)
    lz = jnp.concatenate([jnp.zeros_like(tz[..., :1]), tz[..., :-1]], axis=3)
    faces = tx + lx + ty + ly + tz + lz
    d00 = accumulation[0] + faces[0]
    d01 = accumulation[2]
    d10 = accumulation[1]
    d11 = accumulation[3] + faces[1]

    def operate(field):
        padded = jnp.pad(field, ((0, 0), (1, 1), (1, 1), (1, 1)))
        beside = tx * padded[:, 2:, 1:-1, 1:-1] + lx * padded[:, :-2, 1:-1, 1:-1]
        beside = beside + ty * padded[:, 1:-1, 2:, 1:-1] + ly * padded[:, 1:-1, :-2, 1:-1]
        beside = beside + tz * padded[:, 1:-1, 1:-1, 2:] + lz * padded[:, 1:-1, 1:-1, :-2]
        first = d00 * field[0] + d01 * field[1] - beside[0]
        first = first + well_term(field[0], perf_cell, perf_well, perf_weight, perf_count)
        second = d10 * field[0] + d11 * field[1] - beside[1]
        return jnp.stack([first, second])

    center = jnp.stack([jnp.stack([d00, d01]), jnp.stack([d10, d11])])
    keep = (1.0 - breaks.astype(jnp.float32))[None, :, :, None]
    lower = -shift_down(ty, 1) * keep
    upper = -ty * shift_up(keep, 1)

    def precondition(vector):
        def one_row(index):
            return line_solve(center[:, :, index], lower[:, index], upper[:, index], vector[:, index])

        rows = lax.map(one_row, jnp.arange(NX))
        return jnp.transpose(rows, (1, 0, 2, 3))

    p_one = precondition(right_side)
    q_one = operate(p_one)
    qq_one = jnp.sum(q_one * q_one)
    a_one = jnp.sum(right_side * q_one) / qq_one
    adjoint = a_one * p_one
    resid = right_side - a_one * q_one
    p_two = precondition(resid)
    q_two = operate(p_two)
    beta = jnp.sum(q_two * q_one) / qq_one
    p_two = p_two - beta * p_one
    q_two = q_two - beta * q_one
    a_two = jnp.sum(resid * q_two) / jnp.sum(q_two * q_two)
    adjoint = adjoint + a_two * p_two
    resid = resid - a_two * q_two
    return adjoint, resid
```

```python
import jax
import jax.numpy as jnp
from jax import lax
from jax.experimental import pallas as pl
from jax.experimental.pallas import tpu as pltpu
from jax.sharding import PartitionSpec as P

F32 = jnp.float32
BF16 = jnp.bfloat16
VMEM = pl.BlockSpec(memory_space=pltpu.VMEM)
SMEM = pl.BlockSpec(memory_space=pltpu.SMEM)
CX, CY, NZ = 16, 8, 128
PLANE = (CX, NZ)
N_GX, N_GY = 8, 16
W_ALL = 128
SLOTS_ALL = 256


def mm(p, q):
    return (
        p[0] * q[0] + p[1] * q[2],
        p[0] * q[1] + p[1] * q[3],
        p[2] * q[0] + p[3] * q[2],
        p[2] * q[1] + p[3] * q[3],
    )


def mv(p, v):
    return (p[0] * v[0] + p[1] * v[1], p[2] * v[0] + p[3] * v[1])


def madd(p, q):
    return tuple(a + b for a, b in zip(p, q))


def inv2(p):
    t = 1.0 / (p[0] * p[3] - p[1] * p[2])
    return (p[3] * t, -p[1] * t, -p[2] * t, p[0] * t)


def one_minus(p):
    return (1.0 - p[0], -p[1], -p[2], 1.0 - p[3])


def rows_by(t, p):
    return (t[0] * p[0], t[0] * p[1], t[1] * p[2], t[1] * p[3])


def columns_by(p, t):
    return (p[0] * t[0], p[1] * t[1], p[2] * t[0], p[3] * t[1])


def join(a, b):
    ff1, fl1, lf1, ll1, gf1, gl1 = a
    ff2, fl2, lf2, ll2, gf2, gl2 = b
    k = inv2(one_minus(mm(ll1, ff2)))
    last = mv(k, madd(gl1, mv(ll1, gf2)))
    last_b = mm(k, lf1)
    last_a = mm(k, mm(ll1, fl2))
    first = madd(gf2, mv(ff2, last))
    first_b = mm(ff2, last_b)
    first_a = madd(fl2, mm(ff2, last_a))
    return (
        madd(ff1, mm(fl1, first_b)),
        mm(fl1, first_a),
        mm(lf2, last_b),
        madd(ll2, mm(lf2, last_a)),
        madd(gf1, mv(fl1, first)),
        madd(gl2, mv(lf2, last)),
    )


def join_before(before, s):
    gm, g = before
    ff, fl, lf, ll, gf, gl = s
    k = inv2(one_minus(mm(ff, gm)))
    a = mv(k, madd(gf, mv(ff, g)))
    am = mm(k, fl)
    return (madd(ll, mm(lf, mm(gm, am))), madd(gl, mv(lf, madd(g, mv(gm, a)))))


def join_after(s, after):
    gm, g = after
    ff, fl, lf, ll, gf, gl = s
    k = inv2(one_minus(mm(ll, gm)))
    a = mv(k, madd(gl, mv(ll, g)))
    am = mm(k, lf)
    return (madd(ff, mm(fl, mm(gm, am))), madd(gf, mv(fl, madd(g, mv(gm, a)))))


def choose(flag, new, old):
    return tuple(tuple(jnp.where(flag, n, o) for n, o in zip(ns, os)) for ns, os in zip(new, old))


def load_segment(mat, vec, offset):
    m = [mat[i] for i in range(16)]
    v = [vec[offset + i] for i in range(4)]
    return (tuple(m[0:4]), tuple(m[4:8]), tuple(m[8:12]), tuple(m[12:16]), (v[0], v[1]), (v[2], v[3]))


def store_segment(ref, seg, whole):
    flat = [x for part in seg for x in part]
    if not whole:
        flat = flat[16:]
    for i, x in enumerate(flat):
        ref[i] = x


def lanes():
    return lax.broadcasted_iota(jnp.int32, PLANE, 1)


def rows():
    return lax.broadcasted_iota(jnp.int32, PLANE, 0)


def from_row_before(plane, edge):
    return jnp.where(rows() == 0, edge, pltpu.roll(plane, 1, 0))


def from_row_after(plane, edge):
    return jnp.where(rows() == CX - 1, edge, pltpu.roll(plane, CX - 1, 0))


def sweep_forward(sinv, tau, rhs):
    y = [rhs[0]]
    for j in range(1, CY):
        t = mv(sinv(j - 1), y[-1])
        y.append((rhs[j][0] + tau(j)[0] * t[0], rhs[j][1] + tau(j)[1] * t[1]))
    return y


def sweep_backward(binv, tau, rhs):
    z = rhs[CY - 1]
    for j in range(CY - 2, -1, -1):
        t = mv(binv(j + 1), z)
        z = (rhs[j][0] + tau(j + 1)[0] * t[0], rhs[j][1] + tau(j + 1)[1] * t[1])
    return z


def block_at(ref, j):
    return tuple(ref[i, j] for i in range(4))


def pair_at(ref, j):
    return (ref[0, j], ref[1, j])


def condense_kernel(idx, b, acc, tx_in, ty_in, tz_in, lx_in, ly_in, brk, seg, dmat, tau_o, sinv, binv, rhs, tx_o, ty_o, tz_o):
    gx, gy = idx[0], idx[1]
    last_x = jnp.logical_and(rows() == CX - 1, gx == N_GX - 1)
    last_z = lanes() == NZ - 1

    def plane(ref, c, j):
        return ref.at[c][pl.ds(j, CX, stride=CY), :]

    for c in range(2):
        ty_o[c, 0] = ly_in[c]
        for j in range(CY):
            tx = jnp.where(last_x, 0.0, plane(tx_in, c, j))
            tz = jnp.where(last_z, 0.0, plane(tz_in, c, j))
            ty = plane(ty_in, c, j)
            if j == CY - 1:
                ty = jnp.where(gy == N_GY - 1, 0.0, ty)
            tx_o[c, j] = tx
            tz_o[c, j] = tz
            ty_o[c, j + 1] = ty
            lx = from_row_before(tx, lx_in[c, j : j + 1, :])
            faces = tx + lx + ty + ty_o[c, j] + tz + pltpu.roll(tz, 1, 1)
            dmat[3 * c, j] = plane(acc, 3 * c, j) + faces
            rhs[c, j] = plane(b, c, j)
        for j in range(CY + 1):
            keep = 1.0 - brk[:, j : j + 1].astype(F32)
            tau_o[c, j] = ty_o[c, j] * keep
    for j in range(CY):
        dmat[1, j] = plane(acc, 2, j)
        dmat[2, j] = plane(acc, 1, j)

    def tau(j):
        return pair_at(tau_o, j)

    def outer(t, p):
        return tuple(x * y for x, y in zip(p, (t[0] * t[0], t[0] * t[1], t[1] * t[0], t[1] * t[1])))

    s = inv2(block_at(dmat, 0))
    e = inv2(block_at(dmat, CY - 1))
    zero = jnp.zeros(PLANE, F32)
    yf = (tau(0)[0], zero, zero, tau(0)[1])
    zl = (tau(CY)[0], zero, zero, tau(CY)[1])
    y = pair_at(rhs, 0)
    z = pair_at(rhs, CY - 1)
    for i in range(4):
        sinv[i, 0] = s[i]
        binv[i, CY - 1] = e[i]
    for j in range(1, CY):
        k = CY - 1 - j
        t, u = tau(j), tau(k + 1)
        yf = rows_by(t, mm(s, yf))
        zl = rows_by(u, mm(e, zl))
        yv, zv = mv(s, y), mv(e, z)
        y = tuple(rhs[c, j] + t[c] * yv[c] for c in range(2))
        z = tuple(rhs[c, k] + u[c] * zv[c] for c in range(2))
        s = inv2(tuple(d - x for d, x in zip(block_at(dmat, j), outer(t, s))))
        e = inv2(tuple(d - x for d, x in zip(block_at(dmat, k), outer(u, e))))
        for i in range(4):
            sinv[i, j] = s[i]
            binv[i, k] = e[i]
    store_segment(
        seg,
        (columns_by(e, tau(0)), mm(e, zl), mm(s, yf), columns_by(s, tau(CY)), mv(e, z), mv(s, y)),
        True,
    )


def gather_segments(position, mats, vecs, offset, mat_s, vec_s):
    for k in range(4):
        at = jnp.bitwise_xor(position, k)
        mat_s[at] = mats[k][0:16]
        vec_s[at] = vecs[k][offset : offset + 4]


def make_total_kernel(whole):
    def kernel(*refs):
        idx = refs[0]
        if whole:
            mats = vecs = refs[1:5]
            out, mat_s, vec_s = refs[5:]
        else:
            mats, vecs = refs[1:5], refs[5:9]
            out, mat_s, vec_s = refs[9:]
        gather_segments(idx[1] % 4, mats, vecs, 16 if whole else 0, mat_s, vec_s)
        segs = [load_segment(mat_s.at[m], vec_s.at[m], 0) for m in range(4)]
        store_segment(out, join(join(segs[0], segs[1]), join(segs[2], segs[3])), whole)

    return kernel


def split3(x):
    hi = x.astype(BF16)
    rest = x - hi.astype(F32)
    mid = rest.astype(BF16)
    low = (rest - mid.astype(F32)).astype(BF16)
    return hi, mid, low


def slot_tables(cells, wells):
    cell = cells[...]
    row = jnp.bitwise_and(lax.shift_right_logical(cell, 7), 7) * CX + lax.shift_right_logical(cell, 10)
    shape = (NZ, SLOTS_ALL)
    up = lax.broadcasted_iota(jnp.int32, shape, 0)
    at_row = up == row
    at_layer = up == jnp.bitwise_and(cell, NZ - 1)
    at_well = up == wells[...]
    return at_row, at_layer, at_well


def ones_of(mask):
    return jnp.where(mask, 1.0, 0.0).astype(F32).astype(BF16)


NT = (((1,), (1,)), ((), ()))


def row_times(rows_in, table, dims):
    parts = [part for x in rows_in for part in split3(x)]
    n = len(rows_in)
    pad = 16 - 3 * n
    width = rows_in[0].shape[1]
    stacked = jnp.concatenate([p.astype(F32) for p in parts] + [jnp.zeros((pad, width), F32)], axis=0).astype(BF16)
    out = lax.dot_general(stacked, table, dims, preferred_element_type=F32)
    return [out[3 * i : 3 * i + 1] + out[3 * i + 1 : 3 * i + 2] + out[3 * i + 2 : 3 * i + 3] for i in range(n)]


def make_solve_kernel(whole):
    def kernel(*refs):
        idx = refs[0]
        if whole:
            inner, outer_ = refs[1:5], refs[5:9]
            inner_v, outer_v = inner, outer_
            rest = refs[9:]
            offset = 16
        else:
            inner, outer_, inner_v, outer_v = refs[1:5], refs[5:9], refs[9:13], refs[13:17]
            rest = refs[17:]
            offset = 0
        sinv, tau_r, rhs, cells, wells, weights = rest[:6]
        p_out, ends, msg = rest[6:9]
        mat_i, vec_i, mat_o, vec_o, edge = rest[9:]
        gx, gy = idx[0], idx[1]
        z_at, y_at = gy % 4, gy // 4
        gather_segments(z_at, inner, inner_v, offset, mat_i, vec_i)
        gather_segments(y_at, outer_, outer_v, offset, mat_o, vec_o)
        zero = jnp.zeros(PLANE, F32)
        before = ((zero,) * 4, (zero,) * 2)
        after = ((zero,) * 4, (zero,) * 2)
        for mat_s, vec_s, here in ((mat_o, vec_o, y_at), (mat_i, vec_i, z_at)):
            for m in range(3):
                seg = load_segment(mat_s.at[m], vec_s.at[m], 0)
                before = choose(m < here, join_before(before, seg), before)
                m = 3 - m
                seg = load_segment(mat_s.at[m], vec_s.at[m], 0)
                after = choose(m > here, join_after(seg, after), after)
        own = load_segment(inner[0], inner_v[0], offset)
        ff, fl, lf, ll, gf, gl = own
        up_m, up_v = join_before(before, own)
        last = mv(inv2(one_minus(mm(up_m, after[0]))), madd(up_v, mv(up_m, after[1])))
        beyond = madd(after[1], mv(after[0], last))
        k = inv2(one_minus(mm(ff, before[0])))
        first = mv(k, madd(madd(gf, mv(ff, before[1])), mv(fl, beyond)))
        behind = madd(before[1], mv(before[0], first))
        for c in range(2):
            ends[c] = behind[c]
            ends[2 + c] = beyond[c]

        def tau(j):
            return pair_at(tau_r, j)

        def sv(j):
            return block_at(sinv, j)

        r = [pair_at(rhs, j) for j in range(CY)]
        r[0] = tuple(r[0][c] + tau(0)[c] * behind[c] for c in range(2))
        y = sweep_forward(sv, tau, r)
        u = beyond
        for j in range(CY - 1, -1, -1):
            u = mv(sv(j), tuple(y[j][c] + tau(j + 1)[c] * u[c] for c in range(2)))
            for c in range(2):
                p_out[c, j] = u[c]
                edge[0, c * CY + j : c * CY + j + 1, :] = u[c][0:1, :]
                edge[1, c * CY + j : c * CY + j + 1, :] = u[c][CX - 1 : CX, :]
        at_row, at_layer, at_well = slot_tables(cells, wells)
        pressure = jnp.concatenate([p_out[0, j] for j in range(CY)], axis=0)
        table = ones_of(at_layer)
        picked = sum(jnp.dot(part, table, preferred_element_type=F32) for part in split3(pressure))
        values = jnp.sum(jnp.where(at_row, picked, 0.0), axis=0, keepdims=True)
        w = weights[...]
        sums, totals = row_times([w * values, w], ones_of(at_well), NT)
        tail = jnp.concatenate([sums, totals, jnp.zeros((6, W_ALL), F32)], axis=0)
        for d in range(N_GX):
            msg[d, 0:16, :] = jnp.zeros((16, NZ), F32)
            msg[d, 16:24, :] = tail

        @pl.when(gx < N_GX - 1)
        def _():
            msg[gx + 1, 0:16, :] = edge[1]

        @pl.when(gx > 0)
        def _():
            msg[gx - 1, 0:16, :] = edge[0]

    return kernel


def apply_operator(idx, got, p, ends, dmat, tx, ty, tz, cells, wells, weights):
    gx = idx[0]
    tail = got[0, 16:24, :]
    for d in range(1, N_GX):
        tail = tail + got[d, 16:24, :]
    rates = tail[0:1] / jnp.maximum(tail[1:2], 1.0)
    at_row, at_layer, at_well = slot_tables(cells, wells)
    slot_rate = row_times([rates], ones_of(at_well), (((1,), (0,)), ((), ())))[0]
    added = jnp.where(at_layer, weights[...] * slot_rate, 0.0)
    table = ones_of(at_row)
    well_add = sum(lax.dot_general(table, part, NT, preferred_element_type=F32) for part in split3(added))
    from_after = jnp.where(gx < N_GX - 1, got[jnp.minimum(gx + 1, N_GX - 1), 0:16, :], 0.0)
    from_before = jnp.where(gx > 0, got[jnp.maximum(gx - 1, 0), 0:16, :], 0.0)
    return well_add, from_after, from_before


def operator_plane(c, j, p, ends, dmat, tx, ty, tz, lx_in, halo, well_add):
    from_after, from_before = halo
    here = p[c, j]
    up = p[c, j + 1] if j < CY - 1 else ends[2 + c]
    down = p[c, j - 1] if j > 0 else ends[c]
    t = tx[c, j]
    at = c * CY + j
    beside = t * from_row_after(here, from_after[at : at + 1])
    beside = beside + from_row_before(t * here, lx_in[c, j : j + 1, :] * from_before[at : at + 1])
    beside = beside + ty[c, j + 1] * up + ty[c, j] * down
    tzp = tz[c, j]
    beside = beside + tzp * pltpu.roll(here, NZ - 1, 1) + pltpu.roll(tzp * here, 1, 1)
    out = dmat[2 * c, j] * p[0, j] + dmat[2 * c + 1, j] * p[1, j] - beside
    if c == 0:
        out = out + well_add[j * CX : (j + 1) * CX]
    return out


def first_image_kernel(idx, got, p, ends, dmat, tau_r, sinv, binv, rhs, tx, ty, tz, lx_in, cells, wells, weights, q_out, e_out, vec_out, dots):
    well_add, after, before = apply_operator(idx, got, p, ends, dmat, tx, ty, tz, cells, wells, weights)
    eq = jnp.zeros(PLANE, F32)
    qq = jnp.zeros(PLANE, F32)
    e = []
    for j in range(CY):
        pair = []
        for c in range(2):
            q = operator_plane(c, j, p, ends, dmat, tx, ty, tz, lx_in, (after, before), well_add)
            rest = rhs[c, j] - q
            q_out[c, j] = q
            e_out[c, j] = rest
            eq = eq + rest * q
            qq = qq + q * q
            pair.append(rest)
        e.append(tuple(pair))
    dots[0] = eq
    dots[1] = qq

    def tau(j):
        return pair_at(tau_r, j)

    y = sweep_forward(lambda j: block_at(sinv, j), tau, e)[CY - 1]
    z = sweep_backward(lambda j: block_at(binv, j), tau, e)
    first = mv(block_at(binv, 0), z)
    last = mv(block_at(sinv, CY - 1), y)
    for c in range(2):
        vec_out[c] = first[c]
        vec_out[2 + c] = last[c]


def second_image_kernel(idx, got, p, ends, dmat, tx, ty, tz, lx_in, cells, wells, weights, q_in, e_in, dots_in, s_out, dots):
    well_add, after, before = apply_operator(idx, got, p, ends, dmat, tx, ty, tz, cells, wells, weights)
    sq = jnp.zeros(PLANE, F32)
    ss = jnp.zeros(PLANE, F32)
    es = jnp.zeros(PLANE, F32)
    for j in range(CY):
        for c in range(2):
            s = operator_plane(c, j, p, ends, dmat, tx, ty, tz, lx_in, (after, before), well_add)
            s_out[c, j] = s
            sq = sq + s * q_in[c, j]
            ss = ss + s * s
            es = es + s * e_in[c, j]
    sums = [jnp.sum(x, axis=0, keepdims=True) for x in (dots_in[0], dots_in[1], sq, ss, es)]
    block = jnp.concatenate(sums + [jnp.zeros((3, NZ), F32)], axis=0)
    for d in range(N_GX):
        dots[d] = block


def finish_kernel(got, p, w, q, e, s, x_out, r_out):
    total = got[0]
    for d in range(1, N_GY):
        total = total + got[d]
    total = jnp.broadcast_to(jnp.sum(total, axis=1, keepdims=True), (8, NZ))
    eq, qq, sq, ss, es = (total[i : i + 1] for i in range(5))
    rest = -eq / qq
    g = sq / qq
    k = (es - g * eq) / (ss - g * sq)
    on_p = (1.0 - rest) - k * g
    on_q = rest + k * g
    for c in range(2):
        for j in range(CY):
            at = pl.ds(j, CX, stride=CY)
            x_out.at[c][at, :] = on_p * p[c, j] + k * w[c, j]
            r_out.at[c][at, :] = e[c, j] + on_q * q[c, j] - k * s[c, j]


def call(kernel, name, outs, scratch, *args, smem=1):
    return pl.pallas_call(
        kernel,
        name=name,
        out_shape=tuple(jax.ShapeDtypeStruct(o, F32) for o in outs),
        in_specs=[SMEM] * smem + [VMEM] * (len(args) - smem),
        out_specs=tuple(VMEM for _ in outs),
        scratch_shapes=[pltpu.VMEM(s, F32) for s in scratch],
        compiler_params=pltpu.CompilerParams(vmem_limit_bytes=24 * 1024 * 1024),
    )(*args)


def swapped(block, stride):
    return [block] + [lax.ppermute(block, "gy", [(i, i ^ (k * stride)) for i in range(N_GY)]) for k in (1, 2, 3)]


def body(right_side, accumulation, trans_x, trans_y, trans_z, perf_cell, perf_well, perf_weight, perf_count, breaks):
    gx, gy = lax.axis_index("gx"), lax.axis_index("gy")
    idx = jnp.stack([gx, gy]).astype(jnp.int32)
    cuts = breaks.reshape(N_GY, CY)
    beyond = jnp.concatenate([cuts[1:, :1], jnp.zeros((1, 1), cuts.dtype)], axis=0)
    cuts = jnp.concatenate([cuts, beyond], axis=1)
    cuts = lax.all_to_all(cuts, "gy", split_axis=0, concat_axis=0, tiled=True)
    lx = lax.ppermute(trans_x[:, -1], "gx", [(i, i + 1) for i in range(N_GX - 1)])
    ly = lax.ppermute(trans_y[:, :, -1], "gy", [(i, i + 1) for i in range(N_GY - 1)])
    slots = perf_cell.shape[3]
    live = jnp.arange(slots, dtype=jnp.int32)[None, :] < perf_count.reshape(N_GX, 1)
    weights = jnp.where(live, perf_weight.reshape(N_GX, slots), 0.0).reshape(1, SLOTS_ALL)
    owners = jnp.arange(N_GX, dtype=jnp.int32)[:, None] * 16
    wells = (perf_well.reshape(N_GX, slots) + owners).reshape(1, SLOTS_ALL)
    cells = perf_cell.reshape(1, SLOTS_ALL)

    def flat(a):
        return a.reshape(a.shape[0], CX * CY, NZ)

    field, block, part = (2, CY, CX, NZ), (4, CY, CX, NZ), (2, CY + 1, CX, NZ)
    seg, vec = (20, CX, NZ), (4, CX, NZ)
    message = (N_GX, 24, NZ)
    order = [(4, 16, CX, NZ), (4, 4, CX, NZ)]
    own, dmat, tau, sinv, binv, rhs, tx, ty, tz = call(
        condense_kernel, "condense",
        (seg, block, part, block, block, field, field, part, field), [],
        idx, flat(right_side), flat(accumulation), flat(trans_x), flat(trans_y), flat(trans_z), lx, ly, cuts,
    )
    perfs = (cells, wells, weights)
    inner = swapped(own, 1)
    (group,) = call(make_total_kernel(True), "group_total", (seg,), order, idx, *inner)
    outer = swapped(group, 4)
    solve_scratch = order + order + [(2, 16, NZ)]
    p, ends, msg = call(
        make_solve_kernel(True), "solve_first", (field, vec, message), solve_scratch,
        idx, *inner, *outer, sinv, tau, rhs, *perfs,
    )
    got = lax.all_to_all(msg, "gx", split_axis=0, concat_axis=0, tiled=True)
    q, e, own_v, dots = call(
        first_image_kernel, "first_image", (field, field, vec, (2, CX, NZ)), [],
        idx, got, p, ends, dmat, tau, sinv, binv, rhs, tx, ty, tz, lx, *perfs,
    )
    inner_v = swapped(own_v, 1)
    (group_v,) = call(make_total_kernel(False), "group_total_again", (vec,), order, idx, *inner, *inner_v)
    outer_v = swapped(group_v, 4)
    w, ends, msg = call(
        make_solve_kernel(False), "solve_second", (field, vec, message), solve_scratch,
        idx, *inner, *outer, *inner_v, *outer_v, sinv, tau, e, *perfs,
    )
    got = lax.all_to_all(msg, "gx", split_axis=0, concat_axis=0, tiled=True)
    s, dots = call(
        second_image_kernel, "second_image", (field, (N_GX, 8, NZ)), [],
        idx, got, w, ends, dmat, tx, ty, tz, lx, *perfs, q, e, dots,
    )
    dots = lax.all_to_all(dots, "gx", split_axis=0, concat_axis=0, tiled=True)
    dots = jnp.broadcast_to(jnp.sum(dots, axis=0)[None], (N_GY, 8, NZ))
    dots = lax.all_to_all(dots, "gy", split_axis=0, concat_axis=0, tiled=True)
    flat_out = (2, CX * CY, NZ)
    x, r = call(finish_kernel, "finish", (flat_out, flat_out), [], dots, p, w, q, e, s, smem=0)
    shape = (2, CX, CY, NZ)
    return x.reshape(shape), r.reshape(shape)


def solution(mesh):
    tile = P(None, "gx", "gy", None)
    slots = P("gx", "gy", None, None)
    return jax.shard_map(
        body,
        mesh=mesh,
        in_specs=(tile,) * 5 + (slots,) * 3 + (P("gx", "gy", None), P(("gx", "gy"), None)),
        out_specs=(tile, tile),
        check_vma=False,
    )
```

```python
import jax
import jax.numpy as jnp
from jax import lax
from jax.experimental import pallas as pl
from jax.experimental.pallas import tpu as pltpu
from jax.sharding import PartitionSpec as P

F32 = jnp.float32
BF16 = jnp.bfloat16
VMEM = pl.BlockSpec(memory_space=pltpu.VMEM)
HBM = pl.BlockSpec(memory_space=pltpu.HBM)
SMEM = pl.BlockSpec(memory_space=pltpu.SMEM)
CX, CY, NZ = 16, 8, 128
PLANE = (CX, NZ)
N_GX, N_GY = 8, 16
W_ALL = 128
PREPARE_VMEM = 54400
SLOTS_ALL = 256


def mm(p, q):
    return (
        p[0] * q[0] + p[1] * q[2],
        p[0] * q[1] + p[1] * q[3],
        p[2] * q[0] + p[3] * q[2],
        p[2] * q[1] + p[3] * q[3],
    )


def mv(p, v):
    return (p[0] * v[0] + p[1] * v[1], p[2] * v[0] + p[3] * v[1])


def madd(p, q):
    return tuple(a + b for a, b in zip(p, q))


def inv2(p):
    t = 1.0 / (p[0] * p[3] - p[1] * p[2])
    return (p[3] * t, -p[1] * t, -p[2] * t, p[0] * t)


def one_minus(p):
    return (1.0 - p[0], -p[1], -p[2], 1.0 - p[3])


def rows_by(t, p):
    return (t[0] * p[0], t[0] * p[1], t[1] * p[2], t[1] * p[3])


def columns_by(p, t):
    return (p[0] * t[0], p[1] * t[1], p[2] * t[0], p[3] * t[1])


def join(a, b):
    ff1, fl1, lf1, ll1, gf1, gl1 = a
    ff2, fl2, lf2, ll2, gf2, gl2 = b
    k = inv2(one_minus(mm(ll1, ff2)))
    last = mv(k, madd(gl1, mv(ll1, gf2)))
    last_b = mm(k, lf1)
    last_a = mm(k, mm(ll1, fl2))
    first = madd(gf2, mv(ff2, last))
    first_b = mm(ff2, last_b)
    first_a = madd(fl2, mm(ff2, last_a))
    return (
        madd(ff1, mm(fl1, first_b)),
        mm(fl1, first_a),
        mm(lf2, last_b),
        madd(ll2, mm(lf2, last_a)),
        madd(gf1, mv(fl1, first)),
        madd(gl2, mv(lf2, last)),
    )


def join_before(before, s):
    gm, g = before
    ff, fl, lf, ll, gf, gl = s
    k = inv2(one_minus(mm(ff, gm)))
    a = mv(k, madd(gf, mv(ff, g)))
    am = mm(k, fl)
    return (madd(ll, mm(lf, mm(gm, am))), madd(gl, mv(lf, madd(g, mv(gm, a)))))


def join_after(s, after):
    gm, g = after
    ff, fl, lf, ll, gf, gl = s
    k = inv2(one_minus(mm(ll, gm)))
    a = mv(k, madd(gl, mv(ll, g)))
    am = mm(k, lf)
    return (madd(ff, mm(fl, mm(gm, am))), madd(gf, mv(fl, madd(g, mv(gm, a)))))


def choose(flag, new, old):
    return tuple(tuple(jnp.where(flag, n, o) for n, o in zip(ns, os)) for ns, os in zip(new, old))


def load_segment(mat, vec, offset):
    m = [mat[i] for i in range(16)]
    v = [vec[offset + i] for i in range(4)]
    return (tuple(m[0:4]), tuple(m[4:8]), tuple(m[8:12]), tuple(m[12:16]), (v[0], v[1]), (v[2], v[3]))


def store_segment(ref, seg, whole):
    flat = [x for part in seg for x in part]
    if not whole:
        flat = flat[16:]
    for i, x in enumerate(flat):
        ref[i] = x


def lanes():
    return lax.broadcasted_iota(jnp.int32, PLANE, 1)


def rows():
    return lax.broadcasted_iota(jnp.int32, PLANE, 0)


def from_row_before(plane, edge):
    return jnp.where(rows() == 0, edge, pltpu.roll(plane, 1, 0))


def from_row_after(plane, edge):
    return jnp.where(rows() == CX - 1, edge, pltpu.roll(plane, CX - 1, 0))


def sweep_forward(sinv, tau, rhs):
    y = [rhs[0]]
    for j in range(1, CY):
        t = mv(sinv(j - 1), y[-1])
        y.append((rhs[j][0] + tau(j)[0] * t[0], rhs[j][1] + tau(j)[1] * t[1]))
    return y


def sweep_backward(binv, tau, rhs):
    z = rhs[CY - 1]
    for j in range(CY - 2, -1, -1):
        t = mv(binv(j + 1), z)
        z = (rhs[j][0] + tau(j + 1)[0] * t[0], rhs[j][1] + tau(j + 1)[1] * t[1])
    return z


def block_at(ref, j):
    return tuple(ref[i, j] for i in range(4))


def pair_at(ref, j):
    return (ref[0, j], ref[1, j])


def plane(ref, c, j):
    return ref.at[c][pl.ds(j, CX, stride=CY), :]


def prepare_kernel(idx, b_h, acc_h, tx_h, ty_h, tz_h, rhs, tx_o, ty_o, tz_o, diag, cross, sx, sy, b, acc, tx_v, ty_v, tz_v, sems):
    gx, gy = idx[0], idx[1]
    pairs = ((tx_h, tx_v), (ty_h, ty_v), (tz_h, tz_v), (acc_h, acc), (b_h, b))
    copies = [pltpu.make_async_copy(h, v, sems.at[i]) for i, (h, v) in enumerate(pairs)]
    for copy in copies:
        copy.start()
    last_x = jnp.logical_and(rows() == CX - 1, gx == N_GX - 1)
    last_z = lanes() == NZ - 1
    for copy in copies:
        copy.wait()
    for c in range(2):
        sx[c] = tx_v[c, (CX - 1) * CY : CX * CY, :]
        sy[c] = plane(ty_v, c, CY - 1)
        ly = 0.0
        for j in range(CY):
            tx = jnp.where(last_x, 0.0, plane(tx_v, c, j))
            tz = jnp.where(last_z, 0.0, plane(tz_v, c, j))
            ty = plane(ty_v, c, j)
            if j == CY - 1:
                ty = jnp.where(gy == N_GY - 1, 0.0, ty)
            tx_o[c, j] = tx
            tz_o[c, j] = tz
            ty_o[c, j] = ty
            faces = tx + from_row_before(tx, 0.0) + ty + ly + tz + pltpu.roll(tz, 1, 1)
            diag[c, j] = plane(acc, 3 * c, j) + faces
            cross[c, j] = plane(acc, 2 - c, j)
            rhs[c, j] = plane(b, c, j)
            ly = ty


def condense_kernel(idx, diag, cross, ty, rhs, lx_in, ly_in, brk_0, brk_1, brk_2, brk_3, seg, dmat, tau_o, sinv, binv, brk):
    gy = idx[1]
    for k, ref in enumerate((brk_0, brk_1, brk_2, brk_3)):
        for i in range(4):
            brk[pl.ds(jnp.bitwise_xor(gy, 4 * k + i), 1), :] = ref[i : i + 1, :]
    cuts = pltpu.roll(brk[...], (NZ - CY * gy) % NZ, 1)
    for c in range(2):
        ly = ly_in[c]
        for j in range(CY):
            d = diag[c, j] + jnp.where(rows() == 0, lx_in[c, j : j + 1, :], 0.0)
            dmat[3 * c, j] = d + ly if j == 0 else d
        for j in range(CY + 1):
            keep = 1.0 - cuts[:, j : j + 1].astype(F32)
            tau_o[c, j] = (ty[c, j - 1] if j else ly) * keep
    for j in range(CY):
        dmat[1, j] = cross[0, j]
        dmat[2, j] = cross[1, j]

    def tau(j):
        return pair_at(tau_o, j)

    def outer(t, p):
        return tuple(x * y for x, y in zip(p, (t[0] * t[0], t[0] * t[1], t[1] * t[0], t[1] * t[1])))

    s = inv2(block_at(dmat, 0))
    e = inv2(block_at(dmat, CY - 1))
    zero = jnp.zeros(PLANE, F32)
    yf = (tau(0)[0], zero, zero, tau(0)[1])
    zl = (tau(CY)[0], zero, zero, tau(CY)[1])
    y = pair_at(rhs, 0)
    z = pair_at(rhs, CY - 1)
    for i in range(4):
        sinv[i, 0] = s[i]
        binv[i, CY - 1] = e[i]
    for j in range(1, CY):
        k = CY - 1 - j
        t, u = tau(j), tau(k + 1)
        yf = rows_by(t, mm(s, yf))
        zl = rows_by(u, mm(e, zl))
        yv, zv = mv(s, y), mv(e, z)
        y = tuple(rhs[c, j] + t[c] * yv[c] for c in range(2))
        z = tuple(rhs[c, k] + u[c] * zv[c] for c in range(2))
        s = inv2(tuple(d - x for d, x in zip(block_at(dmat, j), outer(t, s))))
        e = inv2(tuple(d - x for d, x in zip(block_at(dmat, k), outer(u, e))))
        for i in range(4):
            sinv[i, j] = s[i]
            binv[i, k] = e[i]
    store_segment(
        seg,
        (columns_by(e, tau(0)), mm(e, zl), mm(s, yf), columns_by(s, tau(CY)), mv(e, z), mv(s, y)),
        True,
    )


def gather_segments(position, mats, vecs, offset, mat_s, vec_s):
    for k in range(4):
        at = jnp.bitwise_xor(position, k)
        mat_s[at] = mats[k][0:16]
        vec_s[at] = vecs[k][offset : offset + 4]


def make_total_kernel(whole):
    def kernel(*refs):
        idx = refs[0]
        if whole:
            mats = vecs = refs[1:5]
            out, mat_s, vec_s = refs[5:]
        else:
            mats, vecs = refs[1:5], refs[5:9]
            out, mat_s, vec_s = refs[9:]
        gather_segments(idx[1] % 4, mats, vecs, 16 if whole else 0, mat_s, vec_s)
        segs = [load_segment(mat_s.at[m], vec_s.at[m], 0) for m in range(4)]
        store_segment(out, join(join(segs[0], segs[1]), join(segs[2], segs[3])), whole)

    return kernel


def split3(x):
    hi = x.astype(BF16)
    rest = x - hi.astype(F32)
    mid = rest.astype(BF16)
    low = (rest - mid.astype(F32)).astype(BF16)
    return hi, mid, low


def slot_tables(cells, wells):
    cell = cells[...]
    row = jnp.bitwise_and(lax.shift_right_logical(cell, 7), 7) * CX + lax.shift_right_logical(cell, 10)
    shape = (NZ, SLOTS_ALL)
    up = lax.broadcasted_iota(jnp.int32, shape, 0)
    at_row = up == row
    at_layer = up == jnp.bitwise_and(cell, NZ - 1)
    at_well = up == wells[...]
    return at_row, at_layer, at_well


def ones_of(mask):
    return jnp.where(mask, 1.0, 0.0).astype(F32).astype(BF16)


NT = (((1,), (1,)), ((), ()))


def row_times(rows_in, table, dims):
    parts = [part for x in rows_in for part in split3(x)]
    n = len(rows_in)
    pad = 16 - 3 * n
    width = rows_in[0].shape[1]
    stacked = jnp.concatenate([p.astype(F32) for p in parts] + [jnp.zeros((pad, width), F32)], axis=0).astype(BF16)
    out = lax.dot_general(stacked, table, dims, preferred_element_type=F32)
    return [out[3 * i : 3 * i + 1] + out[3 * i + 1 : 3 * i + 2] + out[3 * i + 2 : 3 * i + 3] for i in range(n)]


def make_solve_kernel(whole):
    def kernel(*refs):
        idx = refs[0]
        if whole:
            inner, outer_ = refs[1:5], refs[5:9]
            inner_v, outer_v = inner, outer_
            rest = refs[9:]
            offset = 16
        else:
            inner, outer_, inner_v, outer_v = refs[1:5], refs[5:9], refs[9:13], refs[13:17]
            rest = refs[17:]
            offset = 0
        sinv, tau_r, rhs, cells, wells, weights = rest[:6]
        p_out, ends, msg_a, msg_b = rest[6:10]
        mat_i, vec_i, mat_o, vec_o, edge = rest[10:]
        gx, gy = idx[0], idx[1]
        z_at, y_at = gy % 4, gy // 4
        gather_segments(z_at, inner, inner_v, offset, mat_i, vec_i)
        gather_segments(y_at, outer_, outer_v, offset, mat_o, vec_o)
        zero = jnp.zeros(PLANE, F32)
        before = ((zero,) * 4, (zero,) * 2)
        after = ((zero,) * 4, (zero,) * 2)
        for mat_s, vec_s, here in ((mat_o, vec_o, y_at), (mat_i, vec_i, z_at)):
            for m in range(3):
                seg = load_segment(mat_s.at[m], vec_s.at[m], 0)
                before = choose(m < here, join_before(before, seg), before)
                m = 3 - m
                seg = load_segment(mat_s.at[m], vec_s.at[m], 0)
                after = choose(m > here, join_after(seg, after), after)
        own = load_segment(inner[0], inner_v[0], offset)
        ff, fl, lf, ll, gf, gl = own
        up_m, up_v = join_before(before, own)
        last = mv(inv2(one_minus(mm(up_m, after[0]))), madd(up_v, mv(up_m, after[1])))
        beyond = madd(after[1], mv(after[0], last))
        k = inv2(one_minus(mm(ff, before[0])))
        first = mv(k, madd(madd(gf, mv(ff, before[1])), mv(fl, beyond)))
        behind = madd(before[1], mv(before[0], first))
        for c in range(2):
            ends[c] = behind[c]
            ends[2 + c] = beyond[c]

        def tau(j):
            return pair_at(tau_r, j)

        def sv(j):
            return block_at(sinv, j)

        r = [pair_at(rhs, j) for j in range(CY)]
        r[0] = tuple(r[0][c] + tau(0)[c] * behind[c] for c in range(2))
        y = sweep_forward(sv, tau, r)
        u = beyond
        for j in range(CY - 1, -1, -1):
            u = mv(sv(j), tuple(y[j][c] + tau(j + 1)[c] * u[c] for c in range(2)))
            for c in range(2):
                p_out[c, j] = u[c]
                edge[0, c * CY + j : c * CY + j + 1, :] = u[c][0:1, :]
                edge[1, c * CY + j : c * CY + j + 1, :] = u[c][CX - 1 : CX, :]
        at_row, at_layer, at_well = slot_tables(cells, wells)
        pressure = jnp.concatenate([p_out[0, j] for j in range(CY)], axis=0)
        table = ones_of(at_layer)
        picked = sum(jnp.dot(part, table, preferred_element_type=F32) for part in split3(pressure))
        values = jnp.sum(jnp.where(at_row, picked, 0.0), axis=0, keepdims=True)
        w = weights[...]
        sums, totals = row_times([w * values, w], ones_of(at_well), NT)
        tail = jnp.concatenate([sums, totals, jnp.zeros((6, W_ALL), F32)], axis=0)
        even = gx % 2 == 0
        low, high = edge[0], edge[1]
        msg_a[0:16, :] = jnp.where(even, high, low)
        msg_b[0:16, :] = jnp.where(even, low, high)
        msg_a[16:24, :] = tail
        msg_b[16:24, :] = tail

    return kernel


def apply_operator(idx, got, cells, wells, weights):
    gx = idx[0]
    got_a, sent_b, got_b, got_c, got_d = got
    tail = sent_b[16:24, :] + got_b[16:24, :] + got_c[...] + got_d[...]
    rates = tail[0:1] / jnp.maximum(tail[1:2], 1.0)
    at_row, at_layer, at_well = slot_tables(cells, wells)
    slot_rate = row_times([rates], ones_of(at_well), (((1,), (0,)), ((), ())))[0]
    added = jnp.where(at_layer, weights[...] * slot_rate, 0.0)
    table = ones_of(at_row)
    well_add = sum(lax.dot_general(table, part, NT, preferred_element_type=F32) for part in split3(added))
    even = gx % 2 == 0
    halo_a, halo_b = got_a[0:16, :], got_b[0:16, :]
    from_after = jnp.where(gx < N_GX - 1, jnp.where(even, halo_a, halo_b), 0.0)
    from_before = jnp.where(gx > 0, jnp.where(even, halo_b, halo_a), 0.0)
    return well_add, from_after, from_before


def operator_plane(c, j, p, ends, dmat, tx, ty, tz, lx_in, ly_in, halo, well_add):
    from_after, from_before = halo
    here = p[c, j]
    up = p[c, j + 1] if j < CY - 1 else ends[2 + c]
    down = p[c, j - 1] if j > 0 else ends[c]
    t = tx[c, j]
    at = c * CY + j
    beside = t * from_row_after(here, from_after[at : at + 1])
    beside = beside + from_row_before(t * here, lx_in[c, j : j + 1, :] * from_before[at : at + 1])
    beside = beside + ty[c, j] * up + (ty[c, j - 1] if j else ly_in[c]) * down
    tzp = tz[c, j]
    beside = beside + tzp * pltpu.roll(here, NZ - 1, 1) + pltpu.roll(tzp * here, 1, 1)
    out = dmat[2 * c, j] * p[0, j] + dmat[2 * c + 1, j] * p[1, j] - beside
    if c == 0:
        out = out + well_add[j * CX : (j + 1) * CX]
    return out


def first_image_kernel(idx, got_a, sent_b, got_b, got_c, got_d, p, ends, dmat, tau_r, sinv, binv, rhs, tx, ty, tz, lx_in, ly_in, cells, wells, weights, q_out, e_out, vec_out, dots):
    well_add, after, before = apply_operator(idx, (got_a, sent_b, got_b, got_c, got_d), cells, wells, weights)
    eq = jnp.zeros(PLANE, F32)
    qq = jnp.zeros(PLANE, F32)
    e = []
    for j in range(CY):
        pair = []
        for c in range(2):
            q = operator_plane(c, j, p, ends, dmat, tx, ty, tz, lx_in, ly_in, (after, before), well_add)
            rest = rhs[c, j] - q
            q_out[c, j] = q
            e_out[c, j] = rest
            eq = eq + rest * q
            qq = qq + q * q
            pair.append(rest)
        e.append(tuple(pair))
    dots[0] = eq
    dots[1] = qq

    def tau(j):
        return pair_at(tau_r, j)

    y = sweep_forward(lambda j: block_at(sinv, j), tau, e)[CY - 1]
    z = sweep_backward(lambda j: block_at(binv, j), tau, e)
    first = mv(block_at(binv, 0), z)
    last = mv(block_at(sinv, CY - 1), y)
    for c in range(2):
        vec_out[c] = first[c]
        vec_out[2 + c] = last[c]


def second_image_kernel(idx, got_a, sent_b, got_b, got_c, got_d, p, ends, dmat, tx, ty, tz, lx_in, ly_in, cells, wells, weights, q_in, e_in, dots_in, s_out, dots):
    well_add, after, before = apply_operator(idx, (got_a, sent_b, got_b, got_c, got_d), cells, wells, weights)
    sq = jnp.zeros(PLANE, F32)
    ss = jnp.zeros(PLANE, F32)
    es = jnp.zeros(PLANE, F32)
    for j in range(CY):
        for c in range(2):
            s = operator_plane(c, j, p, ends, dmat, tx, ty, tz, lx_in, ly_in, (after, before), well_add)
            s_out[c, j] = s
            sq = sq + s * q_in[c, j]
            ss = ss + s * s
            es = es + s * e_in[c, j]
    sums = [jnp.sum(x, axis=0, keepdims=True) for x in (dots_in[0], dots_in[1], sq, ss, es)]
    dots[...] = jnp.concatenate(sums + [jnp.zeros((3, NZ), F32)], axis=0)


def finish_kernel(got, p, w, q, e, s, x_out, r_out):
    total = got[0]
    for d in range(1, N_GY):
        total = total + got[d]
    total = jnp.broadcast_to(jnp.sum(total, axis=1, keepdims=True), (8, NZ))
    eq, qq, sq, ss, es = (total[i : i + 1] for i in range(5))
    rest = -eq / qq
    g = sq / qq
    k = (es - g * eq) / (ss - g * sq)
    on_p = (1.0 - rest) - k * g
    on_q = rest + k * g
    for c in range(2):
        for j in range(CY):
            at = pl.ds(j, CX, stride=CY)
            x_out.at[c][at, :] = on_p * p[c, j] + k * w[c, j]
            r_out.at[c][at, :] = e[c, j] + on_q * q[c, j] - k * s[c, j]


def call(kernel, name, outs, scratch, *args, specs=None, vmem=24 * 1024):
    outs = [o if isinstance(o, jax.ShapeDtypeStruct) else jax.ShapeDtypeStruct(o, F32) for o in outs]
    return pl.pallas_call(
        kernel,
        name=name,
        out_shape=tuple(outs),
        in_specs=specs or [SMEM] + [VMEM] * (len(args) - 1),
        out_specs=tuple(VMEM for _ in outs),
        scratch_shapes=[pltpu.VMEM(s, F32) if isinstance(s, tuple) else s for s in scratch],
        compiler_params=pltpu.CompilerParams(vmem_limit_bytes=vmem * 1024),
    )(*args)


def swapped(block, stride):
    return [block] + [lax.ppermute(block, "gy", [(i, i ^ (k * stride)) for i in range(N_GY)]) for k in (1, 2, 3)]


def exchange_rows(msg_a, msg_b):
    got_a = lax.ppermute(msg_a, "gx", [(i, i ^ 1) for i in range(N_GX)])
    below = lax.broadcasted_iota(jnp.int32, msg_b.shape, 0) >= 16
    sent_b = msg_b + jnp.where(below, got_a, 0.0)
    got_b = lax.ppermute(sent_b, "gx", [(i, (i + 1 if i % 2 else i - 1) % N_GX) for i in range(N_GX)])
    tail = sent_b[16:]
    got_c = lax.ppermute(tail, "gx", [(i, i ^ 4) for i in range(N_GX)])
    got_d = lax.ppermute(tail, "gx", [(i, (i + 2 if i % 2 else i - 2) % N_GX) for i in range(N_GX)])
    return got_a, sent_b, got_b, got_c, got_d


def sum_everywhere(x):
    x = x + lax.ppermute(x, "gx", [(i, i ^ 1) for i in range(N_GX)])
    others = [lax.ppermute(x, "gx", [(i, (i + 2 * k) % N_GX) for i in range(N_GX)]) for k in (1, 2, 3)]
    x = x + others[0] + others[1] + others[2]
    x = jnp.broadcast_to(x[None], (N_GY,) + x.shape)
    return lax.all_to_all(x, "gy", split_axis=0, concat_axis=0, tiled=True)


def body(right_side, accumulation, trans_x, trans_y, trans_z, perf_cell, perf_well, perf_weight, perf_count, breaks):
    gx, gy = lax.axis_index("gx"), lax.axis_index("gy")
    idx = jnp.stack([gx, gy]).astype(jnp.int32)

    def flat(a):
        return a.reshape(a.shape[0], CX * CY, NZ)

    field, block, part = (2, CY, CX, NZ), (4, CY, CX, NZ), (2, CY + 1, CX, NZ)
    seg, vec, message = (20, CX, NZ), (4, CX, NZ), (24, NZ)
    order = [(4, 16, CX, NZ), (4, 4, CX, NZ)]
    two, four = (2, CX * CY, NZ), (4, CX * CY, NZ)
    cuts = swapped(jnp.concatenate(swapped(breaks, 1), axis=0), 4)
    rhs, tx, ty, tz, diag, cross, sx, sy = call(
        prepare_kernel, "prepare",
        (field, field, field, field, field, field, (2, CY, NZ), (2, CX, NZ)),
        [two, four, two, two, two, pltpu.SemaphoreType.DMA((5,))],
        idx, flat(right_side), flat(accumulation), flat(trans_x), flat(trans_y), flat(trans_z),
        specs=[SMEM] + [HBM] * 5, vmem=PREPARE_VMEM,
    )
    lx = lax.ppermute(sx, "gx", [(i, i + 1) for i in range(N_GX - 1)])
    ly = lax.ppermute(sy, "gy", [(i, i + 1) for i in range(N_GY - 1)])
    slots = perf_cell.shape[3]
    live = jnp.arange(slots, dtype=jnp.int32)[None, :] < perf_count.reshape(N_GX, 1)
    weights = jnp.where(live, perf_weight.reshape(N_GX, slots), 0.0).reshape(1, SLOTS_ALL)
    owners = jnp.arange(N_GX, dtype=jnp.int32)[:, None] * 16
    wells = (perf_well.reshape(N_GX, slots) + owners).reshape(1, SLOTS_ALL)
    cells = perf_cell.reshape(1, SLOTS_ALL)
    perfs = (cells, wells, weights)

    own, dmat, tau, sinv, binv = call(
        condense_kernel, "condense", (seg, block, part, block, block),
        [pltpu.VMEM((N_GY, NZ), jnp.int32)], idx, diag, cross, ty, rhs, lx, ly, *cuts,
    )
    inner = swapped(own, 1)
    (group,) = call(make_total_kernel(True), "group_total", (seg,), order, idx, *inner)
    outer = swapped(group, 4)
    solve_scratch = order + order + [(2, 16, NZ)]
    p, ends, msg_a, msg_b = call(
        make_solve_kernel(True), "solve_first", (field, vec, message, message), solve_scratch,
        idx, *inner, *outer, sinv, tau, rhs, *perfs,
    )
    got = exchange_rows(msg_a, msg_b)
    q, e, own_v, dots = call(
        first_image_kernel, "first_image", (field, field, vec, (2, CX, NZ)), [],
        idx, *got, p, ends, dmat, tau, sinv, binv, rhs, tx, ty, tz, lx, ly, *perfs,
    )
    inner_v = swapped(own_v, 1)
    (group_v,) = call(make_total_kernel(False), "group_total_again", (vec,), order, idx, *inner, *inner_v)
    outer_v = swapped(group_v, 4)
    w, ends, msg_a, msg_b = call(
        make_solve_kernel(False), "solve_second", (field, vec, message, message), solve_scratch,
        idx, *inner, *outer, *inner_v, *outer_v, sinv, tau, e, *perfs,
    )
    got = exchange_rows(msg_a, msg_b)
    s, dots = call(
        second_image_kernel, "second_image", (field, (8, NZ)), [],
        idx, *got, w, ends, dmat, tx, ty, tz, lx, ly, *perfs, q, e, dots,
    )
    dots = sum_everywhere(dots)
    x, r = call(finish_kernel, "finish", (two, two), [], dots, p, w, q, e, s, specs=[VMEM] * 6)
    shape = (2, CX, CY, NZ)
    return x.reshape(shape), r.reshape(shape)


def solution(mesh):
    tile = P(None, "gx", "gy", None)
    slots = P("gx", "gy", None, None)
    return jax.shard_map(
        body,
        mesh=mesh,
        in_specs=(tile,) * 5 + (slots,) * 3 + (P("gx", "gy", None), P(("gx", "gy"), None)),
        out_specs=(tile, tile),
        check_vma=False,
    )
```

```python
import jax
import jax.numpy as jnp
from jax import lax
from jax.experimental import pallas as pl
from jax.experimental.pallas import tpu as pltpu
from jax.sharding import PartitionSpec as P

F32 = jnp.float32
BF16 = jnp.bfloat16
VMEM = pl.BlockSpec(memory_space=pltpu.VMEM)
HBM = pl.BlockSpec(memory_space=pltpu.HBM)
SMEM = pl.BlockSpec(memory_space=pltpu.SMEM)
CX, CY, NZ = 16, 8, 128
PLANE = (CX, NZ)
N_GX, N_GY = 8, 16
W_ALL = 128
PREPARE_VMEM = 54400
SLOTS_ALL = 256


def mm(p, q):
    return (
        p[0] * q[0] + p[1] * q[2],
        p[0] * q[1] + p[1] * q[3],
        p[2] * q[0] + p[3] * q[2],
        p[2] * q[1] + p[3] * q[3],
    )


def mv(p, v):
    return (p[0] * v[0] + p[1] * v[1], p[2] * v[0] + p[3] * v[1])


def madd(p, q):
    return tuple(a + b for a, b in zip(p, q))


def inv2(p):
    t = 1.0 / (p[0] * p[3] - p[1] * p[2])
    return (p[3] * t, -p[1] * t, -p[2] * t, p[0] * t)


def one_minus(p):
    return (1.0 - p[0], -p[1], -p[2], 1.0 - p[3])


def rows_by(t, p):
    return (t[0] * p[0], t[0] * p[1], t[1] * p[2], t[1] * p[3])


def columns_by(p, t):
    return (p[0] * t[0], p[1] * t[1], p[2] * t[0], p[3] * t[1])


def join(a, b):
    ff1, fl1, lf1, ll1, gf1, gl1 = a
    ff2, fl2, lf2, ll2, gf2, gl2 = b
    k = inv2(one_minus(mm(ll1, ff2)))
    last = mv(k, madd(gl1, mv(ll1, gf2)))
    last_b = mm(k, lf1)
    last_a = mm(k, mm(ll1, fl2))
    first = madd(gf2, mv(ff2, last))
    first_b = mm(ff2, last_b)
    first_a = madd(fl2, mm(ff2, last_a))
    return (
        madd(ff1, mm(fl1, first_b)),
        mm(fl1, first_a),
        mm(lf2, last_b),
        madd(ll2, mm(lf2, last_a)),
        madd(gf1, mv(fl1, first)),
        madd(gl2, mv(lf2, last)),
    )


def join_before(before, s):
    gm, g = before
    ff, fl, lf, ll, gf, gl = s
    k = inv2(one_minus(mm(ff, gm)))
    a = mv(k, madd(gf, mv(ff, g)))
    am = mm(k, fl)
    return (madd(ll, mm(lf, mm(gm, am))), madd(gl, mv(lf, madd(g, mv(gm, a)))))


def join_after(s, after):
    gm, g = after
    ff, fl, lf, ll, gf, gl = s
    k = inv2(one_minus(mm(ll, gm)))
    a = mv(k, madd(gl, mv(ll, g)))
    am = mm(k, lf)
    return (madd(ff, mm(fl, mm(gm, am))), madd(gf, mv(fl, madd(g, mv(gm, a)))))


def choose(flag, new, old):
    return tuple(tuple(jnp.where(flag, n, o) for n, o in zip(ns, os)) for ns, os in zip(new, old))


def load_segment(mat, vec, offset):
    m = [mat[i] for i in range(16)]
    v = [vec[offset + i] for i in range(4)]
    return (tuple(m[0:4]), tuple(m[4:8]), tuple(m[8:12]), tuple(m[12:16]), (v[0], v[1]), (v[2], v[3]))


def store_segment(ref, seg, whole):
    flat = [x for part in seg for x in part]
    if not whole:
        flat = flat[16:]
    for i, x in enumerate(flat):
        ref[i] = x


def lanes():
    return lax.broadcasted_iota(jnp.int32, PLANE, 1)


def rows():
    return lax.broadcasted_iota(jnp.int32, PLANE, 0)


def from_row_before(plane, edge):
    return jnp.where(rows() == 0, edge, pltpu.roll(plane, 1, 0))


def from_row_after(plane, edge):
    return jnp.where(rows() == CX - 1, edge, pltpu.roll(plane, CX - 1, 0))


def sweep_forward(sinv, tau, rhs):
    y = [rhs[0]]
    for j in range(1, CY):
        t = mv(sinv(j - 1), y[-1])
        y.append((rhs[j][0] + tau(j)[0] * t[0], rhs[j][1] + tau(j)[1] * t[1]))
    return y


def sweep_backward(binv, tau, rhs):
    z = rhs[CY - 1]
    for j in range(CY - 2, -1, -1):
        t = mv(binv(j + 1), z)
        z = (rhs[j][0] + tau(j + 1)[0] * t[0], rhs[j][1] + tau(j + 1)[1] * t[1])
    return z


def block_at(ref, j):
    return tuple(ref[i, j] for i in range(4))


def pair_at(ref, j):
    return (ref[0, j], ref[1, j])


def plane(ref, c, j):
    return ref.at[c][pl.ds(j, CX, stride=CY), :]


def prepare_kernel(idx, b_h, acc_h, tx_h, ty_h, tz_h, brk_h, rhs, tx_o, ty_o, tz_o, diag, cross, sx, edge, b, acc, tx_v, ty_v, tz_v, brk, sems):
    gx, gy = idx[0], idx[1]
    pairs = ((ty_h, ty_v), (brk_h, brk), (tx_h, tx_v), (tz_h, tz_v), (acc_h, acc), (b_h, b))
    copies = [pltpu.make_async_copy(h, v, sems.at[i]) for i, (h, v) in enumerate(pairs)]
    for copy in copies:
        copy.start()
    last_x = jnp.logical_and(rows() == CX - 1, gx == N_GX - 1)
    last_z = lanes() == NZ - 1
    for copy in copies:
        copy.wait()
    edge[2 * CX :, :] = jnp.broadcast_to(brk[...].astype(F32), (8, NZ))
    for c in range(2):
        sx[c] = tx_v[c, (CX - 1) * CY : CX * CY, :]
        edge[c * CX : (c + 1) * CX, :] = plane(ty_v, c, CY - 1)
        ly = 0.0
        for j in range(CY):
            tx = jnp.where(last_x, 0.0, plane(tx_v, c, j))
            tz = jnp.where(last_z, 0.0, plane(tz_v, c, j))
            ty = plane(ty_v, c, j)
            if j == CY - 1:
                ty = jnp.where(gy == N_GY - 1, 0.0, ty)
            tx_o[c, j] = tx
            tz_o[c, j] = tz
            ty_o[c, j] = ty
            faces = tx + from_row_before(tx, 0.0) + ty + ly + tz + pltpu.roll(tz, 1, 1)
            diag[c, j] = plane(acc, 3 * c, j) + faces
            cross[c, j] = plane(acc, 2 - c, j)
            rhs[c, j] = plane(b, c, j)
            ly = ty


def relay_kernel(idx, own, m1, m2, m3, out):
    z = idx[1] % 4
    refs = (own, m1, m2, m3)
    faces = own[0 : 2 * CX, :]
    for k in (1, 2, 3):
        faces = jnp.where(z == 3 - k, refs[k][0 : 2 * CX, :], faces)
    out[0 : 2 * CX, :] = faces
    out[2 * CX :, :] = jnp.zeros((8, NZ), F32)
    for k in range(4):
        out[pl.ds(2 * CX + jnp.bitwise_xor(z, k), 1), :] = refs[k][2 * CX : 2 * CX + 1, :]


def condense_kernel(idx, diag, cross, ty, rhs, lx_in, *refs):
    own, m1, m2, m3, o0, o1, o2, o3 = refs[:8]
    seg_a, seg_b, dmat, tau_o, sinv, binv, ly_in = refs[8:15]
    brk, near, far = refs[15:]
    gy = idx[1]
    z_at, y_at = gy % 4, gy // 4
    for k in range(4):
        near[jnp.bitwise_xor(z_at, k)] = (own, m1, m2, m3)[k][0 : 2 * CX, :]
        at = jnp.bitwise_xor(y_at, k)
        ref = (o0, o1, o2, o3)[k]
        far[at] = ref[0 : 2 * CX, :]
        for i in range(4):
            brk[pl.ds(4 * at + i, 1), :] = ref[2 * CX + i : 2 * CX + i + 1, :]
    cuts = pltpu.roll(brk[...], (NZ - CY * gy) % NZ, 1)
    before = jnp.where(y_at > 0, far[jnp.maximum(y_at - 1, 0)], 0.0)
    before = jnp.where(z_at > 0, near[jnp.maximum(z_at - 1, 0)], before)
    for c in range(2):
        ly_in[c] = before[c * CX : (c + 1) * CX]
    for c in range(2):
        ly = ly_in[c]
        for j in range(CY):
            d = diag[c, j] + jnp.where(rows() == 0, lx_in[c, j : j + 1, :], 0.0)
            dmat[3 * c, j] = d + ly if j == 0 else d
        for j in range(CY + 1):
            keep = 1.0 - cuts[:, j : j + 1]
            tau_o[c, j] = (ty[c, j - 1] if j else ly) * keep
    for j in range(CY):
        dmat[1, j] = cross[0, j]
        dmat[2, j] = cross[1, j]

    def tau(j):
        return pair_at(tau_o, j)

    def outer(t, p):
        return tuple(x * y for x, y in zip(p, (t[0] * t[0], t[0] * t[1], t[1] * t[0], t[1] * t[1])))

    s = inv2(block_at(dmat, 0))
    e = inv2(block_at(dmat, CY - 1))
    zero = jnp.zeros(PLANE, F32)
    yf = (tau(0)[0], zero, zero, tau(0)[1])
    zl = (tau(CY)[0], zero, zero, tau(CY)[1])
    y = pair_at(rhs, 0)
    z = pair_at(rhs, CY - 1)
    for i in range(4):
        sinv[i, 0] = s[i]
        binv[i, CY - 1] = e[i]
    for j in range(1, CY):
        k = CY - 1 - j
        t, u = tau(j), tau(k + 1)
        yf = rows_by(t, mm(s, yf))
        zl = rows_by(u, mm(e, zl))
        yv, zv = mv(s, y), mv(e, z)
        y = tuple(rhs[c, j] + t[c] * yv[c] for c in range(2))
        z = tuple(rhs[c, k] + u[c] * zv[c] for c in range(2))
        s = inv2(tuple(d - x for d, x in zip(block_at(dmat, j), outer(t, s))))
        e = inv2(tuple(d - x for d, x in zip(block_at(dmat, k), outer(u, e))))
        for i in range(4):
            sinv[i, j] = s[i]
            binv[i, k] = e[i]
    whole = (columns_by(e, tau(0)), mm(e, zl), mm(s, yf), columns_by(s, tau(CY)), mv(e, z), mv(s, y))
    for half, ref in enumerate((seg_a, seg_b)):
        store_segment(ref, [[x[8 * half : 8 * half + 8] for x in part] for part in whole], True)


def gather_matrices(position, halves, mat_s):
    for k in range(4):
        at = jnp.bitwise_xor(position, k)
        for half, refs in enumerate(halves):
            mat_s[at, :, 8 * half : 8 * half + 8, :] = refs[k][0:16]


def gather_vectors(position, vecs, vec_s):
    for k in range(4):
        vec_s[jnp.bitwise_xor(position, k)] = vecs[k][...]


def gather_both(position, halves, mat_s, vec_s):
    gather_matrices(position, halves, mat_s)
    for k in range(4):
        at = jnp.bitwise_xor(position, k)
        for half, refs in enumerate(halves):
            vec_s[at, :, 8 * half : 8 * half + 8, :] = refs[k][16:20]


def total_half_kernel(idx, own, m1, m2, m3, out, segs_s):
    for k, ref in enumerate((own, m1, m2, m3)):
        segs_s[jnp.bitwise_xor(idx[1] % 4, k)] = ref[...]
    segs = [load_segment(segs_s.at[m], segs_s.at[m], 16) for m in range(4)]
    store_segment(out, join(join(segs[0], segs[1]), join(segs[2], segs[3])), True)


def total_again_kernel(idx, *refs):
    halves, vecs = (refs[0:4], refs[4:8]), refs[8:12]
    out, mat_s, vec_s = refs[12:]
    gather_matrices(idx[1] % 4, halves, mat_s)
    gather_vectors(idx[1] % 4, vecs, vec_s)
    segs = [load_segment(mat_s.at[m], vec_s.at[m], 0) for m in range(4)]
    store_segment(out, join(join(segs[0], segs[1]), join(segs[2], segs[3])), False)


def split3(x):
    hi = x.astype(BF16)
    rest = x - hi.astype(F32)
    mid = rest.astype(BF16)
    low = (rest - mid.astype(F32)).astype(BF16)
    return hi, mid, low


def slot_tables(cells, wells):
    cell = cells[...]
    row = jnp.bitwise_and(lax.shift_right_logical(cell, 7), 7) * CX + lax.shift_right_logical(cell, 10)
    shape = (NZ, SLOTS_ALL)
    up = lax.broadcasted_iota(jnp.int32, shape, 0)
    at_row = up == row
    at_layer = up == jnp.bitwise_and(cell, NZ - 1)
    at_well = up == wells[...]
    return at_row, at_layer, at_well


def ones_of(mask):
    return jnp.where(mask, 1.0, 0.0).astype(F32).astype(BF16)


NT = (((1,), (1,)), ((), ()))


def row_times(rows_in, table, dims):
    parts = [part for x in rows_in for part in split3(x)]
    n = len(rows_in)
    pad = 16 - 3 * n
    width = rows_in[0].shape[1]
    stacked = jnp.concatenate([p.astype(F32) for p in parts] + [jnp.zeros((pad, width), F32)], axis=0).astype(BF16)
    out = lax.dot_general(stacked, table, dims, preferred_element_type=F32)
    return [out[3 * i : 3 * i + 1] + out[3 * i + 1 : 3 * i + 2] + out[3 * i + 2 : 3 * i + 3] for i in range(n)]


def make_solve_kernel(whole):
    def kernel(*refs):
        idx = refs[0]
        inner, outer = (refs[1:5], refs[5:9]), (refs[9:13], refs[13:17])
        rest = refs[17:] if whole else refs[25:]
        sinv, tau_r, rhs, cells, wells, weights = rest[:6]
        p_out, ends, msg = rest[6:9]
        mat_i, vec_i, mat_o, vec_o = rest[9:]
        gx, gy = idx[0], idx[1]
        z_at, y_at = gy % 4, gy // 4
        if whole:
            gather_both(z_at, inner, mat_i, vec_i)
            gather_both(y_at, outer, mat_o, vec_o)
        else:
            gather_matrices(z_at, inner, mat_i)
            gather_matrices(y_at, outer, mat_o)
            gather_vectors(z_at, refs[17:21], vec_i)
            gather_vectors(y_at, refs[21:25], vec_o)
        zero = jnp.zeros(PLANE, F32)
        before = ((zero,) * 4, (zero,) * 2)
        after = ((zero,) * 4, (zero,) * 2)
        for mat_s, vec_s, here in ((mat_o, vec_o, y_at), (mat_i, vec_i, z_at)):
            for m in range(3):
                seg = load_segment(mat_s.at[m], vec_s.at[m], 0)
                before = choose(m < here, join_before(before, seg), before)
                m = 3 - m
                seg = load_segment(mat_s.at[m], vec_s.at[m], 0)
                after = choose(m > here, join_after(seg, after), after)
        own = load_segment(mat_i.at[z_at], vec_i.at[z_at], 0)
        ff, fl, lf, ll, gf, gl = own
        up_m, up_v = join_before(before, own)
        last = mv(inv2(one_minus(mm(up_m, after[0]))), madd(up_v, mv(up_m, after[1])))
        beyond = madd(after[1], mv(after[0], last))
        k = inv2(one_minus(mm(ff, before[0])))
        first = mv(k, madd(madd(gf, mv(ff, before[1])), mv(fl, beyond)))
        behind = madd(before[1], mv(before[0], first))
        for c in range(2):
            ends[c] = behind[c]
            ends[2 + c] = beyond[c]

        def tau(j):
            return pair_at(tau_r, j)

        def sv(j):
            return block_at(sinv, j)

        r = [pair_at(rhs, j) for j in range(CY)]
        r[0] = tuple(r[0][c] + tau(0)[c] * behind[c] for c in range(2))
        y = sweep_forward(sv, tau, r)
        u = beyond
        for j in range(CY - 1, -1, -1):
            u = mv(sv(j), tuple(y[j][c] + tau(j + 1)[c] * u[c] for c in range(2)))
            for c in range(2):
                p_out[c, j] = u[c]
                msg[c * CY + j : c * CY + j + 1, :] = u[c][0:1, :]
                msg[16 + c * CY + j : 17 + c * CY + j, :] = u[c][CX - 1 : CX, :]
        at_row, at_layer, at_well = slot_tables(cells, wells)
        pressure = jnp.concatenate([p_out[0, j] for j in range(CY)], axis=0)
        table = ones_of(at_layer)
        picked = sum(jnp.dot(part, table, preferred_element_type=F32) for part in split3(pressure))
        values = jnp.sum(jnp.where(at_row, picked, 0.0), axis=0, keepdims=True)
        w = weights[...]
        sums, totals = row_times([w * values, w], ones_of(at_well), NT)
        tail = jnp.concatenate([sums, totals, jnp.zeros((6, W_ALL), F32)], axis=0)
        msg[32:40, :] = tail

    return kernel


def apply_operator(idx, got, cells, wells, weights):
    gx = idx[0]
    tail = got[0, 32:40, :]
    for d in range(1, N_GX):
        tail = tail + got[d, 32:40, :]
    rates = tail[0:1] / jnp.maximum(tail[1:2], 1.0)
    at_row, at_layer, at_well = slot_tables(cells, wells)
    slot_rate = row_times([rates], ones_of(at_well), (((1,), (0,)), ((), ())))[0]
    added = jnp.where(at_layer, weights[...] * slot_rate, 0.0)
    table = ones_of(at_row)
    well_add = sum(lax.dot_general(table, part, NT, preferred_element_type=F32) for part in split3(added))
    from_after = jnp.where(gx < N_GX - 1, got[jnp.minimum(gx + 1, N_GX - 1), 0:16, :], 0.0)
    from_before = jnp.where(gx > 0, got[jnp.maximum(gx - 1, 0), 16:32, :], 0.0)
    return well_add, from_after, from_before


def operator_plane(c, j, p, ends, dmat, tx, ty, tz, lx_in, ly_in, halo, well_add):
    from_after, from_before = halo
    here = p[c, j]
    up = p[c, j + 1] if j < CY - 1 else ends[2 + c]
    down = p[c, j - 1] if j > 0 else ends[c]
    t = tx[c, j]
    at = c * CY + j
    beside = t * from_row_after(here, from_after[at : at + 1])
    beside = beside + from_row_before(t * here, lx_in[c, j : j + 1, :] * from_before[at : at + 1])
    beside = beside + ty[c, j] * up + (ty[c, j - 1] if j else ly_in[c]) * down
    tzp = tz[c, j]
    beside = beside + tzp * pltpu.roll(here, NZ - 1, 1) + pltpu.roll(tzp * here, 1, 1)
    out = dmat[2 * c, j] * p[0, j] + dmat[2 * c + 1, j] * p[1, j] - beside
    if c == 0:
        out = out + well_add[j * CX : (j + 1) * CX]
    return out


def first_image_kernel(idx, got, p, ends, dmat, tau_r, sinv, binv, rhs, tx, ty, tz, lx_in, ly_in, cells, wells, weights, q_out, e_out, vec_out, dots):
    well_add, after, before = apply_operator(idx, got, cells, wells, weights)
    eq = jnp.zeros(PLANE, F32)
    qq = jnp.zeros(PLANE, F32)
    e = []
    for j in range(CY):
        pair = []
        for c in range(2):
            q = operator_plane(c, j, p, ends, dmat, tx, ty, tz, lx_in, ly_in, (after, before), well_add)
            rest = rhs[c, j] - q
            q_out[c, j] = q
            e_out[c, j] = rest
            eq = eq + rest * q
            qq = qq + q * q
            pair.append(rest)
        e.append(tuple(pair))
    dots[0] = eq
    dots[1] = qq

    def tau(j):
        return pair_at(tau_r, j)

    y = sweep_forward(lambda j: block_at(sinv, j), tau, e)[CY - 1]
    z = sweep_backward(lambda j: block_at(binv, j), tau, e)
    first = mv(block_at(binv, 0), z)
    last = mv(block_at(sinv, CY - 1), y)
    for c in range(2):
        vec_out[c] = first[c]
        vec_out[2 + c] = last[c]


def second_image_kernel(idx, got, p, ends, dmat, tx, ty, tz, lx_in, ly_in, cells, wells, weights, q_in, e_in, dots_in, s_out, dots):
    well_add, after, before = apply_operator(idx, got, cells, wells, weights)
    sq = jnp.zeros(PLANE, F32)
    ss = jnp.zeros(PLANE, F32)
    es = jnp.zeros(PLANE, F32)
    for j in range(CY):
        for c in range(2):
            s = operator_plane(c, j, p, ends, dmat, tx, ty, tz, lx_in, ly_in, (after, before), well_add)
            s_out[c, j] = s
            sq = sq + s * q_in[c, j]
            ss = ss + s * s
            es = es + s * e_in[c, j]
    sums = [jnp.sum(x, axis=0, keepdims=True) for x in (dots_in[0], dots_in[1], sq, ss, es)]
    lane = lax.broadcasted_iota(jnp.int32, (1, NZ), 1)
    row = jnp.zeros((1, NZ), F32)
    for i, x in enumerate(sums):
        row = jnp.where(lane == i, jnp.sum(x, axis=1, keepdims=True), row)
    dots[...] = row


def finish_kernel(got, p, w, q, e, s, x_out, r_out):
    total = jnp.sum(got[...], axis=0, keepdims=True)
    lane = lax.broadcasted_iota(jnp.int32, (1, NZ), 1)
    eq, qq, sq, ss, es = (
        jnp.broadcast_to(jnp.sum(jnp.where(lane == i, total, 0.0), axis=1, keepdims=True), (1, NZ)) for i in range(5)
    )
    rest = -eq / qq
    g = sq / qq
    k = (es - g * eq) / (ss - g * sq)
    on_p = (1.0 - rest) - k * g
    on_q = rest + k * g
    for c in range(2):
        for j in range(CY):
            at = pl.ds(j, CX, stride=CY)
            x_out.at[c][at, :] = on_p * p[c, j] + k * w[c, j]
            r_out.at[c][at, :] = e[c, j] + on_q * q[c, j] - k * s[c, j]


def call(kernel, name, outs, scratch, *args, specs=None, vmem=24 * 1024):
    outs = [o if isinstance(o, jax.ShapeDtypeStruct) else jax.ShapeDtypeStruct(o, F32) for o in outs]
    return pl.pallas_call(
        kernel,
        name=name,
        out_shape=tuple(outs),
        in_specs=specs or [SMEM] + [VMEM] * (len(args) - 1),
        out_specs=tuple(VMEM for _ in outs),
        scratch_shapes=[pltpu.VMEM(s, F32) if isinstance(s, tuple) else s for s in scratch],
        compiler_params=pltpu.CompilerParams(vmem_limit_bytes=vmem * 1024),
    )(*args)


def swapped(block, stride):
    return [block] + [lax.ppermute(block, "gy", [(i, i ^ (k * stride)) for i in range(N_GY)]) for k in (1, 2, 3)]


def body(right_side, accumulation, trans_x, trans_y, trans_z, perf_cell, perf_well, perf_weight, perf_count, breaks):
    gx, gy = lax.axis_index("gx"), lax.axis_index("gy")
    idx = jnp.stack([gx, gy]).astype(jnp.int32)

    def flat(a):
        return a.reshape(a.shape[0], CX * CY, NZ)

    field, block, part = (2, CY, CX, NZ), (4, CY, CX, NZ), (2, CY + 1, CX, NZ)
    half, vec, message = (20, 8, NZ), (4, CX, NZ), (40, NZ)
    order = [(4, 16, CX, NZ), (4, 4, CX, NZ)]
    two, four = (2, CX * CY, NZ), (4, CX * CY, NZ)
    rhs, tx, ty, tz, diag, cross, sx, edge = call(
        prepare_kernel, "prepare",
        (field, field, field, field, field, field, (2, CY, NZ), (40, NZ)),
        [two, four, two, two, two, pltpu.VMEM((1, NZ), jnp.int32), pltpu.SemaphoreType.DMA((6,))],
        idx, flat(right_side), flat(accumulation), flat(trans_x), flat(trans_y), flat(trans_z), breaks,
        specs=[SMEM] + [HBM] * 6, vmem=PREPARE_VMEM,
    )
    edges = swapped(edge, 1)
    lx = lax.ppermute(sx, "gx", [(i, i + 1) for i in range(N_GX - 1)])
    (relayed,) = call(relay_kernel, "relay", ((40, NZ),), [], idx, *edges)
    relayed = swapped(relayed, 4)
    slots = perf_cell.shape[3]
    live = jnp.arange(slots, dtype=jnp.int32)[None, :] < perf_count.reshape(N_GX, 1)
    weights = jnp.where(live, perf_weight.reshape(N_GX, slots), 0.0).reshape(1, SLOTS_ALL)
    owners = jnp.arange(N_GX, dtype=jnp.int32)[:, None] * 16
    wells = (perf_well.reshape(N_GX, slots) + owners).reshape(1, SLOTS_ALL)
    cells = perf_cell.reshape(1, SLOTS_ALL)
    perfs = (cells, wells, weights)

    own_a, own_b, dmat, tau, sinv, binv, ly = call(
        condense_kernel, "condense", (half, half, block, part, block, block, (2, CX, NZ)),
        [(N_GY, NZ), (4, 2 * CX, NZ), (4, 2 * CX, NZ)], idx, diag, cross, ty, rhs, lx, *edges, *relayed,
    )
    inner, outer = [], []
    for own in (own_a, own_b):
        inner.append(swapped(own, 1))
    for near in inner:
        (group,) = call(total_half_kernel, "group_total", (half,), [(4,) + half], idx, *near)
        outer.append(swapped(group, 4))
    inner = inner[0] + inner[1]
    outer = outer[0] + outer[1]
    solve_scratch = order + order
    p, ends, msg = call(
        make_solve_kernel(True), "solve_first", (field, vec, message), solve_scratch,
        idx, *inner, *outer, sinv, tau, rhs, *perfs,
    )
    got = lax.all_gather(msg, "gx")
    q, e, own_v, dots = call(
        first_image_kernel, "first_image", (field, field, vec, (2, CX, NZ)), [],
        idx, got, p, ends, dmat, tau, sinv, binv, rhs, tx, ty, tz, lx, ly, *perfs,
    )
    inner_v = swapped(own_v, 1)
    (group_v,) = call(total_again_kernel, "group_total_again", (vec,), order, idx, *inner, *inner_v)
    outer_v = swapped(group_v, 4)
    w, ends, msg = call(
        make_solve_kernel(False), "solve_second", (field, vec, message), solve_scratch,
        idx, *inner, *outer, *inner_v, *outer_v, sinv, tau, e, *perfs,
    )
    got = lax.all_gather(msg, "gx")
    s, dots = call(
        second_image_kernel, "second_image", (field, (1, NZ)), [],
        idx, got, w, ends, dmat, tx, ty, tz, lx, ly, *perfs, q, e, dots,
    )
    dots = lax.all_gather(dots, ("gx", "gy"), axis=0, tiled=True)
    x, r = call(finish_kernel, "finish", (two, two), [], dots, p, w, q, e, s, specs=[VMEM] * 6)
    shape = (2, CX, CY, NZ)
    return x.reshape(shape), r.reshape(shape)


def solution(mesh):
    tile = P(None, "gx", "gy", None)
    slots = P("gx", "gy", None, None)
    return jax.shard_map(
        body,
        mesh=mesh,
        in_specs=(tile,) * 5 + (slots,) * 3 + (P("gx", "gy", None), P(("gx", "gy"), None)),
        out_specs=(tile, tile),
        check_vma=False,
    )
```

```python
import jax
import jax.numpy as jnp
from jax import lax
from jax.experimental import pallas as pl
from jax.experimental.pallas import tpu as pltpu
from jax.sharding import PartitionSpec as P

F32 = jnp.float32
BF16 = jnp.bfloat16
VMEM = pl.BlockSpec(memory_space=pltpu.VMEM)
HBM = pl.BlockSpec(memory_space=pltpu.HBM)
SMEM = pl.BlockSpec(memory_space=pltpu.SMEM)
CX, CY, NZ = 16, 8, 128
PLANE = (CX, NZ)
N_GX, N_GY = 8, 16
W_ALL = 128
PREPARE_VMEM = 54400
EDGES_VMEM = 55296
SLOTS_ALL = 256


def mm(p, q):
    return (
        p[0] * q[0] + p[1] * q[2],
        p[0] * q[1] + p[1] * q[3],
        p[2] * q[0] + p[3] * q[2],
        p[2] * q[1] + p[3] * q[3],
    )


def mv(p, v):
    return (p[0] * v[0] + p[1] * v[1], p[2] * v[0] + p[3] * v[1])


def madd(p, q):
    return tuple(a + b for a, b in zip(p, q))


def inv2(p):
    t = 1.0 / (p[0] * p[3] - p[1] * p[2])
    return (p[3] * t, -p[1] * t, -p[2] * t, p[0] * t)


def one_minus(p):
    return (1.0 - p[0], -p[1], -p[2], 1.0 - p[3])


def rows_by(t, p):
    return (t[0] * p[0], t[0] * p[1], t[1] * p[2], t[1] * p[3])


def columns_by(p, t):
    return (p[0] * t[0], p[1] * t[1], p[2] * t[0], p[3] * t[1])


def join(a, b):
    ff1, fl1, lf1, ll1, gf1, gl1 = a
    ff2, fl2, lf2, ll2, gf2, gl2 = b
    k = inv2(one_minus(mm(ll1, ff2)))
    last = mv(k, madd(gl1, mv(ll1, gf2)))
    last_b = mm(k, lf1)
    last_a = mm(k, mm(ll1, fl2))
    first = madd(gf2, mv(ff2, last))
    first_b = mm(ff2, last_b)
    first_a = madd(fl2, mm(ff2, last_a))
    return (
        madd(ff1, mm(fl1, first_b)),
        mm(fl1, first_a),
        mm(lf2, last_b),
        madd(ll2, mm(lf2, last_a)),
        madd(gf1, mv(fl1, first)),
        madd(gl2, mv(lf2, last)),
    )


def join_before(before, s):
    gm, g = before
    ff, fl, lf, ll, gf, gl = s
    k = inv2(one_minus(mm(ff, gm)))
    a = mv(k, madd(gf, mv(ff, g)))
    am = mm(k, fl)
    return (madd(ll, mm(lf, mm(gm, am))), madd(gl, mv(lf, madd(g, mv(gm, a)))))


def join_after(s, after):
    gm, g = after
    ff, fl, lf, ll, gf, gl = s
    k = inv2(one_minus(mm(ll, gm)))
    a = mv(k, madd(gl, mv(ll, g)))
    am = mm(k, lf)
    return (madd(ff, mm(fl, mm(gm, am))), madd(gf, mv(fl, madd(g, mv(gm, a)))))


def position():
    return lax.axis_index("gx"), lax.axis_index("gy")


def choose(flag, new, old):
    return tuple(tuple(jnp.where(flag, n, o) for n, o in zip(ns, os)) for ns, os in zip(new, old))


def load_segment(mat, vec, offset):
    m = [mat[i] for i in range(16)]
    v = [vec[offset + i] for i in range(4)]
    return (tuple(m[0:4]), tuple(m[4:8]), tuple(m[8:12]), tuple(m[12:16]), (v[0], v[1]), (v[2], v[3]))


def store_segment(ref, seg, whole):
    flat = [x for part in seg for x in part]
    if not whole:
        flat = flat[16:]
    for i, x in enumerate(flat):
        ref[i] = x


def lanes():
    return lax.broadcasted_iota(jnp.int32, PLANE, 1)


def rows():
    return lax.broadcasted_iota(jnp.int32, PLANE, 0)


def from_row_before(plane, edge):
    return jnp.where(rows() == 0, edge, pltpu.roll(plane, 1, 0))


def from_row_after(plane, edge):
    return jnp.where(rows() == CX - 1, edge, pltpu.roll(plane, CX - 1, 0))


def sweep_forward(sinv, tau, rhs):
    y = [rhs[0]]
    for j in range(1, CY):
        t = mv(sinv(j - 1), y[-1])
        y.append((rhs[j][0] + tau(j)[0] * t[0], rhs[j][1] + tau(j)[1] * t[1]))
    return y


def sweep_backward(binv, tau, rhs):
    z = rhs[CY - 1]
    for j in range(CY - 2, -1, -1):
        t = mv(binv(j + 1), z)
        z = (rhs[j][0] + tau(j + 1)[0] * t[0], rhs[j][1] + tau(j + 1)[1] * t[1])
    return z


def block_at(ref, j):
    return tuple(ref[i, j] for i in range(4))


def pair_at(ref, j):
    return (ref[0, j], ref[1, j])


def plane(ref, c, j):
    return ref.at[c][pl.ds(j, CX, stride=CY), :]


def edges_kernel(tx_h, ty_h, brk_h, sx, edge, ty, brk, sems):
    copies = [pltpu.make_async_copy(h, v, sems.at[i]) for i, (h, v) in enumerate(((ty_h, ty), (brk_h, brk)))]
    copies += [
        pltpu.make_async_copy(tx_h.at[c, (CX - 1) * CY : CX * CY, :], sx.at[c], sems.at[2 + c]) for c in range(2)
    ]
    for copy in copies:
        copy.start()
    for copy in copies:
        copy.wait()
    edge[2 * CX :, :] = jnp.broadcast_to(brk[...].astype(F32), (8, NZ))
    for c in range(2):
        edge[c * CX : (c + 1) * CX, :] = plane(ty, c, CY - 1)


def relay(own, m1, m2, m3):
    z = position()[1] % 4
    row = lax.broadcasted_iota(jnp.int32, own.shape, 0)
    out = jnp.where(row < 2 * CX, z == 3, row == 2 * CX)
    out = jnp.where(out, own, 0.0)
    for k, ref in ((1, m1), (2, m2), (3, m3)):
        out = jnp.where(jnp.where(row < 2 * CX, z == 3 - k, row == 2 * CX + k), ref, out)
    return out


def prepare_kernel(b_h, acc_h, tx_h, ty_h, tz_h, rhs, tx_o, ty_o, tz_o, diag, cross, b, acc, tx_v, ty_v, tz_v, sems):
    gx, gy = position()
    pairs = ((tx_h, tx_v), (ty_h, ty_v), (tz_h, tz_v), (acc_h, acc), (b_h, b))
    copies = [pltpu.make_async_copy(h, v, sems.at[i]) for i, (h, v) in enumerate(pairs)]
    for copy in copies:
        copy.start()
    last_x = jnp.logical_and(rows() == CX - 1, gx == N_GX - 1)
    last_z = lanes() == NZ - 1
    for copy in copies:
        copy.wait()
    for c in range(2):
        ly = 0.0
        for j in range(CY):
            tx = jnp.where(last_x, 0.0, plane(tx_v, c, j))
            tz = jnp.where(last_z, 0.0, plane(tz_v, c, j))
            ty = plane(ty_v, c, j)
            if j == CY - 1:
                ty = jnp.where(gy == N_GY - 1, 0.0, ty)
            tx_o[c, j] = tx
            tz_o[c, j] = tz
            ty_o[c, j] = ty
            faces = tx + from_row_before(tx, 0.0) + ty + ly + tz + pltpu.roll(tz, 1, 1)
            diag[c, j] = plane(acc, 3 * c, j) + faces
            cross[c, j] = plane(acc, 2 - c, j)
            rhs[c, j] = plane(b, c, j)
            ly = ty


def condense_kernel(diag, cross, ty, rhs, lx_in, *refs):
    own, m1, m2, m3, o0, o1, o2, o3 = refs[:8]
    seg_a, seg_b, dmat, tau_o, sinv, binv, ly_in = refs[8:15]
    brk, near, far = refs[15:]
    gy = position()[1]
    z_at, y_at = gy % 4, gy // 4
    for k in range(4):
        near[jnp.bitwise_xor(z_at, k)] = (own, m1, m2, m3)[k][0 : 2 * CX, :]
        at = jnp.bitwise_xor(y_at, k)
        ref = (o0, o1, o2, o3)[k]
        far[at] = ref[0 : 2 * CX, :]
        for i in range(4):
            brk[pl.ds(4 * at + jnp.bitwise_xor(z_at, i), 1), :] = ref[2 * CX + i : 2 * CX + i + 1, :]
    cuts = pltpu.roll(brk[...], (NZ - CY * gy) % NZ, 1)
    before = jnp.where(y_at > 0, far[jnp.maximum(y_at - 1, 0)], 0.0)
    before = jnp.where(z_at > 0, near[jnp.maximum(z_at - 1, 0)], before)
    for c in range(2):
        ly_in[c] = before[c * CX : (c + 1) * CX]
    for c in range(2):
        ly = ly_in[c]
        for j in range(CY):
            d = diag[c, j] + jnp.where(rows() == 0, lx_in[c, j : j + 1, :], 0.0)
            dmat[3 * c, j] = d + ly if j == 0 else d
        for j in range(CY + 1):
            keep = 1.0 - cuts[:, j : j + 1]
            tau_o[c, j] = (ty[c, j - 1] if j else ly) * keep
    for j in range(CY):
        dmat[1, j] = cross[0, j]
        dmat[2, j] = cross[1, j]

    def tau(j):
        return pair_at(tau_o, j)

    def outer(t, p):
        return tuple(x * y for x, y in zip(p, (t[0] * t[0], t[0] * t[1], t[1] * t[0], t[1] * t[1])))

    s = inv2(block_at(dmat, 0))
    e = inv2(block_at(dmat, CY - 1))
    zero = jnp.zeros(PLANE, F32)
    yf = (tau(0)[0], zero, zero, tau(0)[1])
    zl = (tau(CY)[0], zero, zero, tau(CY)[1])
    y = pair_at(rhs, 0)
    z = pair_at(rhs, CY - 1)
    for i in range(4):
        sinv[i, 0] = s[i]
        binv[i, CY - 1] = e[i]
    for j in range(1, CY):
        k = CY - 1 - j
        t, u = tau(j), tau(k + 1)
        yf = rows_by(t, mm(s, yf))
        zl = rows_by(u, mm(e, zl))
        yv, zv = mv(s, y), mv(e, z)
        y = tuple(rhs[c, j] + t[c] * yv[c] for c in range(2))
        z = tuple(rhs[c, k] + u[c] * zv[c] for c in range(2))
        s = inv2(tuple(d - x for d, x in zip(block_at(dmat, j), outer(t, s))))
        e = inv2(tuple(d - x for d, x in zip(block_at(dmat, k), outer(u, e))))
        for i in range(4):
            sinv[i, j] = s[i]
            binv[i, k] = e[i]
    whole = (columns_by(e, tau(0)), mm(e, zl), mm(s, yf), columns_by(s, tau(CY)), mv(e, z), mv(s, y))
    for half, ref in enumerate((seg_a, seg_b)):
        store_segment(ref, [[x[8 * half : 8 * half + 8] for x in part] for part in whole], True)


def gather_matrices(position, halves, mat_s):
    for k in range(4):
        at = jnp.bitwise_xor(position, k)
        for half, refs in enumerate(halves):
            mat_s[at, :, 8 * half : 8 * half + 8, :] = refs[k][0:16]


def gather_vectors(position, vecs, vec_s):
    for k in range(4):
        vec_s[jnp.bitwise_xor(position, k)] = vecs[k][...]


def gather_both(position, halves, mat_s, vec_s):
    gather_matrices(position, halves, mat_s)
    for k in range(4):
        at = jnp.bitwise_xor(position, k)
        for half, refs in enumerate(halves):
            vec_s[at, :, 8 * half : 8 * half + 8, :] = refs[k][16:20]


def total_half_kernel(own, m1, m2, m3, out, segs_s):
    for k, ref in enumerate((own, m1, m2, m3)):
        segs_s[jnp.bitwise_xor(position()[1] % 4, k)] = ref[...]
    segs = [load_segment(segs_s.at[m], segs_s.at[m], 16) for m in range(4)]
    store_segment(out, join(join(segs[0], segs[1]), join(segs[2], segs[3])), True)


def total_again_kernel(*refs):
    halves, vecs = (refs[0:4], refs[4:8]), refs[8:12]
    out, mat_s, vec_s = refs[12:]
    gather_matrices(position()[1] % 4, halves, mat_s)
    gather_vectors(position()[1] % 4, vecs, vec_s)
    segs = [load_segment(mat_s.at[m], vec_s.at[m], 0) for m in range(4)]
    store_segment(out, join(join(segs[0], segs[1]), join(segs[2], segs[3])), False)


def split3(x):
    hi = x.astype(BF16)
    rest = x - hi.astype(F32)
    mid = rest.astype(BF16)
    low = (rest - mid.astype(F32)).astype(BF16)
    return hi, mid, low


def slot_tables(cells, wells):
    cell = cells[...]
    row = jnp.bitwise_and(lax.shift_right_logical(cell, 7), 7) * CX + lax.shift_right_logical(cell, 10)
    shape = (NZ, SLOTS_ALL)
    up = lax.broadcasted_iota(jnp.int32, shape, 0)
    at_row = up == row
    at_layer = up == jnp.bitwise_and(cell, NZ - 1)
    at_well = up == wells[...]
    return at_row, at_layer, at_well


def ones_of(mask):
    return jnp.where(mask, 1.0, 0.0).astype(F32).astype(BF16)


NT = (((1,), (1,)), ((), ()))


def row_times(rows_in, table, dims):
    parts = [part for x in rows_in for part in split3(x)]
    n = len(rows_in)
    pad = 16 - 3 * n
    width = rows_in[0].shape[1]
    stacked = jnp.concatenate([p.astype(F32) for p in parts] + [jnp.zeros((pad, width), F32)], axis=0).astype(BF16)
    out = lax.dot_general(stacked, table, dims, preferred_element_type=F32)
    return [out[3 * i : 3 * i + 1] + out[3 * i + 1 : 3 * i + 2] + out[3 * i + 2 : 3 * i + 3] for i in range(n)]


def make_solve_kernel(whole):
    def kernel(*refs):
        inner, outer = (refs[0:4], refs[4:8]), (refs[8:12], refs[12:16])
        rest = refs[16:] if whole else refs[24:]
        sinv, tau_r, rhs, cells, wells, weights = rest[:6]
        p_out, ends, msg_a, msg_b = rest[6:10]
        mat_i, vec_i, mat_o, vec_o, edge = rest[10:]
        gx, gy = position()
        z_at, y_at = gy % 4, gy // 4
        if whole:
            gather_both(z_at, inner, mat_i, vec_i)
            gather_both(y_at, outer, mat_o, vec_o)
        else:
            gather_matrices(z_at, inner, mat_i)
            gather_matrices(y_at, outer, mat_o)
            gather_vectors(z_at, refs[16:20], vec_i)
            gather_vectors(y_at, refs[20:24], vec_o)
        zero = jnp.zeros(PLANE, F32)
        before = ((zero,) * 4, (zero,) * 2)
        after = ((zero,) * 4, (zero,) * 2)
        for mat_s, vec_s, here in ((mat_o, vec_o, y_at), (mat_i, vec_i, z_at)):
            for m in range(3):
                seg = load_segment(mat_s.at[m], vec_s.at[m], 0)
                before = choose(m < here, join_before(before, seg), before)
                m = 3 - m
                seg = load_segment(mat_s.at[m], vec_s.at[m], 0)
                after = choose(m > here, join_after(seg, after), after)
        own = load_segment(mat_i.at[z_at], vec_i.at[z_at], 0)
        ff, fl, lf, ll, gf, gl = own
        up_m, up_v = join_before(before, own)
        last = mv(inv2(one_minus(mm(up_m, after[0]))), madd(up_v, mv(up_m, after[1])))
        beyond = madd(after[1], mv(after[0], last))
        k = inv2(one_minus(mm(ff, before[0])))
        first = mv(k, madd(madd(gf, mv(ff, before[1])), mv(fl, beyond)))
        behind = madd(before[1], mv(before[0], first))
        for c in range(2):
            ends[c] = behind[c]
            ends[2 + c] = beyond[c]

        def tau(j):
            return pair_at(tau_r, j)

        def sv(j):
            return block_at(sinv, j)

        r = [pair_at(rhs, j) for j in range(CY)]
        r[0] = tuple(r[0][c] + tau(0)[c] * behind[c] for c in range(2))
        y = sweep_forward(sv, tau, r)
        u = beyond
        for j in range(CY - 1, -1, -1):
            u = mv(sv(j), tuple(y[j][c] + tau(j + 1)[c] * u[c] for c in range(2)))
            for c in range(2):
                p_out[c, j] = u[c]
                edge[0, c * CY + j : c * CY + j + 1, :] = u[c][0:1, :]
                edge[1, c * CY + j : c * CY + j + 1, :] = u[c][CX - 1 : CX, :]
        at_row, at_layer, at_well = slot_tables(cells, wells)
        pressure = jnp.concatenate([p_out[0, j] for j in range(CY)], axis=0)
        table = ones_of(at_layer)
        picked = sum(jnp.dot(part, table, preferred_element_type=F32) for part in split3(pressure))
        values = jnp.sum(jnp.where(at_row, picked, 0.0), axis=0, keepdims=True)
        w = weights[...]
        sums, totals = row_times([w * values, w], ones_of(at_well), NT)
        tail = jnp.concatenate([sums, totals, jnp.zeros((6, W_ALL), F32)], axis=0)
        even = gx % 2 == 0
        low, high = edge[0], edge[1]
        msg_a[0:16, :] = jnp.where(even, high, low)
        msg_b[0:16, :] = jnp.where(even, low, high)
        msg_a[16:24, :] = tail
        msg_b[16:24, :] = tail

    return kernel


def apply_operator(got, cells, wells, weights):
    gx = position()[0]
    got_a, sent_b, got_b, got_c, got_d = got
    tail = sent_b[16:24, :] + got_b[16:24, :] + got_c[...] + got_d[...]
    rates = tail[0:1] / jnp.maximum(tail[1:2], 1.0)
    at_row, at_layer, at_well = slot_tables(cells, wells)
    slot_rate = row_times([rates], ones_of(at_well), (((1,), (0,)), ((), ())))[0]
    added = jnp.where(at_layer, weights[...] * slot_rate, 0.0)
    table = ones_of(at_row)
    well_add = sum(lax.dot_general(table, part, NT, preferred_element_type=F32) for part in split3(added))
    even = gx % 2 == 0
    halo_a, halo_b = got_a[0:16, :], got_b[0:16, :]
    from_after = jnp.where(gx < N_GX - 1, jnp.where(even, halo_a, halo_b), 0.0)
    from_before = jnp.where(gx > 0, jnp.where(even, halo_b, halo_a), 0.0)
    return well_add, from_after, from_before


def operator_plane(c, j, p, ends, dmat, tx, ty, tz, lx_in, ly_in, halo, well_add):
    from_after, from_before = halo
    here = p[c, j]
    up = p[c, j + 1] if j < CY - 1 else ends[2 + c]
    down = p[c, j - 1] if j > 0 else ends[c]
    t = tx[c, j]
    at = c * CY + j
    beside = t * from_row_after(here, from_after[at : at + 1])
    beside = beside + from_row_before(t * here, lx_in[c, j : j + 1, :] * from_before[at : at + 1])
    beside = beside + ty[c, j] * up + (ty[c, j - 1] if j else ly_in[c]) * down
    tzp = tz[c, j]
    beside = beside + tzp * pltpu.roll(here, NZ - 1, 1) + pltpu.roll(tzp * here, 1, 1)
    out = dmat[2 * c, j] * p[0, j] + dmat[2 * c + 1, j] * p[1, j] - beside
    if c == 0:
        out = out + well_add[j * CX : (j + 1) * CX]
    return out


def first_image_kernel(got_a, sent_b, got_b, got_c, got_d, p, ends, dmat, tau_r, sinv, binv, rhs, tx, ty, tz, lx_in, ly_in, cells, wells, weights, q_out, e_out, vec_out, dots):
    well_add, after, before = apply_operator((got_a, sent_b, got_b, got_c, got_d), cells, wells, weights)
    eq = jnp.zeros(PLANE, F32)
    qq = jnp.zeros(PLANE, F32)
    e = []
    for j in range(CY):
        pair = []
        for c in range(2):
            q = operator_plane(c, j, p, ends, dmat, tx, ty, tz, lx_in, ly_in, (after, before), well_add)
            rest = rhs[c, j] - q
            q_out[c, j] = q
            e_out[c, j] = rest
            eq = eq + rest * q
            qq = qq + q * q
            pair.append(rest)
        e.append(tuple(pair))
    dots[0] = eq
    dots[1] = qq

    def tau(j):
        return pair_at(tau_r, j)

    y = sweep_forward(lambda j: block_at(sinv, j), tau, e)[CY - 1]
    z = sweep_backward(lambda j: block_at(binv, j), tau, e)
    first = mv(block_at(binv, 0), z)
    last = mv(block_at(sinv, CY - 1), y)
    for c in range(2):
        vec_out[c] = first[c]
        vec_out[2 + c] = last[c]


def second_image_kernel(got_a, sent_b, got_b, got_c, got_d, p, ends, dmat, tx, ty, tz, lx_in, ly_in, cells, wells, weights, q_in, e_in, dots_in, s_out, dots):
    well_add, after, before = apply_operator((got_a, sent_b, got_b, got_c, got_d), cells, wells, weights)
    sq = jnp.zeros(PLANE, F32)
    ss = jnp.zeros(PLANE, F32)
    es = jnp.zeros(PLANE, F32)
    for j in range(CY):
        for c in range(2):
            s = operator_plane(c, j, p, ends, dmat, tx, ty, tz, lx_in, ly_in, (after, before), well_add)
            s_out[c, j] = s
            sq = sq + s * q_in[c, j]
            ss = ss + s * s
            es = es + s * e_in[c, j]
    sums = [jnp.sum(x, axis=0, keepdims=True) for x in (dots_in[0], dots_in[1], sq, ss, es)]
    dots[...] = jnp.concatenate(sums + [jnp.zeros((3, NZ), F32)], axis=0)


def finish_kernel(got, p, w, q, e, s, x_out, r_out):
    total = got[0]
    for d in range(1, N_GY):
        total = total + got[d]
    total = jnp.broadcast_to(jnp.sum(total, axis=1, keepdims=True), (8, NZ))
    eq, qq, sq, ss, es = (total[i : i + 1] for i in range(5))
    rest = -eq / qq
    g = sq / qq
    k = (es - g * eq) / (ss - g * sq)
    on_p = (1.0 - rest) - k * g
    on_q = rest + k * g
    for c in range(2):
        for j in range(CY):
            at = pl.ds(j, CX, stride=CY)
            x_out.at[c][at, :] = on_p * p[c, j] + k * w[c, j]
            r_out.at[c][at, :] = e[c, j] + on_q * q[c, j] - k * s[c, j]


def call(kernel, name, outs, scratch, *args, specs=None, vmem=24 * 1024):
    outs = [o if isinstance(o, jax.ShapeDtypeStruct) else jax.ShapeDtypeStruct(o, F32) for o in outs]
    return pl.pallas_call(
        kernel,
        name=name,
        out_shape=tuple(outs),
        in_specs=specs or [VMEM] * len(args),
        out_specs=tuple(VMEM for _ in outs),
        scratch_shapes=[pltpu.VMEM(s, F32) if isinstance(s, tuple) else s for s in scratch],
        compiler_params=pltpu.CompilerParams(vmem_limit_bytes=vmem * 1024),
    )(*args)


def swapped(block, stride):
    return [block] + [lax.ppermute(block, "gy", [(i, i ^ (k * stride)) for i in range(N_GY)]) for k in (1, 2, 3)]


def exchange_rows(msg_a, msg_b):
    got_a = lax.ppermute(msg_a, "gx", [(i, i ^ 1) for i in range(N_GX)])
    below = lax.broadcasted_iota(jnp.int32, msg_b.shape, 0) >= 16
    sent_b = msg_b + jnp.where(below, got_a, 0.0)
    got_b = lax.ppermute(sent_b, "gx", [(i, (i + 1 if i % 2 else i - 1) % N_GX) for i in range(N_GX)])
    tail = sent_b[16:]
    got_c = lax.ppermute(tail, "gx", [(i, i ^ 4) for i in range(N_GX)])
    got_d = lax.ppermute(tail, "gx", [(i, (i + 2 if i % 2 else i - 2) % N_GX) for i in range(N_GX)])
    return got_a, sent_b, got_b, got_c, got_d


def sum_everywhere(x):
    x = x + lax.ppermute(x, "gx", [(i, i ^ 1) for i in range(N_GX)])
    others = [lax.ppermute(x, "gx", [(i, (i + 2 * k) % N_GX) for i in range(N_GX)]) for k in (1, 2, 3)]
    x = x + others[0] + others[1] + others[2]
    x = jnp.broadcast_to(x[None], (N_GY,) + x.shape)
    return lax.all_to_all(x, "gy", split_axis=0, concat_axis=0, tiled=True)


def body(right_side, accumulation, trans_x, trans_y, trans_z, perf_cell, perf_well, perf_weight, perf_count, breaks):

    def flat(a):
        return a.reshape(a.shape[0], CX * CY, NZ)

    field, block, part = (2, CY, CX, NZ), (4, CY, CX, NZ), (2, CY + 1, CX, NZ)
    half, vec, message = (20, 8, NZ), (4, CX, NZ), (24, NZ)
    order = [(4, 16, CX, NZ), (4, 4, CX, NZ)]
    two, four = (2, CX * CY, NZ), (4, CX * CY, NZ)
    sx, edge = call(
        edges_kernel, "edges", ((2, CY, NZ), (40, NZ)),
        [two, pltpu.VMEM((1, NZ), jnp.int32), pltpu.SemaphoreType.DMA((4,))],
        flat(trans_x), flat(trans_y), breaks, specs=[HBM] * 3, vmem=EDGES_VMEM,
    )
    rhs, tx, ty, tz, diag, cross = call(
        prepare_kernel, "prepare", (field,) * 6,
        [two, four, two, two, two, pltpu.SemaphoreType.DMA((5,))],
        flat(right_side), flat(accumulation), flat(trans_x), flat(trans_y), flat(trans_z),
        specs=[HBM] * 5, vmem=PREPARE_VMEM,
    )
    lx = lax.ppermute(sx, "gx", [(i, i + 1) for i in range(N_GX - 1)])
    edges = swapped(edge, 1)
    lx, *edges = lax.optimization_barrier((lx, *edges))
    relayed = swapped(relay(*edges), 4)
    slots = perf_cell.shape[3]
    live = jnp.arange(slots, dtype=jnp.int32)[None, :] < perf_count.reshape(N_GX, 1)
    weights = jnp.where(live, perf_weight.reshape(N_GX, slots), 0.0).reshape(1, SLOTS_ALL)
    owners = jnp.arange(N_GX, dtype=jnp.int32)[:, None] * 16
    wells = (perf_well.reshape(N_GX, slots) + owners).reshape(1, SLOTS_ALL)
    cells = perf_cell.reshape(1, SLOTS_ALL)
    perfs = (cells, wells, weights)

    own_a, own_b, dmat, tau, sinv, binv, ly = call(
        condense_kernel, "condense", (half, half, block, part, block, block, (2, CX, NZ)),
        [(N_GY, NZ), (4, 2 * CX, NZ), (4, 2 * CX, NZ)], diag, cross, ty, rhs, lx, *edges, *relayed,
    )
    inner, outer = [], []
    for own in (own_a, own_b):
        inner.append(swapped(own, 1))
    for near in inner:
        (group,) = call(total_half_kernel, "group_total", (half,), [(4,) + half], *near)
        outer.append(swapped(group, 4))
    inner = inner[0] + inner[1]
    outer = outer[0] + outer[1]
    solve_scratch = order + order + [(2, 16, NZ)]
    p, ends, msg_a, msg_b = call(
        make_solve_kernel(True), "solve_first", (field, vec, message, message), solve_scratch,
        *inner, *outer, sinv, tau, rhs, *perfs,
    )
    got = exchange_rows(msg_a, msg_b)
    q, e, own_v, dots = call(
        first_image_kernel, "first_image", (field, field, vec, (2, CX, NZ)), [],
        *got, p, ends, dmat, tau, sinv, binv, rhs, tx, ty, tz, lx, ly, *perfs,
    )
    inner_v = swapped(own_v, 1)
    (group_v,) = call(total_again_kernel, "group_total_again", (vec,), order, *inner, *inner_v)
    outer_v = swapped(group_v, 4)
    w, ends, msg_a, msg_b = call(
        make_solve_kernel(False), "solve_second", (field, vec, message, message), solve_scratch,
        *inner, *outer, *inner_v, *outer_v, sinv, tau, e, *perfs,
    )
    got = exchange_rows(msg_a, msg_b)
    s, dots = call(
        second_image_kernel, "second_image", (field, (8, NZ)), [],
        *got, w, ends, dmat, tx, ty, tz, lx, ly, *perfs, q, e, dots,
    )
    dots = sum_everywhere(dots)
    x, r = call(finish_kernel, "finish", (two, two), [], dots, p, w, q, e, s)
    shape = (2, CX, CY, NZ)
    return x.reshape(shape), r.reshape(shape)


def solution(mesh):
    tile = P(None, "gx", "gy", None)
    slots = P("gx", "gy", None, None)
    return jax.shard_map(
        body,
        mesh=mesh,
        in_specs=(tile,) * 5 + (slots,) * 3 + (P("gx", "gy", None), P(("gx", "gy"), None)),
        out_specs=(tile, tile),
        check_vma=False,
    )
```

```python
import jax
import jax.numpy as jnp
from jax import lax
from jax.experimental import pallas as pl
from jax.experimental.pallas import tpu as pltpu
from jax.sharding import PartitionSpec as P

F32 = jnp.float32
BF16 = jnp.bfloat16
VMEM = pl.BlockSpec(memory_space=pltpu.VMEM)
HBM = pl.BlockSpec(memory_space=pltpu.HBM)
SMEM = pl.BlockSpec(memory_space=pltpu.SMEM)
CX, CY, NZ = 16, 8, 128
PLANE = (CX, NZ)
N_GX, N_GY = 8, 16
W_ALL = 128
PARTNERS = (0, 1, 3, 2)
PREPARE_VMEM = 54400
EDGES_VMEM = 55296
SLOTS_ALL = 256


def mm(p, q):
    return (
        p[0] * q[0] + p[1] * q[2],
        p[0] * q[1] + p[1] * q[3],
        p[2] * q[0] + p[3] * q[2],
        p[2] * q[1] + p[3] * q[3],
    )


def mv(p, v):
    return (p[0] * v[0] + p[1] * v[1], p[2] * v[0] + p[3] * v[1])


def madd(p, q):
    return tuple(a + b for a, b in zip(p, q))


def inv2(p):
    t = 1.0 / (p[0] * p[3] - p[1] * p[2])
    return (p[3] * t, -p[1] * t, -p[2] * t, p[0] * t)


def one_minus(p):
    return (1.0 - p[0], -p[1], -p[2], 1.0 - p[3])


def rows_by(t, p):
    return (t[0] * p[0], t[0] * p[1], t[1] * p[2], t[1] * p[3])


def columns_by(p, t):
    return (p[0] * t[0], p[1] * t[1], p[2] * t[0], p[3] * t[1])


def join(a, b):
    ff1, fl1, lf1, ll1, gf1, gl1 = a
    ff2, fl2, lf2, ll2, gf2, gl2 = b
    k = inv2(one_minus(mm(ll1, ff2)))
    last = mv(k, madd(gl1, mv(ll1, gf2)))
    last_b = mm(k, lf1)
    last_a = mm(k, mm(ll1, fl2))
    first = madd(gf2, mv(ff2, last))
    first_b = mm(ff2, last_b)
    first_a = madd(fl2, mm(ff2, last_a))
    return (
        madd(ff1, mm(fl1, first_b)),
        mm(fl1, first_a),
        mm(lf2, last_b),
        madd(ll2, mm(lf2, last_a)),
        madd(gf1, mv(fl1, first)),
        madd(gl2, mv(lf2, last)),
    )


def join_before(before, s):
    gm, g = before
    ff, fl, lf, ll, gf, gl = s
    k = inv2(one_minus(mm(ff, gm)))
    a = mv(k, madd(gf, mv(ff, g)))
    am = mm(k, fl)
    return (madd(ll, mm(lf, mm(gm, am))), madd(gl, mv(lf, madd(g, mv(gm, a)))))


def join_after(s, after):
    gm, g = after
    ff, fl, lf, ll, gf, gl = s
    k = inv2(one_minus(mm(ll, gm)))
    a = mv(k, madd(gl, mv(ll, g)))
    am = mm(k, lf)
    return (madd(ff, mm(fl, mm(gm, am))), madd(gf, mv(fl, madd(g, mv(gm, a)))))


def position():
    return lax.axis_index("gx"), lax.axis_index("gy")


def choose(flag, new, old):
    return tuple(tuple(jnp.where(flag, n, o) for n, o in zip(ns, os)) for ns, os in zip(new, old))


def load_segment(mat, vec, offset):
    m = [mat[i] for i in range(16)]
    v = [vec[offset + i] for i in range(4)]
    return (tuple(m[0:4]), tuple(m[4:8]), tuple(m[8:12]), tuple(m[12:16]), (v[0], v[1]), (v[2], v[3]))


def store_segment(ref, seg, whole):
    flat = [x for part in seg for x in part]
    if not whole:
        flat = flat[16:]
    for i, x in enumerate(flat):
        ref[i] = x


def lanes():
    return lax.broadcasted_iota(jnp.int32, PLANE, 1)


def rows():
    return lax.broadcasted_iota(jnp.int32, PLANE, 0)


def from_row_before(plane, edge):
    return jnp.where(rows() == 0, edge, pltpu.roll(plane, 1, 0))


def from_row_after(plane, edge):
    return jnp.where(rows() == CX - 1, edge, pltpu.roll(plane, CX - 1, 0))


def sweep_forward(sinv, tau, rhs):
    y = [rhs[0]]
    for j in range(1, CY):
        t = mv(sinv(j - 1), y[-1])
        y.append((rhs[j][0] + tau(j)[0] * t[0], rhs[j][1] + tau(j)[1] * t[1]))
    return y


def sweep_backward(binv, tau, rhs):
    z = rhs[CY - 1]
    for j in range(CY - 2, -1, -1):
        t = mv(binv(j + 1), z)
        z = (rhs[j][0] + tau(j + 1)[0] * t[0], rhs[j][1] + tau(j + 1)[1] * t[1])
    return z


def block_at(ref, j):
    return tuple(ref[i, j] for i in range(4))


def pair_at(ref, j):
    return (ref[0, j], ref[1, j])


def plane(ref, c, j):
    return ref.at[c][pl.ds(j, CX, stride=CY), :]


def edges_kernel(tx_h, ty_h, brk_h, sx, edge, ty, brk, sems):
    copies = [pltpu.make_async_copy(h, v, sems.at[i]) for i, (h, v) in enumerate(((ty_h, ty), (brk_h, brk)))]
    copies += [
        pltpu.make_async_copy(tx_h.at[c, (CX - 1) * CY : CX * CY, :], sx.at[c], sems.at[2 + c]) for c in range(2)
    ]
    for copy in copies:
        copy.start()
    for copy in copies:
        copy.wait()
    edge[2 * CX :, :] = jnp.broadcast_to(brk[...].astype(F32), (8, NZ))
    for c in range(2):
        edge[c * CX : (c + 1) * CX, :] = plane(ty, c, CY - 1)


def relay(*messages):
    z = position()[1] % 4
    row = lax.broadcasted_iota(jnp.int32, messages[0].shape, 0)
    out = jnp.zeros_like(messages[0])
    for k, ref in enumerate(messages):
        out = jnp.where(jnp.where(row < 2 * CX, z == 3 - PARTNERS[k], row == 2 * CX + k), ref, out)
    return out


def prepare_kernel(b_h, acc_h, tx_h, ty_h, tz_h, rhs, tx_o, ty_o, tz_o, diag, cross, b, acc, tx_v, ty_v, tz_v, sems):
    gx, gy = position()
    pairs = ((tx_h, tx_v), (ty_h, ty_v), (tz_h, tz_v), (acc_h, acc), (b_h, b))
    copies = [pltpu.make_async_copy(h, v, sems.at[i]) for i, (h, v) in enumerate(pairs)]
    for copy in copies:
        copy.start()
    last_x = jnp.logical_and(rows() == CX - 1, gx == N_GX - 1)
    last_z = lanes() == NZ - 1
    for copy in copies:
        copy.wait()
    for c in range(2):
        ly = 0.0
        for j in range(CY):
            tx = jnp.where(last_x, 0.0, plane(tx_v, c, j))
            tz = jnp.where(last_z, 0.0, plane(tz_v, c, j))
            ty = plane(ty_v, c, j)
            if j == CY - 1:
                ty = jnp.where(gy == N_GY - 1, 0.0, ty)
            tx_o[c, j] = tx
            tz_o[c, j] = tz
            ty_o[c, j] = ty
            faces = tx + from_row_before(tx, 0.0) + ty + ly + tz + pltpu.roll(tz, 1, 1)
            diag[c, j] = plane(acc, 3 * c, j) + faces
            cross[c, j] = plane(acc, 2 - c, j)
            rhs[c, j] = plane(b, c, j)
            ly = ty


def condense_kernel(diag, cross, ty, rhs, lx_in, *refs):
    messages, relayed = refs[:4], refs[4:8]
    seg_a, seg_b, dmat, tau_o, sinv, binv, ly_in = refs[8:15]
    brk, near, far = refs[15:]
    gy = position()[1]
    z_at, y_at = gy % 4, gy // 4
    for k in range(4):
        near[jnp.bitwise_xor(z_at, PARTNERS[k])] = messages[k][0 : 2 * CX, :]
        at = jnp.bitwise_xor(y_at, PARTNERS[k])
        far[at] = relayed[k][0 : 2 * CX, :]
        for i in range(4):
            row = relayed[k][2 * CX + i : 2 * CX + i + 1, :]
            brk[pl.ds(4 * at + jnp.bitwise_xor(z_at, PARTNERS[i]), 1), :] = row
    cuts = pltpu.roll(brk[...], (NZ - CY * gy) % NZ, 1)
    before = jnp.where(y_at > 0, far[jnp.maximum(y_at - 1, 0)], 0.0)
    before = jnp.where(z_at > 0, near[jnp.maximum(z_at - 1, 0)], before)
    for c in range(2):
        ly_in[c] = before[c * CX : (c + 1) * CX]
    for c in range(2):
        ly = ly_in[c]
        for j in range(CY):
            d = diag[c, j] + jnp.where(rows() == 0, lx_in[c, j : j + 1, :], 0.0)
            dmat[3 * c, j] = d + ly if j == 0 else d
        for j in range(CY + 1):
            keep = 1.0 - cuts[:, j : j + 1]
            tau_o[c, j] = (ty[c, j - 1] if j else ly) * keep
    for j in range(CY):
        dmat[1, j] = cross[0, j]
        dmat[2, j] = cross[1, j]

    def tau(j):
        return pair_at(tau_o, j)

    def outer(t, p):
        return tuple(x * y for x, y in zip(p, (t[0] * t[0], t[0] * t[1], t[1] * t[0], t[1] * t[1])))

    s = inv2(block_at(dmat, 0))
    e = inv2(block_at(dmat, CY - 1))
    zero = jnp.zeros(PLANE, F32)
    yf = (tau(0)[0], zero, zero, tau(0)[1])
    zl = (tau(CY)[0], zero, zero, tau(CY)[1])
    y = pair_at(rhs, 0)
    z = pair_at(rhs, CY - 1)
    for i in range(4):
        sinv[i, 0] = s[i]
        binv[i, CY - 1] = e[i]
    for j in range(1, CY):
        k = CY - 1 - j
        t, u = tau(j), tau(k + 1)
        yf = rows_by(t, mm(s, yf))
        zl = rows_by(u, mm(e, zl))
        yv, zv = mv(s, y), mv(e, z)
        y = tuple(rhs[c, j] + t[c] * yv[c] for c in range(2))
        z = tuple(rhs[c, k] + u[c] * zv[c] for c in range(2))
        s = inv2(tuple(d - x for d, x in zip(block_at(dmat, j), outer(t, s))))
        e = inv2(tuple(d - x for d, x in zip(block_at(dmat, k), outer(u, e))))
        for i in range(4):
            sinv[i, j] = s[i]
            binv[i, k] = e[i]
    whole = (columns_by(e, tau(0)), mm(e, zl), mm(s, yf), columns_by(s, tau(CY)), mv(e, z), mv(s, y))
    for half, ref in enumerate((seg_a, seg_b)):
        store_segment(ref, [[x[8 * half : 8 * half + 8] for x in part] for part in whole], True)


def gather_matrices(at_place, halves, mat_s):
    for k in range(4):
        at = jnp.bitwise_xor(at_place, PARTNERS[k])
        for half, refs in enumerate(halves):
            mat_s[at, :, 8 * half : 8 * half + 8, :] = refs[k][0:16]


def gather_vectors(at_place, vecs, vec_s):
    for k in range(4):
        vec_s[jnp.bitwise_xor(at_place, PARTNERS[k])] = vecs[k][...]


def gather_both(at_place, halves, mat_s, vec_s):
    gather_matrices(at_place, halves, mat_s)
    for k in range(4):
        at = jnp.bitwise_xor(at_place, PARTNERS[k])
        for half, refs in enumerate(halves):
            vec_s[at, :, 8 * half : 8 * half + 8, :] = refs[k][16:20]


def total_half_kernel(own, m1, m2, m3, out, segs_s):
    for k, ref in enumerate((own, m1, m2, m3)):
        segs_s[jnp.bitwise_xor(position()[1] % 4, PARTNERS[k])] = ref[...]
    segs = [load_segment(segs_s.at[m], segs_s.at[m], 16) for m in range(4)]
    store_segment(out, join(join(segs[0], segs[1]), join(segs[2], segs[3])), True)


def total_again_kernel(*refs):
    halves, vecs = (refs[0:4], refs[4:8]), refs[8:12]
    out, mat_s, vec_s = refs[12:]
    gather_matrices(position()[1] % 4, halves, mat_s)
    gather_vectors(position()[1] % 4, vecs, vec_s)
    segs = [load_segment(mat_s.at[m], vec_s.at[m], 0) for m in range(4)]
    store_segment(out, join(join(segs[0], segs[1]), join(segs[2], segs[3])), False)


def split3(x):
    hi = x.astype(BF16)
    rest = x - hi.astype(F32)
    mid = rest.astype(BF16)
    low = (rest - mid.astype(F32)).astype(BF16)
    return hi, mid, low


def slot_tables(cells, wells):
    cell = cells[...]
    row = jnp.bitwise_and(lax.shift_right_logical(cell, 7), 7) * CX + lax.shift_right_logical(cell, 10)
    shape = (NZ, SLOTS_ALL)
    up = lax.broadcasted_iota(jnp.int32, shape, 0)
    at_row = up == row
    at_layer = up == jnp.bitwise_and(cell, NZ - 1)
    at_well = up == wells[...]
    return at_row, at_layer, at_well


def ones_of(mask):
    return jnp.where(mask, 1.0, 0.0).astype(F32).astype(BF16)


NT = (((1,), (1,)), ((), ()))


def row_times(rows_in, table, dims):
    parts = [part for x in rows_in for part in split3(x)]
    n = len(rows_in)
    pad = 16 - 3 * n
    width = rows_in[0].shape[1]
    stacked = jnp.concatenate([p.astype(F32) for p in parts] + [jnp.zeros((pad, width), F32)], axis=0).astype(BF16)
    out = lax.dot_general(stacked, table, dims, preferred_element_type=F32)
    return [out[3 * i : 3 * i + 1] + out[3 * i + 1 : 3 * i + 2] + out[3 * i + 2 : 3 * i + 3] for i in range(n)]


def make_solve_kernel(whole):
    def kernel(*refs):
        inner, outer = (refs[0:4], refs[4:8]), (refs[8:12], refs[12:16])
        rest = refs[16:] if whole else refs[24:]
        sinv, tau_r, rhs, cells, wells, weights = rest[:6]
        p_out, ends, msg_a, msg_b = rest[6:10]
        mat_i, vec_i, mat_o, vec_o, edge = rest[10:]
        gx, gy = position()
        z_at, y_at = gy % 4, gy // 4
        if whole:
            gather_both(z_at, inner, mat_i, vec_i)
            gather_both(y_at, outer, mat_o, vec_o)
        else:
            gather_matrices(z_at, inner, mat_i)
            gather_matrices(y_at, outer, mat_o)
            gather_vectors(z_at, refs[16:20], vec_i)
            gather_vectors(y_at, refs[20:24], vec_o)
        zero = jnp.zeros(PLANE, F32)
        before = ((zero,) * 4, (zero,) * 2)
        after = ((zero,) * 4, (zero,) * 2)
        for mat_s, vec_s, here in ((mat_o, vec_o, y_at), (mat_i, vec_i, z_at)):
            for m in range(3):
                seg = load_segment(mat_s.at[m], vec_s.at[m], 0)
                before = choose(m < here, join_before(before, seg), before)
                m = 3 - m
                seg = load_segment(mat_s.at[m], vec_s.at[m], 0)
                after = choose(m > here, join_after(seg, after), after)
        own = load_segment(mat_i.at[z_at], vec_i.at[z_at], 0)
        ff, fl, lf, ll, gf, gl = own
        up_m, up_v = join_before(before, own)
        last = mv(inv2(one_minus(mm(up_m, after[0]))), madd(up_v, mv(up_m, after[1])))
        beyond = madd(after[1], mv(after[0], last))
        k = inv2(one_minus(mm(ff, before[0])))
        first = mv(k, madd(madd(gf, mv(ff, before[1])), mv(fl, beyond)))
        behind = madd(before[1], mv(before[0], first))
        for c in range(2):
            ends[c] = behind[c]
            ends[2 + c] = beyond[c]

        def tau(j):
            return pair_at(tau_r, j)

        def sv(j):
            return block_at(sinv, j)

        r = [pair_at(rhs, j) for j in range(CY)]
        r[0] = tuple(r[0][c] + tau(0)[c] * behind[c] for c in range(2))
        y = sweep_forward(sv, tau, r)
        u = beyond
        for j in range(CY - 1, -1, -1):
            u = mv(sv(j), tuple(y[j][c] + tau(j + 1)[c] * u[c] for c in range(2)))
            for c in range(2):
                p_out[c, j] = u[c]
                edge[0, c * CY + j : c * CY + j + 1, :] = u[c][0:1, :]
                edge[1, c * CY + j : c * CY + j + 1, :] = u[c][CX - 1 : CX, :]
        at_row, at_layer, at_well = slot_tables(cells, wells)
        pressure = jnp.concatenate([p_out[0, j] for j in range(CY)], axis=0)
        table = ones_of(at_layer)
        picked = sum(jnp.dot(part, table, preferred_element_type=F32) for part in split3(pressure))
        values = jnp.sum(jnp.where(at_row, picked, 0.0), axis=0, keepdims=True)
        w = weights[...]
        sums, totals = row_times([w * values, w], ones_of(at_well), NT)
        tail = jnp.concatenate([sums, totals, jnp.zeros((6, W_ALL), F32)], axis=0)
        even = gx % 2 == 0
        low, high = edge[0], edge[1]
        msg_a[0:16, :] = jnp.where(even, high, low)
        msg_b[0:16, :] = jnp.where(even, low, high)
        msg_a[16:24, :] = tail
        msg_b[16:24, :] = tail

    return kernel


def apply_operator(got, cells, wells, weights):
    gx = position()[0]
    got_a, sent_b, got_d, got_b, got_c = got
    tail = sent_b[16:24, :] + got_b[16:24, :] + got_c[...] + got_d[...]
    rates = tail[0:1] / jnp.maximum(tail[1:2], 1.0)
    at_row, at_layer, at_well = slot_tables(cells, wells)
    slot_rate = row_times([rates], ones_of(at_well), (((1,), (0,)), ((), ())))[0]
    added = jnp.where(at_layer, weights[...] * slot_rate, 0.0)
    table = ones_of(at_row)
    well_add = sum(lax.dot_general(table, part, NT, preferred_element_type=F32) for part in split3(added))
    even = gx % 2 == 0
    halo_a, halo_b = got_a[0:16, :], got_b[0:16, :]
    from_after = jnp.where(gx < N_GX - 1, jnp.where(even, halo_a, halo_b), 0.0)
    from_before = jnp.where(gx > 0, jnp.where(even, halo_b, halo_a), 0.0)
    return well_add, from_after, from_before


def operator_plane(c, j, p, ends, dmat, tx, ty, tz, lx_in, ly_in, halo, well_add):
    from_after, from_before = halo
    here = p[c, j]
    up = p[c, j + 1] if j < CY - 1 else ends[2 + c]
    down = p[c, j - 1] if j > 0 else ends[c]
    t = tx[c, j]
    at = c * CY + j
    beside = t * from_row_after(here, from_after[at : at + 1])
    beside = beside + from_row_before(t * here, lx_in[c, j : j + 1, :] * from_before[at : at + 1])
    beside = beside + ty[c, j] * up + (ty[c, j - 1] if j else ly_in[c]) * down
    tzp = tz[c, j]
    beside = beside + tzp * pltpu.roll(here, NZ - 1, 1) + pltpu.roll(tzp * here, 1, 1)
    out = dmat[2 * c, j] * p[0, j] + dmat[2 * c + 1, j] * p[1, j] - beside
    if c == 0:
        out = out + well_add[j * CX : (j + 1) * CX]
    return out


def first_image_kernel(got_a, sent_b, got_d, got_b, got_c, p, ends, dmat, tau_r, sinv, binv, rhs, tx, ty, tz, lx_in, ly_in, cells, wells, weights, q_out, e_out, vec_out, dots):
    well_add, after, before = apply_operator((got_a, sent_b, got_d, got_b, got_c), cells, wells, weights)
    eq = jnp.zeros(PLANE, F32)
    qq = jnp.zeros(PLANE, F32)
    e = []
    for j in range(CY):
        pair = []
        for c in range(2):
            q = operator_plane(c, j, p, ends, dmat, tx, ty, tz, lx_in, ly_in, (after, before), well_add)
            rest = rhs[c, j] - q
            q_out[c, j] = q
            e_out[c, j] = rest
            eq = eq + rest * q
            qq = qq + q * q
            pair.append(rest)
        e.append(tuple(pair))
    dots[0] = eq
    dots[1] = qq

    def tau(j):
        return pair_at(tau_r, j)

    y = sweep_forward(lambda j: block_at(sinv, j), tau, e)[CY - 1]
    z = sweep_backward(lambda j: block_at(binv, j), tau, e)
    first = mv(block_at(binv, 0), z)
    last = mv(block_at(sinv, CY - 1), y)
    for c in range(2):
        vec_out[c] = first[c]
        vec_out[2 + c] = last[c]


def second_image_kernel(got_a, sent_b, got_d, got_b, got_c, p, ends, dmat, tx, ty, tz, lx_in, ly_in, cells, wells, weights, q_in, e_in, dots_in, s_out, dots):
    well_add, after, before = apply_operator((got_a, sent_b, got_d, got_b, got_c), cells, wells, weights)
    sq = jnp.zeros(PLANE, F32)
    ss = jnp.zeros(PLANE, F32)
    es = jnp.zeros(PLANE, F32)
    for j in range(CY):
        for c in range(2):
            s = operator_plane(c, j, p, ends, dmat, tx, ty, tz, lx_in, ly_in, (after, before), well_add)
            s_out[c, j] = s
            sq = sq + s * q_in[c, j]
            ss = ss + s * s
            es = es + s * e_in[c, j]
    sums = [jnp.sum(x, axis=0, keepdims=True) for x in (dots_in[0], dots_in[1], sq, ss, es)]
    dots[...] = jnp.concatenate(sums + [jnp.zeros((3, NZ), F32)], axis=0)


def finish_kernel(got, p, w, q, e, s, x_out, r_out):
    total = got[0]
    for d in range(1, N_GY):
        total = total + got[d]
    total = jnp.broadcast_to(jnp.sum(total, axis=1, keepdims=True), (8, NZ))
    eq, qq, sq, ss, es = (total[i : i + 1] for i in range(5))
    rest = -eq / qq
    g = sq / qq
    k = (es - g * eq) / (ss - g * sq)
    on_p = (1.0 - rest) - k * g
    on_q = rest + k * g
    for c in range(2):
        for j in range(CY):
            at = pl.ds(j, CX, stride=CY)
            x_out.at[c][at, :] = on_p * p[c, j] + k * w[c, j]
            r_out.at[c][at, :] = e[c, j] + on_q * q[c, j] - k * s[c, j]


def call(kernel, name, outs, scratch, *args, specs=None, vmem=24 * 1024):
    outs = [o if isinstance(o, jax.ShapeDtypeStruct) else jax.ShapeDtypeStruct(o, F32) for o in outs]
    return pl.pallas_call(
        kernel,
        name=name,
        out_shape=tuple(outs),
        in_specs=specs or [VMEM] * len(args),
        out_specs=tuple(VMEM for _ in outs),
        scratch_shapes=[pltpu.VMEM(s, F32) if isinstance(s, tuple) else s for s in scratch],
        compiler_params=pltpu.CompilerParams(vmem_limit_bytes=vmem * 1024),
    )(*args)


def swapped(block, stride):
    others = [lax.ppermute(block, "gy", [(i, i ^ (k * stride)) for i in range(N_GY)]) for k in PARTNERS[1:]]
    return [block] + others


def exchange_rows(msg_a, msg_b):
    got_a = lax.ppermute(msg_a, "gx", [(i, i ^ 1) for i in range(N_GX)])
    below = lax.broadcasted_iota(jnp.int32, msg_b.shape, 0) >= 16
    tail = msg_b[16:] + got_a[16:]
    sent_b = msg_b + jnp.where(below, got_a, 0.0)
    got_d = lax.ppermute(tail, "gx", [(i, (i + 2 if i % 2 else i - 2) % N_GX) for i in range(N_GX)])
    got_b = lax.ppermute(sent_b, "gx", [(i, (i + 1 if i % 2 else i - 1) % N_GX) for i in range(N_GX)])
    got_c = lax.ppermute(tail, "gx", [(i, i ^ 4) for i in range(N_GX)])
    return got_a, sent_b, got_d, got_b, got_c


def sum_everywhere(x):
    x = x + lax.ppermute(x, "gx", [(i, i ^ 1) for i in range(N_GX)])
    others = [lax.ppermute(x, "gx", [(i, (i + 2 * k) % N_GX) for i in range(N_GX)]) for k in (1, 3, 2)]
    x = x + others[0] + others[1] + others[2]
    x = jnp.broadcast_to(x[None], (N_GY,) + x.shape)
    return lax.all_to_all(x, "gy", split_axis=0, concat_axis=0, tiled=True)


def body(right_side, accumulation, trans_x, trans_y, trans_z, perf_cell, perf_well, perf_weight, perf_count, breaks):

    def flat(a):
        return a.reshape(a.shape[0], CX * CY, NZ)

    field, block, part = (2, CY, CX, NZ), (4, CY, CX, NZ), (2, CY + 1, CX, NZ)
    half, vec, message = (20, 8, NZ), (4, CX, NZ), (24, NZ)
    order = [(4, 16, CX, NZ), (4, 4, CX, NZ)]
    two, four = (2, CX * CY, NZ), (4, CX * CY, NZ)
    sx, edge = call(
        edges_kernel, "edges", ((2, CY, NZ), (40, NZ)),
        [two, pltpu.VMEM((1, NZ), jnp.int32), pltpu.SemaphoreType.DMA((4,))],
        flat(trans_x), flat(trans_y), breaks, specs=[HBM] * 3, vmem=EDGES_VMEM,
    )
    rhs, tx, ty, tz, diag, cross = call(
        prepare_kernel, "prepare", (field,) * 6,
        [two, four, two, two, two, pltpu.SemaphoreType.DMA((5,))],
        flat(right_side), flat(accumulation), flat(trans_x), flat(trans_y), flat(trans_z),
        specs=[HBM] * 5, vmem=PREPARE_VMEM,
    )
    edges = swapped(edge, 1)
    lx = lax.ppermute(sx, "gx", [(i, i + 1) for i in range(N_GX - 1)])
    *edges, lx = lax.optimization_barrier((*edges, lx))
    relayed = swapped(relay(*edges), 4)
    slots = perf_cell.shape[3]
    live = jnp.arange(slots, dtype=jnp.int32)[None, :] < perf_count.reshape(N_GX, 1)
    weights = jnp.where(live, perf_weight.reshape(N_GX, slots), 0.0).reshape(1, SLOTS_ALL)
    owners = jnp.arange(N_GX, dtype=jnp.int32)[:, None] * 16
    wells = (perf_well.reshape(N_GX, slots) + owners).reshape(1, SLOTS_ALL)
    cells = perf_cell.reshape(1, SLOTS_ALL)
    perfs = (cells, wells, weights)

    own_a, own_b, dmat, tau, sinv, binv, ly = call(
        condense_kernel, "condense", (half, half, block, part, block, block, (2, CX, NZ)),
        [(N_GY, NZ), (4, 2 * CX, NZ), (4, 2 * CX, NZ)], diag, cross, ty, rhs, lx, *edges, *relayed,
    )
    inner, outer = [], []
    for own in (own_a, own_b):
        inner.append(swapped(own, 1))
    for near in inner:
        (group,) = call(total_half_kernel, "group_total", (half,), [(4,) + half], *near)
        outer.append(swapped(group, 4))
    inner = inner[0] + inner[1]
    outer = outer[0] + outer[1]
    solve_scratch = order + order + [(2, 16, NZ)]
    p, ends, msg_a, msg_b = call(
        make_solve_kernel(True), "solve_first", (field, vec, message, message), solve_scratch,
        *inner, *outer, sinv, tau, rhs, *perfs,
    )
    got = exchange_rows(msg_a, msg_b)
    q, e, own_v, dots = call(
        first_image_kernel, "first_image", (field, field, vec, (2, CX, NZ)), [],
        *got, p, ends, dmat, tau, sinv, binv, rhs, tx, ty, tz, lx, ly, *perfs,
    )
    inner_v = swapped(own_v, 1)
    (group_v,) = call(total_again_kernel, "group_total_again", (vec,), order, *inner, *inner_v)
    outer_v = swapped(group_v, 4)
    w, ends, msg_a, msg_b = call(
        make_solve_kernel(False), "solve_second", (field, vec, message, message), solve_scratch,
        *inner, *outer, *inner_v, *outer_v, sinv, tau, e, *perfs,
    )
    got = exchange_rows(msg_a, msg_b)
    s, dots = call(
        second_image_kernel, "second_image", (field, (8, NZ)), [],
        *got, w, ends, dmat, tx, ty, tz, lx, ly, *perfs, q, e, dots,
    )
    dots = sum_everywhere(dots)
    x, r = call(finish_kernel, "finish", (two, two), [], dots, p, w, q, e, s)
    shape = (2, CX, CY, NZ)
    return x.reshape(shape), r.reshape(shape)


def solution(mesh):
    tile = P(None, "gx", "gy", None)
    slots = P("gx", "gy", None, None)
    return jax.shard_map(
        body,
        mesh=mesh,
        in_specs=(tile,) * 5 + (slots,) * 3 + (P("gx", "gy", None), P(("gx", "gy"), None)),
        out_specs=(tile, tile),
        check_vma=False,
    )
```

```python
import jax
import jax.numpy as jnp
from jax import lax
from jax.experimental import pallas as pl
from jax.experimental.pallas import tpu as pltpu
from jax.sharding import PartitionSpec as P

F32 = jnp.float32
BF16 = jnp.bfloat16
VMEM = pl.BlockSpec(memory_space=pltpu.VMEM)
HBM = pl.BlockSpec(memory_space=pltpu.HBM)
SMEM = pl.BlockSpec(memory_space=pltpu.SMEM)
CX, CY, NZ = 16, 8, 128
PLANE = (CX, NZ)
N_GX, N_GY = 8, 16
W_ALL = 128
PARTNERS = (0, 2, 1, 3)
PREPARE_VMEM = 54400
EDGES_VMEM = 55296
SLOTS_ALL = 256


def mm(p, q):
    return (
        p[0] * q[0] + p[1] * q[2],
        p[0] * q[1] + p[1] * q[3],
        p[2] * q[0] + p[3] * q[2],
        p[2] * q[1] + p[3] * q[3],
    )


def mv(p, v):
    return (p[0] * v[0] + p[1] * v[1], p[2] * v[0] + p[3] * v[1])


def madd(p, q):
    return tuple(a + b for a, b in zip(p, q))


def inv2(p):
    t = 1.0 / (p[0] * p[3] - p[1] * p[2])
    return (p[3] * t, -p[1] * t, -p[2] * t, p[0] * t)


def one_minus(p):
    return (1.0 - p[0], -p[1], -p[2], 1.0 - p[3])


def rows_by(t, p):
    return (t[0] * p[0], t[0] * p[1], t[1] * p[2], t[1] * p[3])


def columns_by(p, t):
    return (p[0] * t[0], p[1] * t[1], p[2] * t[0], p[3] * t[1])


def join(a, b):
    ff1, fl1, lf1, ll1, gf1, gl1 = a
    ff2, fl2, lf2, ll2, gf2, gl2 = b
    k = inv2(one_minus(mm(ll1, ff2)))
    last = mv(k, madd(gl1, mv(ll1, gf2)))
    last_b = mm(k, lf1)
    last_a = mm(k, mm(ll1, fl2))
    first = madd(gf2, mv(ff2, last))
    first_b = mm(ff2, last_b)
    first_a = madd(fl2, mm(ff2, last_a))
    return (
        madd(ff1, mm(fl1, first_b)),
        mm(fl1, first_a),
        mm(lf2, last_b),
        madd(ll2, mm(lf2, last_a)),
        madd(gf1, mv(fl1, first)),
        madd(gl2, mv(lf2, last)),
    )


def join_before(before, s):
    gm, g = before
    ff, fl, lf, ll, gf, gl = s
    k = inv2(one_minus(mm(ff, gm)))
    a = mv(k, madd(gf, mv(ff, g)))
    am = mm(k, fl)
    return (madd(ll, mm(lf, mm(gm, am))), madd(gl, mv(lf, madd(g, mv(gm, a)))))


def join_after(s, after):
    gm, g = after
    ff, fl, lf, ll, gf, gl = s
    k = inv2(one_minus(mm(ll, gm)))
    a = mv(k, madd(gl, mv(ll, g)))
    am = mm(k, lf)
    return (madd(ff, mm(fl, mm(gm, am))), madd(gf, mv(fl, madd(g, mv(gm, a)))))


def position():
    return lax.axis_index("gx"), lax.axis_index("gy")


def choose(flag, new, old):
    return tuple(tuple(jnp.where(flag, n, o) for n, o in zip(ns, os)) for ns, os in zip(new, old))


def load_segment(mat, vec, offset):
    m = [mat[i] for i in range(16)]
    v = [vec[offset + i] for i in range(4)]
    return (tuple(m[0:4]), tuple(m[4:8]), tuple(m[8:12]), tuple(m[12:16]), (v[0], v[1]), (v[2], v[3]))


def store_segment(ref, seg, whole):
    flat = [x for part in seg for x in part]
    if not whole:
        flat = flat[16:]
    for i, x in enumerate(flat):
        ref[i] = x


def lanes():
    return lax.broadcasted_iota(jnp.int32, PLANE, 1)


def rows():
    return lax.broadcasted_iota(jnp.int32, PLANE, 0)


def from_row_before(plane, edge):
    return jnp.where(rows() == 0, edge, pltpu.roll(plane, 1, 0))


def from_row_after(plane, edge):
    return jnp.where(rows() == CX - 1, edge, pltpu.roll(plane, CX - 1, 0))


def sweep_forward(sinv, tau, rhs):
    y = [rhs[0]]
    for j in range(1, CY):
        t = mv(sinv(j - 1), y[-1])
        y.append((rhs[j][0] + tau(j)[0] * t[0], rhs[j][1] + tau(j)[1] * t[1]))
    return y


def sweep_backward(binv, tau, rhs):
    z = rhs[CY - 1]
    for j in range(CY - 2, -1, -1):
        t = mv(binv(j + 1), z)
        z = (rhs[j][0] + tau(j + 1)[0] * t[0], rhs[j][1] + tau(j + 1)[1] * t[1])
    return z


def block_at(ref, j):
    return tuple(ref[i, j] for i in range(4))


def pair_at(ref, j):
    return (ref[0, j], ref[1, j])


def plane(ref, c, j):
    return ref.at[c][pl.ds(j, CX, stride=CY), :]


def edges_kernel(tx_h, ty_h, brk_h, sx, edge, ty, brk, sems):
    copies = [pltpu.make_async_copy(h, v, sems.at[i]) for i, (h, v) in enumerate(((ty_h, ty), (brk_h, brk)))]
    copies += [
        pltpu.make_async_copy(tx_h.at[c, (CX - 1) * CY : CX * CY, :], sx.at[c], sems.at[2 + c]) for c in range(2)
    ]
    for copy in copies:
        copy.start()
    for copy in copies:
        copy.wait()
    edge[2 * CX :, :] = jnp.broadcast_to(brk[...].astype(F32), (8, NZ))
    for c in range(2):
        edge[c * CX : (c + 1) * CX, :] = plane(ty, c, CY - 1)


def relay(*messages):
    z = position()[1] % 4
    row = lax.broadcasted_iota(jnp.int32, messages[0].shape, 0)
    out = jnp.zeros_like(messages[0])
    for k, ref in enumerate(messages):
        out = jnp.where(jnp.where(row < 2 * CX, z == 3 - PARTNERS[k], row == 2 * CX + k), ref, out)
    return out


def prepare_kernel(b_h, acc_h, tx_h, ty_h, tz_h, rhs, tx_o, ty_o, tz_o, diag, cross, b, acc, tx_v, ty_v, tz_v, sems):
    gx, gy = position()
    pairs = ((tx_h, tx_v), (ty_h, ty_v), (tz_h, tz_v), (acc_h, acc), (b_h, b))
    copies = [pltpu.make_async_copy(h, v, sems.at[i]) for i, (h, v) in enumerate(pairs)]
    for copy in copies:
        copy.start()
    last_x = jnp.logical_and(rows() == CX - 1, gx == N_GX - 1)
    last_z = lanes() == NZ - 1
    for copy in copies:
        copy.wait()
    for c in range(2):
        ly = 0.0
        for j in range(CY):
            tx = jnp.where(last_x, 0.0, plane(tx_v, c, j))
            tz = jnp.where(last_z, 0.0, plane(tz_v, c, j))
            ty = plane(ty_v, c, j)
            if j == CY - 1:
                ty = jnp.where(gy == N_GY - 1, 0.0, ty)
            tx_o[c, j] = tx
            tz_o[c, j] = tz
            ty_o[c, j] = ty
            faces = tx + from_row_before(tx, 0.0) + ty + ly + tz + pltpu.roll(tz, 1, 1)
            diag[c, j] = plane(acc, 3 * c, j) + faces
            cross[c, j] = plane(acc, 2 - c, j)
            rhs[c, j] = plane(b, c, j)
            ly = ty


def condense_kernel(diag, cross, ty, rhs, lx_in, *refs):
    messages, relayed = refs[:4], refs[4:8]
    seg_a, seg_b, dmat, tau_o, sinv, binv, ly_in = refs[8:15]
    brk, near, far = refs[15:]
    gy = position()[1]
    z_at, y_at = gy % 4, gy // 4
    for k in range(4):
        near[jnp.bitwise_xor(z_at, PARTNERS[k])] = messages[k][0 : 2 * CX, :]
        at = jnp.bitwise_xor(y_at, PARTNERS[k])
        far[at] = relayed[k][0 : 2 * CX, :]
        for i in range(4):
            row = relayed[k][2 * CX + i : 2 * CX + i + 1, :]
            brk[pl.ds(4 * at + jnp.bitwise_xor(z_at, PARTNERS[i]), 1), :] = row
    cuts = pltpu.roll(brk[...], (NZ - CY * gy) % NZ, 1)
    before = jnp.where(y_at > 0, far[jnp.maximum(y_at - 1, 0)], 0.0)
    before = jnp.where(z_at > 0, near[jnp.maximum(z_at - 1, 0)], before)
    for c in range(2):
        ly_in[c] = before[c * CX : (c + 1) * CX]
    for c in range(2):
        ly = ly_in[c]
        for j in range(CY):
            d = diag[c, j] + jnp.where(rows() == 0, lx_in[c, j : j + 1, :], 0.0)
            dmat[3 * c, j] = d + ly if j == 0 else d
        for j in range(CY + 1):
            keep = 1.0 - cuts[:, j : j + 1]
            tau_o[c, j] = (ty[c, j - 1] if j else ly) * keep
    for j in range(CY):
        dmat[1, j] = cross[0, j]
        dmat[2, j] = cross[1, j]

    def tau(j):
        return pair_at(tau_o, j)

    def outer(t, p):
        return tuple(x * y for x, y in zip(p, (t[0] * t[0], t[0] * t[1], t[1] * t[0], t[1] * t[1])))

    s = inv2(block_at(dmat, 0))
    e = inv2(block_at(dmat, CY - 1))
    zero = jnp.zeros(PLANE, F32)
    yf = (tau(0)[0], zero, zero, tau(0)[1])
    zl = (tau(CY)[0], zero, zero, tau(CY)[1])
    y = pair_at(rhs, 0)
    z = pair_at(rhs, CY - 1)
    for i in range(4):
        sinv[i, 0] = s[i]
        binv[i, CY - 1] = e[i]
    for j in range(1, CY):
        k = CY - 1 - j
        t, u = tau(j), tau(k + 1)
        yf = rows_by(t, mm(s, yf))
        zl = rows_by(u, mm(e, zl))
        yv, zv = mv(s, y), mv(e, z)
        y = tuple(rhs[c, j] + t[c] * yv[c] for c in range(2))
        z = tuple(rhs[c, k] + u[c] * zv[c] for c in range(2))
        s = inv2(tuple(d - x for d, x in zip(block_at(dmat, j), outer(t, s))))
        e = inv2(tuple(d - x for d, x in zip(block_at(dmat, k), outer(u, e))))
        for i in range(4):
            sinv[i, j] = s[i]
            binv[i, k] = e[i]
    whole = (columns_by(e, tau(0)), mm(e, zl), mm(s, yf), columns_by(s, tau(CY)), mv(e, z), mv(s, y))
    for half, ref in enumerate((seg_a, seg_b)):
        store_segment(ref, [[x[8 * half : 8 * half + 8] for x in part] for part in whole], True)


def gather_matrices(at_place, halves, mat_s):
    for k in range(4):
        at = jnp.bitwise_xor(at_place, PARTNERS[k])
        for half, refs in enumerate(halves):
            mat_s[at, :, 8 * half : 8 * half + 8, :] = refs[k][0:16]


def gather_vectors(at_place, vecs, vec_s):
    for k in range(4):
        vec_s[jnp.bitwise_xor(at_place, PARTNERS[k])] = vecs[k][...]


def gather_both(at_place, halves, mat_s, vec_s):
    gather_matrices(at_place, halves, mat_s)
    for k in range(4):
        at = jnp.bitwise_xor(at_place, PARTNERS[k])
        for half, refs in enumerate(halves):
            vec_s[at, :, 8 * half : 8 * half + 8, :] = refs[k][16:20]


def total_half_kernel(own, m1, m2, m3, out, segs_s):
    for k, ref in enumerate((own, m1, m2, m3)):
        segs_s[jnp.bitwise_xor(position()[1] % 4, PARTNERS[k])] = ref[...]
    segs = [load_segment(segs_s.at[m], segs_s.at[m], 16) for m in range(4)]
    store_segment(out, join(join(segs[0], segs[1]), join(segs[2], segs[3])), True)


def total_again_kernel(*refs):
    halves, vecs = (refs[0:4], refs[4:8]), refs[8:12]
    out, mat_s, vec_s = refs[12:]
    gather_matrices(position()[1] % 4, halves, mat_s)
    gather_vectors(position()[1] % 4, vecs, vec_s)
    segs = [load_segment(mat_s.at[m], vec_s.at[m], 0) for m in range(4)]
    store_segment(out, join(join(segs[0], segs[1]), join(segs[2], segs[3])), False)


def split3(x):
    hi = x.astype(BF16)
    rest = x - hi.astype(F32)
    mid = rest.astype(BF16)
    low = (rest - mid.astype(F32)).astype(BF16)
    return hi, mid, low


def slot_tables(cells, wells):
    cell = cells[...]
    row = jnp.bitwise_and(lax.shift_right_logical(cell, 7), 7) * CX + lax.shift_right_logical(cell, 10)
    shape = (NZ, SLOTS_ALL)
    up = lax.broadcasted_iota(jnp.int32, shape, 0)
    at_row = up == row
    at_layer = up == jnp.bitwise_and(cell, NZ - 1)
    at_well = up == wells[...]
    return at_row, at_layer, at_well


def ones_of(mask):
    return jnp.where(mask, 1.0, 0.0).astype(F32).astype(BF16)


NT = (((1,), (1,)), ((), ()))


def row_times(rows_in, table, dims):
    parts = [part for x in rows_in for part in split3(x)]
    n = len(rows_in)
    pad = 16 - 3 * n
    width = rows_in[0].shape[1]
    stacked = jnp.concatenate([p.astype(F32) for p in parts] + [jnp.zeros((pad, width), F32)], axis=0).astype(BF16)
    out = lax.dot_general(stacked, table, dims, preferred_element_type=F32)
    return [out[3 * i : 3 * i + 1] + out[3 * i + 1 : 3 * i + 2] + out[3 * i + 2 : 3 * i + 3] for i in range(n)]


def make_inner_kernel(whole):
    def kernel(*refs):
        halves = (refs[0:4], refs[4:8])
        vecs, rest = (None, refs[8:]) if whole else (refs[8:12], refs[12:])
        if whole:
            sinv, tau_r, rhs, left, right, base, from_left, from_right, mat_s, vec_s = rest
        else:
            sinv, tau_r, rhs, left, right, base, mat_s, vec_s = rest
        z = position()[1] % 4
        if whole:
            gather_both(z, halves, mat_s, vec_s)
        else:
            gather_matrices(z, halves, mat_s)
            gather_vectors(z, vecs, vec_s)
        segs = [load_segment(mat_s.at[m], vec_s.at[m], 0) for m in range(4)]
        pair = join(segs[0], segs[1])
        store_segment(left, choose(z == 1, segs[0], choose(z == 2, pair, join(pair, segs[2]))), True)
        pair = join(segs[2], segs[3])
        store_segment(right, choose(z == 2, segs[3], choose(z == 1, pair, join(segs[1], pair))), True)

        def tau(j):
            return pair_at(tau_r, j)

        def sv(j):
            return block_at(sinv, j)

        y = sweep_forward(sv, tau, [pair_at(rhs, j) for j in range(CY)])
        u = None
        for j in range(CY - 1, -1, -1):
            v = y[j] if u is None else tuple(y[j][c] + tau(j + 1)[c] * u[c] for c in range(2))
            u = mv(sv(j), v)
            for c in range(2):
                base[c, j] = u[c]
        if not whole:
            return
        zero = jnp.zeros(PLANE, F32)
        units = [(tau(0)[0], zero, zero, tau(0)[1])]
        for j in range(1, CY):
            units.append(rows_by(tau(j), mm(sv(j - 1), units[-1])))
        ul = ur = None
        for j in range(CY - 1, -1, -1):
            if ul is None:
                ul = mm(sv(j), units[j])
                ur = columns_by(sv(j), tau(CY))
            else:
                ul = mm(sv(j), madd(units[j], rows_by(tau(j + 1), ul)))
                ur = mm(sv(j), rows_by(tau(j + 1), ur))
            for i in range(4):
                from_left[i, j] = ul[i]
                from_right[i, j] = ur[i]

    return kernel


def make_solve_kernel(whole):
    def kernel(*refs):
        own_m, outer = refs[0:2], (refs[2:6], refs[6:10])
        own_v, outer_v, rest = (None, None, refs[10:]) if whole else (refs[10], refs[11:15], refs[15:])
        left, right, base, from_left, from_right, cells, wells, weights = rest[:8]
        p_out, ends, msg_a, msg_b = rest[8:12]
        mat_o, vec_o, mat_i, vec_i, edge = rest[12:]
        gx, gy = position()
        z_at, y_at = gy % 4, gy // 4
        for half, ref in enumerate(own_m):
            mat_i[:, 8 * half : 8 * half + 8, :] = ref[0:16]
            if whole:
                vec_i[:, 8 * half : 8 * half + 8, :] = ref[16:20]
        if whole:
            gather_both(y_at, outer, mat_o, vec_o)
        else:
            vec_i[...] = own_v[...]
            gather_matrices(y_at, outer, mat_o)
            gather_vectors(y_at, outer_v, vec_o)
        zero = jnp.zeros(PLANE, F32)
        before = ((zero,) * 4, (zero,) * 2)
        after = ((zero,) * 4, (zero,) * 2)
        for m in range(3):
            seg = load_segment(mat_o.at[m], vec_o.at[m], 0)
            before = choose(m < y_at, join_before(before, seg), before)
            m = 3 - m
            seg = load_segment(mat_o.at[m], vec_o.at[m], 0)
            after = choose(m > y_at, join_after(seg, after), after)
        before = choose(z_at > 0, join_before(before, load_segment(left, left, 16)), before)
        after = choose(z_at < 3, join_after(load_segment(right, right, 16), after), after)
        own = load_segment(mat_i, vec_i, 0)
        ff, fl, lf, ll, gf, gl = own
        up_m, up_v = join_before(before, own)
        last = mv(inv2(one_minus(mm(up_m, after[0]))), madd(up_v, mv(up_m, after[1])))
        beyond = madd(after[1], mv(after[0], last))
        k = inv2(one_minus(mm(ff, before[0])))
        first = mv(k, madd(madd(gf, mv(ff, before[1])), mv(fl, beyond)))
        behind = madd(before[1], mv(before[0], first))
        for c in range(2):
            ends[c] = behind[c]
            ends[2 + c] = beyond[c]

        for j in range(CY):
            u = madd(pair_at(base, j), madd(mv(block_at(from_left, j), behind), mv(block_at(from_right, j), beyond)))
            for c in range(2):
                p_out[c, j] = u[c]
                edge[0, c * CY + j : c * CY + j + 1, :] = u[c][0:1, :]
                edge[1, c * CY + j : c * CY + j + 1, :] = u[c][CX - 1 : CX, :]
        at_row, at_layer, at_well = slot_tables(cells, wells)
        pressure = jnp.concatenate([p_out[0, j] for j in range(CY)], axis=0)
        table = ones_of(at_layer)
        picked = sum(jnp.dot(part, table, preferred_element_type=F32) for part in split3(pressure))
        values = jnp.sum(jnp.where(at_row, picked, 0.0), axis=0, keepdims=True)
        w = weights[...]
        sums, totals = row_times([w * values, w], ones_of(at_well), NT)
        tail = jnp.concatenate([sums, totals, jnp.zeros((6, W_ALL), F32)], axis=0)
        even = gx % 2 == 0
        low, high = edge[0], edge[1]
        msg_a[0:16, :] = jnp.where(even, high, low)
        msg_b[0:16, :] = jnp.where(even, low, high)
        msg_a[16:24, :] = tail
        msg_b[16:24, :] = tail

    return kernel


def apply_operator(got, cells, wells, weights):
    gx = position()[0]
    got_a, sent_b, got_c, got_b, got_d = got
    tail = sent_b[16:24, :] + got_b[16:24, :] + got_c[...] + got_d[...]
    rates = tail[0:1] / jnp.maximum(tail[1:2], 1.0)
    at_row, at_layer, at_well = slot_tables(cells, wells)
    slot_rate = row_times([rates], ones_of(at_well), (((1,), (0,)), ((), ())))[0]
    added = jnp.where(at_layer, weights[...] * slot_rate, 0.0)
    table = ones_of(at_row)
    well_add = sum(lax.dot_general(table, part, NT, preferred_element_type=F32) for part in split3(added))
    even = gx % 2 == 0
    halo_a, halo_b = got_a[0:16, :], got_b[0:16, :]
    from_after = jnp.where(gx < N_GX - 1, jnp.where(even, halo_a, halo_b), 0.0)
    from_before = jnp.where(gx > 0, jnp.where(even, halo_b, halo_a), 0.0)
    return well_add, from_after, from_before


def operator_plane(c, j, p, ends, dmat, tx, ty, tz, lx_in, ly_in, halo, well_add):
    from_after, from_before = halo
    here = p[c, j]
    up = p[c, j + 1] if j < CY - 1 else ends[2 + c]
    down = p[c, j - 1] if j > 0 else ends[c]
    t = tx[c, j]
    at = c * CY + j
    beside = t * from_row_after(here, from_after[at : at + 1])
    beside = beside + from_row_before(t * here, lx_in[c, j : j + 1, :] * from_before[at : at + 1])
    beside = beside + ty[c, j] * up + (ty[c, j - 1] if j else ly_in[c]) * down
    tzp = tz[c, j]
    beside = beside + tzp * pltpu.roll(here, NZ - 1, 1) + pltpu.roll(tzp * here, 1, 1)
    out = dmat[2 * c, j] * p[0, j] + dmat[2 * c + 1, j] * p[1, j] - beside
    if c == 0:
        out = out + well_add[j * CX : (j + 1) * CX]
    return out


def first_image_kernel(got_a, sent_b, got_c, got_b, got_d, p, ends, dmat, tau_r, sinv, binv, rhs, tx, ty, tz, lx_in, ly_in, cells, wells, weights, q_out, e_out, vec_out, dots):
    well_add, after, before = apply_operator((got_a, sent_b, got_c, got_b, got_d), cells, wells, weights)
    eq = jnp.zeros(PLANE, F32)
    qq = jnp.zeros(PLANE, F32)
    e = []
    for j in range(CY):
        pair = []
        for c in range(2):
            q = operator_plane(c, j, p, ends, dmat, tx, ty, tz, lx_in, ly_in, (after, before), well_add)
            rest = rhs[c, j] - q
            q_out[c, j] = q
            e_out[c, j] = rest
            eq = eq + rest * q
            qq = qq + q * q
            pair.append(rest)
        e.append(tuple(pair))
    dots[0] = eq
    dots[1] = qq

    def tau(j):
        return pair_at(tau_r, j)

    y = sweep_forward(lambda j: block_at(sinv, j), tau, e)[CY - 1]
    z = sweep_backward(lambda j: block_at(binv, j), tau, e)
    first = mv(block_at(binv, 0), z)
    last = mv(block_at(sinv, CY - 1), y)
    for c in range(2):
        vec_out[c] = first[c]
        vec_out[2 + c] = last[c]


def second_image_kernel(got_a, sent_b, got_c, got_b, got_d, p, ends, dmat, tx, ty, tz, lx_in, ly_in, cells, wells, weights, q_in, e_in, dots_in, s_out, dots):
    well_add, after, before = apply_operator((got_a, sent_b, got_c, got_b, got_d), cells, wells, weights)
    sq = jnp.zeros(PLANE, F32)
    ss = jnp.zeros(PLANE, F32)
    es = jnp.zeros(PLANE, F32)
    for j in range(CY):
        for c in range(2):
            s = operator_plane(c, j, p, ends, dmat, tx, ty, tz, lx_in, ly_in, (after, before), well_add)
            s_out[c, j] = s
            sq = sq + s * q_in[c, j]
            ss = ss + s * s
            es = es + s * e_in[c, j]
    sums = [jnp.sum(x, axis=0, keepdims=True) for x in (dots_in[0], dots_in[1], sq, ss, es)]
    dots[...] = jnp.concatenate(sums + [jnp.zeros((3, NZ), F32)], axis=0)


def finish_kernel(got, p, w, q, e, s, x_out, r_out):
    total = got[0]
    for d in range(1, N_GY):
        total = total + got[d]
    total = jnp.broadcast_to(jnp.sum(total, axis=1, keepdims=True), (8, NZ))
    eq, qq, sq, ss, es = (total[i : i + 1] for i in range(5))
    rest = -eq / qq
    g = sq / qq
    k = (es - g * eq) / (ss - g * sq)
    on_p = (1.0 - rest) - k * g
    on_q = rest + k * g
    for c in range(2):
        for j in range(CY):
            at = pl.ds(j, CX, stride=CY)
            x_out.at[c][at, :] = on_p * p[c, j] + k * w[c, j]
            r_out.at[c][at, :] = e[c, j] + on_q * q[c, j] - k * s[c, j]


def call(kernel, name, outs, scratch, *args, specs=None, vmem=24 * 1024):
    outs = [o if isinstance(o, jax.ShapeDtypeStruct) else jax.ShapeDtypeStruct(o, F32) for o in outs]
    return pl.pallas_call(
        kernel,
        name=name,
        out_shape=tuple(outs),
        in_specs=specs or [VMEM] * len(args),
        out_specs=tuple(VMEM for _ in outs),
        scratch_shapes=[pltpu.VMEM(s, F32) if isinstance(s, tuple) else s for s in scratch],
        compiler_params=pltpu.CompilerParams(vmem_limit_bytes=vmem * 1024),
    )(*args)


def swapped(block, stride):
    others = [lax.ppermute(block, "gy", [(i, i ^ (k * stride)) for i in range(N_GY)]) for k in PARTNERS[1:]]
    return [block] + others


def exchange_rows(msg_a, msg_b):
    got_a = lax.ppermute(msg_a, "gx", [(i, i ^ 1) for i in range(N_GX)])
    below = lax.broadcasted_iota(jnp.int32, msg_b.shape, 0) >= 16
    tail = msg_b[16:] + got_a[16:]
    sent_b = msg_b + jnp.where(below, got_a, 0.0)
    got_d = lax.ppermute(tail, "gx", [(i, (i + 2 if i % 2 else i - 2) % N_GX) for i in range(N_GX)])
    got_b = lax.ppermute(sent_b, "gx", [(i, (i + 1 if i % 2 else i - 1) % N_GX) for i in range(N_GX)])
    got_c = lax.ppermute(tail, "gx", [(i, i ^ 4) for i in range(N_GX)])
    return got_a, sent_b, got_c, got_b, got_d


def sum_everywhere(x):
    x = x + lax.ppermute(x, "gx", [(i, i ^ 1) for i in range(N_GX)])
    others = [lax.ppermute(x, "gx", [(i, (i + 2 * k) % N_GX) for i in range(N_GX)]) for k in PARTNERS[1:]]
    x = x + others[0] + others[1] + others[2]
    x = jnp.broadcast_to(x[None], (N_GY,) + x.shape)
    return lax.all_to_all(x, "gy", split_axis=0, concat_axis=0, tiled=True)


def body(right_side, accumulation, trans_x, trans_y, trans_z, perf_cell, perf_well, perf_weight, perf_count, breaks):

    def flat(a):
        return a.reshape(a.shape[0], CX * CY, NZ)

    field, block, part = (2, CY, CX, NZ), (4, CY, CX, NZ), (2, CY + 1, CX, NZ)
    half, vec, message = (20, 8, NZ), (4, CX, NZ), (24, NZ)
    order = [(4, 16, CX, NZ), (4, 4, CX, NZ)]
    two, four = (2, CX * CY, NZ), (4, CX * CY, NZ)
    sx, edge = call(
        edges_kernel, "edges", ((2, CY, NZ), (40, NZ)),
        [two, pltpu.VMEM((1, NZ), jnp.int32), pltpu.SemaphoreType.DMA((4,))],
        flat(trans_x), flat(trans_y), breaks, specs=[HBM] * 3, vmem=EDGES_VMEM,
    )
    rhs, tx, ty, tz, diag, cross = call(
        prepare_kernel, "prepare", (field,) * 6,
        [two, four, two, two, two, pltpu.SemaphoreType.DMA((5,))],
        flat(right_side), flat(accumulation), flat(trans_x), flat(trans_y), flat(trans_z),
        specs=[HBM] * 5, vmem=PREPARE_VMEM,
    )
    edges = swapped(edge, 1)
    lx = lax.ppermute(sx, "gx", [(i, i + 1) for i in range(N_GX - 1)])
    relayed = swapped(relay(*edges), 4)
    slots = perf_cell.shape[3]
    live = jnp.arange(slots, dtype=jnp.int32)[None, :] < perf_count.reshape(N_GX, 1)
    weights = jnp.where(live, perf_weight.reshape(N_GX, slots), 0.0).reshape(1, SLOTS_ALL)
    owners = jnp.arange(N_GX, dtype=jnp.int32)[:, None] * 16
    wells = (perf_well.reshape(N_GX, slots) + owners).reshape(1, SLOTS_ALL)
    cells = perf_cell.reshape(1, SLOTS_ALL)
    perfs = (cells, wells, weights)

    own_a, own_b, dmat, tau, sinv, binv, ly = call(
        condense_kernel, "condense", (half, half, block, part, block, block, (2, CX, NZ)),
        [(N_GY, NZ), (4, 2 * CX, NZ), (4, 2 * CX, NZ)], diag, cross, ty, rhs, lx, *edges, *relayed,
    )
    inner, outer = [], []
    for own in (own_a, own_b):
        inner.append(swapped(own, 1))
    for near in inner:
        (group,) = call(total_half_kernel, "group_total", (half,), [(4,) + half], *near)
        outer.append(swapped(group, 4))
    inner = inner[0] + inner[1]
    outer = outer[0] + outer[1]
    solve_scratch = order + [(16, CX, NZ), (4, CX, NZ), (2, 16, NZ)]
    joined = (20, CX, NZ)
    left, right, base, from_left, from_right = call(
        make_inner_kernel(True), "inner_first", (joined, joined, field, block, block), order, *inner, sinv, tau, rhs,
    )
    owns = (own_a, own_b)
    p, ends, msg_a, msg_b = call(
        make_solve_kernel(True), "solve_first", (field, vec, message, message), solve_scratch,
        *owns, *outer, left, right, base, from_left, from_right, *perfs,
    )
    got = exchange_rows(msg_a, msg_b)
    q, e, own_v, dots = call(
        first_image_kernel, "first_image", (field, field, vec, (2, CX, NZ)), [],
        *got, p, ends, dmat, tau, sinv, binv, rhs, tx, ty, tz, lx, ly, *perfs,
    )
    inner_v = swapped(own_v, 1)
    (group_v,) = call(total_again_kernel, "group_total_again", (vec,), order, *inner, *inner_v)
    outer_v = swapped(group_v, 4)
    left, right, base = call(
        make_inner_kernel(False), "inner_second", (joined, joined, field), order, *inner, *inner_v, sinv, tau, e,
    )
    w, ends, msg_a, msg_b = call(
        make_solve_kernel(False), "solve_second", (field, vec, message, message), solve_scratch,
        *owns, *outer, own_v, *outer_v, left, right, base, from_left, from_right, *perfs,
    )
    got = exchange_rows(msg_a, msg_b)
    s, dots = call(
        second_image_kernel, "second_image", (field, (8, NZ)), [],
        *got, w, ends, dmat, tx, ty, tz, lx, ly, *perfs, q, e, dots,
    )
    dots = sum_everywhere(dots)
    x, r = call(finish_kernel, "finish", (two, two), [], dots, p, w, q, e, s)
    shape = (2, CX, CY, NZ)
    return x.reshape(shape), r.reshape(shape)


def solution(mesh):
    tile = P(None, "gx", "gy", None)
    slots = P("gx", "gy", None, None)
    return jax.shard_map(
        body,
        mesh=mesh,
        in_specs=(tile,) * 5 + (slots,) * 3 + (P("gx", "gy", None), P(("gx", "gy"), None)),
        out_specs=(tile, tile),
        check_vma=False,
    )
```

```python
import jax
import jax.numpy as jnp
from jax import lax
from jax.experimental import pallas as pl
from jax.experimental.pallas import tpu as pltpu
from jax.sharding import PartitionSpec as P

F32 = jnp.float32
BF16 = jnp.bfloat16
VMEM = pl.BlockSpec(memory_space=pltpu.VMEM)
HBM = pl.BlockSpec(memory_space=pltpu.HBM)
SMEM = pl.BlockSpec(memory_space=pltpu.SMEM)
CX, CY, NZ = 16, 8, 128
PLANE = (CX, NZ)
N_GX, N_GY = 8, 16
W_ALL = 128
PARTNERS = (0, 2, 1, 3)
PREPARE_VMEM = 54400
EDGES_VMEM = 55296
SLOTS_ALL = 256


def mm(p, q):
    return (
        p[0] * q[0] + p[1] * q[2],
        p[0] * q[1] + p[1] * q[3],
        p[2] * q[0] + p[3] * q[2],
        p[2] * q[1] + p[3] * q[3],
    )


def mv(p, v):
    return (p[0] * v[0] + p[1] * v[1], p[2] * v[0] + p[3] * v[1])


def madd(p, q):
    return tuple(a + b for a, b in zip(p, q))


def inv2(p):
    t = 1.0 / (p[0] * p[3] - p[1] * p[2])
    return (p[3] * t, -p[1] * t, -p[2] * t, p[0] * t)


def one_minus(p):
    return (1.0 - p[0], -p[1], -p[2], 1.0 - p[3])


def rows_by(t, p):
    return (t[0] * p[0], t[0] * p[1], t[1] * p[2], t[1] * p[3])


def columns_by(p, t):
    return (p[0] * t[0], p[1] * t[1], p[2] * t[0], p[3] * t[1])


def join(a, b):
    ff1, fl1, lf1, ll1, gf1, gl1 = a
    ff2, fl2, lf2, ll2, gf2, gl2 = b
    k = inv2(one_minus(mm(ll1, ff2)))
    last = mv(k, madd(gl1, mv(ll1, gf2)))
    last_b = mm(k, lf1)
    last_a = mm(k, mm(ll1, fl2))
    first = madd(gf2, mv(ff2, last))
    first_b = mm(ff2, last_b)
    first_a = madd(fl2, mm(ff2, last_a))
    return (
        madd(ff1, mm(fl1, first_b)),
        mm(fl1, first_a),
        mm(lf2, last_b),
        madd(ll2, mm(lf2, last_a)),
        madd(gf1, mv(fl1, first)),
        madd(gl2, mv(lf2, last)),
    )


def join_before(before, s):
    gm, g = before
    ff, fl, lf, ll, gf, gl = s
    k = inv2(one_minus(mm(ff, gm)))
    a = mv(k, madd(gf, mv(ff, g)))
    am = mm(k, fl)
    return (madd(ll, mm(lf, mm(gm, am))), madd(gl, mv(lf, madd(g, mv(gm, a)))))


def join_after(s, after):
    gm, g = after
    ff, fl, lf, ll, gf, gl = s
    k = inv2(one_minus(mm(ll, gm)))
    a = mv(k, madd(gl, mv(ll, g)))
    am = mm(k, lf)
    return (madd(ff, mm(fl, mm(gm, am))), madd(gf, mv(fl, madd(g, mv(gm, a)))))


def position():
    return lax.axis_index("gx"), lax.axis_index("gy")


def choose(flag, new, old):
    return tuple(tuple(jnp.where(flag, n, o) for n, o in zip(ns, os)) for ns, os in zip(new, old))


def load_segment(mat, vec, offset):
    m = [mat[i] for i in range(16)]
    v = [vec[offset + i] for i in range(4)]
    return (tuple(m[0:4]), tuple(m[4:8]), tuple(m[8:12]), tuple(m[12:16]), (v[0], v[1]), (v[2], v[3]))


def store_segment(ref, seg, whole):
    flat = [x for part in seg for x in part]
    if not whole:
        flat = flat[16:]
    for i, x in enumerate(flat):
        ref[i] = x


def lanes():
    return lax.broadcasted_iota(jnp.int32, PLANE, 1)


def rows():
    return lax.broadcasted_iota(jnp.int32, PLANE, 0)


def from_row_before(plane, edge):
    return jnp.where(rows() == 0, edge, pltpu.roll(plane, 1, 0))


def from_row_after(plane, edge):
    return jnp.where(rows() == CX - 1, edge, pltpu.roll(plane, CX - 1, 0))


def sweep_forward(sinv, tau, rhs):
    y = [rhs[0]]
    for j in range(1, CY):
        t = mv(sinv(j - 1), y[-1])
        y.append((rhs[j][0] + tau(j)[0] * t[0], rhs[j][1] + tau(j)[1] * t[1]))
    return y


def sweep_backward(binv, tau, rhs):
    z = rhs[CY - 1]
    for j in range(CY - 2, -1, -1):
        t = mv(binv(j + 1), z)
        z = (rhs[j][0] + tau(j + 1)[0] * t[0], rhs[j][1] + tau(j + 1)[1] * t[1])
    return z


def block_at(ref, j):
    return tuple(ref[i, j] for i in range(4))


def pair_at(ref, j):
    return (ref[0, j], ref[1, j])


def plane(ref, c, j):
    return ref.at[c][pl.ds(j, CX, stride=CY), :]


def edges_kernel(tx_h, ty_h, brk_h, sx, edge, ty, brk, sems):
    copies = [pltpu.make_async_copy(h, v, sems.at[i]) for i, (h, v) in enumerate(((ty_h, ty), (brk_h, brk)))]
    copies += [
        pltpu.make_async_copy(tx_h.at[c, (CX - 1) * CY : CX * CY, :], sx.at[c], sems.at[2 + c]) for c in range(2)
    ]
    for copy in copies:
        copy.start()
    for copy in copies:
        copy.wait()
    edge[2 * CX :, :] = jnp.broadcast_to(brk[...].astype(F32), (8, NZ))
    for c in range(2):
        edge[c * CX : (c + 1) * CX, :] = plane(ty, c, CY - 1)


def relay(*messages):
    z = position()[1] % 4
    row = lax.broadcasted_iota(jnp.int32, messages[0].shape, 0)
    out = jnp.zeros_like(messages[0])
    for k, ref in enumerate(messages):
        out = jnp.where(jnp.where(row < 2 * CX, z == 3 - PARTNERS[k], row == 2 * CX + k), ref, out)
    return out


def prepare_kernel(b_h, acc_h, tx_h, ty_h, tz_h, rhs, tx_o, ty_o, tz_o, diag, cross, b, acc, tx_v, ty_v, tz_v, sems):
    gx, gy = position()
    pairs = ((tx_h, tx_v), (ty_h, ty_v), (tz_h, tz_v), (acc_h, acc), (b_h, b))
    copies = [pltpu.make_async_copy(h, v, sems.at[i]) for i, (h, v) in enumerate(pairs)]
    for copy in copies:
        copy.start()
    last_x = jnp.logical_and(rows() == CX - 1, gx == N_GX - 1)
    last_z = lanes() == NZ - 1
    for copy in copies:
        copy.wait()
    for c in range(2):
        ly = 0.0
        for j in range(CY):
            tx = jnp.where(last_x, 0.0, plane(tx_v, c, j))
            tz = jnp.where(last_z, 0.0, plane(tz_v, c, j))
            ty = plane(ty_v, c, j)
            if j == CY - 1:
                ty = jnp.where(gy == N_GY - 1, 0.0, ty)
            tx_o[c, j] = tx
            tz_o[c, j] = tz
            ty_o[c, j] = ty
            faces = tx + from_row_before(tx, 0.0) + ty + ly + tz + pltpu.roll(tz, 1, 1)
            diag[c, j] = plane(acc, 3 * c, j) + faces
            cross[c, j] = plane(acc, 2 - c, j)
            rhs[c, j] = plane(b, c, j)
            ly = ty


def condense_kernel(diag, cross, ty, rhs, lx_in, *refs):
    messages, relayed = refs[:4], refs[4:8]
    seg_a, seg_b, dmat, tau_o, sinv, binv, ly_in = refs[8:15]
    brk, near, far = refs[15:]
    gy = position()[1]
    z_at, y_at = gy % 4, gy // 4
    for k in range(4):
        near[jnp.bitwise_xor(z_at, PARTNERS[k])] = messages[k][0 : 2 * CX, :]
        at = jnp.bitwise_xor(y_at, PARTNERS[k])
        far[at] = relayed[k][0 : 2 * CX, :]
        for i in range(4):
            row = relayed[k][2 * CX + i : 2 * CX + i + 1, :]
            brk[pl.ds(4 * at + jnp.bitwise_xor(z_at, PARTNERS[i]), 1), :] = row
    cuts = pltpu.roll(brk[...], (NZ - CY * gy) % NZ, 1)
    before = jnp.where(y_at > 0, far[jnp.maximum(y_at - 1, 0)], 0.0)
    before = jnp.where(z_at > 0, near[jnp.maximum(z_at - 1, 0)], before)
    for c in range(2):
        ly_in[c] = before[c * CX : (c + 1) * CX]
    for c in range(2):
        ly = ly_in[c]
        for j in range(CY):
            d = diag[c, j] + jnp.where(rows() == 0, lx_in[c, j : j + 1, :], 0.0)
            dmat[3 * c, j] = d + ly if j == 0 else d
        for j in range(CY + 1):
            keep = 1.0 - cuts[:, j : j + 1]
            tau_o[c, j] = (ty[c, j - 1] if j else ly) * keep
    for j in range(CY):
        dmat[1, j] = cross[0, j]
        dmat[2, j] = cross[1, j]

    def tau(j):
        return pair_at(tau_o, j)

    def outer(t, p):
        return tuple(x * y for x, y in zip(p, (t[0] * t[0], t[0] * t[1], t[1] * t[0], t[1] * t[1])))

    s = inv2(block_at(dmat, 0))
    e = inv2(block_at(dmat, CY - 1))
    zero = jnp.zeros(PLANE, F32)
    yf = (tau(0)[0], zero, zero, tau(0)[1])
    zl = (tau(CY)[0], zero, zero, tau(CY)[1])
    y = pair_at(rhs, 0)
    z = pair_at(rhs, CY - 1)
    for i in range(4):
        sinv[i, 0] = s[i]
        binv[i, CY - 1] = e[i]
    for j in range(1, CY):
        k = CY - 1 - j
        t, u = tau(j), tau(k + 1)
        yf = rows_by(t, mm(s, yf))
        zl = rows_by(u, mm(e, zl))
        yv, zv = mv(s, y), mv(e, z)
        y = tuple(rhs[c, j] + t[c] * yv[c] for c in range(2))
        z = tuple(rhs[c, k] + u[c] * zv[c] for c in range(2))
        s = inv2(tuple(d - x for d, x in zip(block_at(dmat, j), outer(t, s))))
        e = inv2(tuple(d - x for d, x in zip(block_at(dmat, k), outer(u, e))))
        for i in range(4):
            sinv[i, j] = s[i]
            binv[i, k] = e[i]
    whole = (columns_by(e, tau(0)), mm(e, zl), mm(s, yf), columns_by(s, tau(CY)), mv(e, z), mv(s, y))
    for half, ref in enumerate((seg_a, seg_b)):
        store_segment(ref, [[x[8 * half : 8 * half + 8] for x in part] for part in whole], True)


def gather_matrices(at_place, halves, mat_s):
    for k in range(4):
        at = jnp.bitwise_xor(at_place, PARTNERS[k])
        for half, refs in enumerate(halves):
            mat_s[at, :, 8 * half : 8 * half + 8, :] = refs[k][0:16]


def gather_vectors(at_place, vecs, vec_s):
    for k in range(4):
        vec_s[jnp.bitwise_xor(at_place, PARTNERS[k])] = vecs[k][...]


def gather_both(at_place, halves, mat_s, vec_s):
    gather_matrices(at_place, halves, mat_s)
    for k in range(4):
        at = jnp.bitwise_xor(at_place, PARTNERS[k])
        for half, refs in enumerate(halves):
            vec_s[at, :, 8 * half : 8 * half + 8, :] = refs[k][16:20]


def total_half_kernel(own, m1, m2, m3, out, segs_s):
    for k, ref in enumerate((own, m1, m2, m3)):
        segs_s[jnp.bitwise_xor(position()[1] % 4, PARTNERS[k])] = ref[...]
    segs = [load_segment(segs_s.at[m], segs_s.at[m], 16) for m in range(4)]
    store_segment(out, join(join(segs[0], segs[1]), join(segs[2], segs[3])), True)


def total_again_kernel(*refs):
    halves, vecs = (refs[0:4], refs[4:8]), refs[8:12]
    out, mat_s, vec_s = refs[12:]
    gather_matrices(position()[1] % 4, halves, mat_s)
    gather_vectors(position()[1] % 4, vecs, vec_s)
    segs = [load_segment(mat_s.at[m], vec_s.at[m], 0) for m in range(4)]
    store_segment(out, join(join(segs[0], segs[1]), join(segs[2], segs[3])), False)


def split3(x):
    hi = x.astype(BF16)
    rest = x - hi.astype(F32)
    mid = rest.astype(BF16)
    low = (rest - mid.astype(F32)).astype(BF16)
    return hi, mid, low


def slot_tables(cells, wells):
    cell = cells[...]
    row = jnp.bitwise_and(lax.shift_right_logical(cell, 7), 7) * CX + lax.shift_right_logical(cell, 10)
    shape = (NZ, SLOTS_ALL)
    up = lax.broadcasted_iota(jnp.int32, shape, 0)
    at_row = up == row
    at_layer = up == jnp.bitwise_and(cell, NZ - 1)
    at_well = up == wells[...]
    return at_row, at_layer, at_well


def ones_of(mask):
    return jnp.where(mask, 1.0, 0.0).astype(F32).astype(BF16)


NT = (((1,), (1,)), ((), ()))


def row_times(rows_in, table, dims):
    parts = [part for x in rows_in for part in split3(x)]
    n = len(rows_in)
    pad = 16 - 3 * n
    width = rows_in[0].shape[1]
    stacked = jnp.concatenate([p.astype(F32) for p in parts] + [jnp.zeros((pad, width), F32)], axis=0).astype(BF16)
    out = lax.dot_general(stacked, table, dims, preferred_element_type=F32)
    return [out[3 * i : 3 * i + 1] + out[3 * i + 1 : 3 * i + 2] + out[3 * i + 2 : 3 * i + 3] for i in range(n)]


def make_inner_kernel(whole):
    def kernel(*refs):
        halves = (refs[0:4], refs[4:8])
        vecs, rest = (None, refs[8:]) if whole else (refs[8:12], refs[12:])
        if whole:
            sinv, tau_r, rhs, left, right, base, from_left, from_right, mat_s, vec_s = rest
        else:
            sinv, tau_r, rhs, left, right, base, mat_s, vec_s = rest
        z = position()[1] % 4
        if whole:
            gather_both(z, halves, mat_s, vec_s)
        else:
            gather_matrices(z, halves, mat_s)
            gather_vectors(z, vecs, vec_s)
        segs = [load_segment(mat_s.at[m], vec_s.at[m], 0) for m in range(4)]
        pair = join(segs[0], segs[1])
        store_segment(left, choose(z == 1, segs[0], choose(z == 2, pair, join(pair, segs[2]))), True)
        pair = join(segs[2], segs[3])
        store_segment(right, choose(z == 2, segs[3], choose(z == 1, pair, join(segs[1], pair))), True)

        def tau(j):
            return pair_at(tau_r, j)

        def sv(j):
            return block_at(sinv, j)

        y = sweep_forward(sv, tau, [pair_at(rhs, j) for j in range(CY)])
        u = None
        for j in range(CY - 1, -1, -1):
            v = y[j] if u is None else tuple(y[j][c] + tau(j + 1)[c] * u[c] for c in range(2))
            u = mv(sv(j), v)
            for c in range(2):
                base[c, j] = u[c]
        if not whole:
            return
        zero = jnp.zeros(PLANE, F32)
        units = [(tau(0)[0], zero, zero, tau(0)[1])]
        for j in range(1, CY):
            units.append(rows_by(tau(j), mm(sv(j - 1), units[-1])))
        ul = ur = None
        for j in range(CY - 1, -1, -1):
            if ul is None:
                ul = mm(sv(j), units[j])
                ur = columns_by(sv(j), tau(CY))
            else:
                ul = mm(sv(j), madd(units[j], rows_by(tau(j + 1), ul)))
                ur = mm(sv(j), rows_by(tau(j + 1), ur))
            for i in range(4):
                from_left[i, j] = ul[i]
                from_right[i, j] = ur[i]

    return kernel


def make_solve_kernel(whole):
    def kernel(*refs):
        own_m, outer = refs[0:2], (refs[2:6], refs[6:10])
        own_v, outer_v, rest = (None, None, refs[10:]) if whole else (refs[10], refs[11:15], refs[15:])
        left, right, base, from_left, from_right, cells, wells, weights = rest[:8]
        p_out, ends, msg_a, msg_b = rest[8:12]
        mat_o, vec_o, mat_i, vec_i, edge = rest[12:]
        gx, gy = position()
        z_at, y_at = gy % 4, gy // 4
        for half, ref in enumerate(own_m):
            mat_i[:, 8 * half : 8 * half + 8, :] = ref[0:16]
            if whole:
                vec_i[:, 8 * half : 8 * half + 8, :] = ref[16:20]
        if whole:
            gather_both(y_at, outer, mat_o, vec_o)
        else:
            vec_i[...] = own_v[...]
            gather_matrices(y_at, outer, mat_o)
            gather_vectors(y_at, outer_v, vec_o)
        zero = jnp.zeros(PLANE, F32)
        before = ((zero,) * 4, (zero,) * 2)
        after = ((zero,) * 4, (zero,) * 2)
        for m in range(3):
            seg = load_segment(mat_o.at[m], vec_o.at[m], 0)
            before = choose(m < y_at, join_before(before, seg), before)
            m = 3 - m
            seg = load_segment(mat_o.at[m], vec_o.at[m], 0)
            after = choose(m > y_at, join_after(seg, after), after)
        before = choose(z_at > 0, join_before(before, load_segment(left, left, 16)), before)
        after = choose(z_at < 3, join_after(load_segment(right, right, 16), after), after)
        own = load_segment(mat_i, vec_i, 0)
        ff, fl, lf, ll, gf, gl = own
        up_m, up_v = join_before(before, own)
        last = mv(inv2(one_minus(mm(up_m, after[0]))), madd(up_v, mv(up_m, after[1])))
        beyond = madd(after[1], mv(after[0], last))
        k = inv2(one_minus(mm(ff, before[0])))
        first = mv(k, madd(madd(gf, mv(ff, before[1])), mv(fl, beyond)))
        behind = madd(before[1], mv(before[0], first))
        for c in range(2):
            ends[c] = behind[c]
            ends[2 + c] = beyond[c]

        for j in range(CY):
            u = madd(pair_at(base, j), madd(mv(block_at(from_left, j), behind), mv(block_at(from_right, j), beyond)))
            for c in range(2):
                p_out[c, j] = u[c]
                edge[0, c * CY + j : c * CY + j + 1, :] = u[c][0:1, :]
                edge[1, c * CY + j : c * CY + j + 1, :] = u[c][CX - 1 : CX, :]
        at_row, at_layer, at_well = slot_tables(cells, wells)
        pressure = jnp.concatenate([p_out[0, j] for j in range(CY)], axis=0)
        table = ones_of(at_layer)
        picked = sum(jnp.dot(part, table, preferred_element_type=F32) for part in split3(pressure))
        values = jnp.sum(jnp.where(at_row, picked, 0.0), axis=0, keepdims=True)
        w = weights[...]
        sums, totals = row_times([w * values, w], ones_of(at_well), NT)
        tail = jnp.concatenate([sums, totals, jnp.zeros((6, W_ALL), F32)], axis=0)
        even = gx % 2 == 0
        low, high = edge[0], edge[1]
        msg_a[0:16, :] = jnp.where(even, high, low)
        msg_b[0:16, :] = jnp.where(even, low, high)
        msg_a[16:24, :] = tail
        msg_b[16:24, :] = tail

    return kernel


def apply_operator(got, cells, wells, weights):
    gx = position()[0]
    got_a, sent_b, got_c, got_b, got_d = got
    tail = sent_b[16:24, :] + got_b[16:24, :] + got_c[...] + got_d[...]
    rates = tail[0:1] / jnp.maximum(tail[1:2], 1.0)
    at_row, at_layer, at_well = slot_tables(cells, wells)
    slot_rate = row_times([rates], ones_of(at_well), (((1,), (0,)), ((), ())))[0]
    added = jnp.where(at_layer, weights[...] * slot_rate, 0.0)
    table = ones_of(at_row)
    well_add = sum(lax.dot_general(table, part, NT, preferred_element_type=F32) for part in split3(added))
    even = gx % 2 == 0
    halo_a, halo_b = got_a[0:16, :], got_b[0:16, :]
    from_after = jnp.where(gx < N_GX - 1, jnp.where(even, halo_a, halo_b), 0.0)
    from_before = jnp.where(gx > 0, jnp.where(even, halo_b, halo_a), 0.0)
    return well_add, from_after, from_before


def operator_plane(c, j, p, ends, dmat, tx, ty, tz, lx_in, ly_in, halo, well_add):
    from_after, from_before = halo
    here = p[c, j]
    up = p[c, j + 1] if j < CY - 1 else ends[2 + c]
    down = p[c, j - 1] if j > 0 else ends[c]
    t = tx[c, j]
    at = c * CY + j
    beside = t * from_row_after(here, from_after[at : at + 1])
    beside = beside + from_row_before(t * here, lx_in[c, j : j + 1, :] * from_before[at : at + 1])
    beside = beside + ty[c, j] * up + (ty[c, j - 1] if j else ly_in[c]) * down
    tzp = tz[c, j]
    beside = beside + tzp * pltpu.roll(here, NZ - 1, 1) + pltpu.roll(tzp * here, 1, 1)
    out = dmat[2 * c, j] * p[0, j] + dmat[2 * c + 1, j] * p[1, j] - beside
    if c == 0:
        out = out + well_add[j * CX : (j + 1) * CX]
    return out


def first_image_kernel(got_a, sent_b, got_c, got_b, got_d, p, ends, dmat, tau_r, sinv, binv, rhs, tx, ty, tz, lx_in, ly_in, cells, wells, weights, q_out, e_out, vec_out, dots):
    well_add, after, before = apply_operator((got_a, sent_b, got_c, got_b, got_d), cells, wells, weights)
    eq = jnp.zeros(PLANE, F32)
    qq = jnp.zeros(PLANE, F32)
    e = []
    for j in range(CY):
        pair = []
        for c in range(2):
            q = operator_plane(c, j, p, ends, dmat, tx, ty, tz, lx_in, ly_in, (after, before), well_add)
            rest = rhs[c, j] - q
            q_out[c, j] = q
            e_out[c, j] = rest
            eq = eq + rest * q
            qq = qq + q * q
            pair.append(rest)
        e.append(tuple(pair))
    dots[0] = eq
    dots[1] = qq

    def tau(j):
        return pair_at(tau_r, j)

    y = sweep_forward(lambda j: block_at(sinv, j), tau, e)[CY - 1]
    z = sweep_backward(lambda j: block_at(binv, j), tau, e)
    first = mv(block_at(binv, 0), z)
    last = mv(block_at(sinv, CY - 1), y)
    for c in range(2):
        vec_out[c] = first[c]
        vec_out[2 + c] = last[c]


def second_image_kernel(got_a, sent_b, got_c, got_b, got_d, p, ends, dmat, tx, ty, tz, lx_in, ly_in, cells, wells, weights, q_in, e_in, dots_in, s_out, dots):
    well_add, after, before = apply_operator((got_a, sent_b, got_c, got_b, got_d), cells, wells, weights)
    sq = jnp.zeros(PLANE, F32)
    ss = jnp.zeros(PLANE, F32)
    es = jnp.zeros(PLANE, F32)
    for j in range(CY):
        for c in range(2):
            s = operator_plane(c, j, p, ends, dmat, tx, ty, tz, lx_in, ly_in, (after, before), well_add)
            s_out[c, j] = s
            sq = sq + s * q_in[c, j]
            ss = ss + s * s
            es = es + s * e_in[c, j]
    sums = [jnp.sum(x, axis=0, keepdims=True) for x in (dots_in[0], dots_in[1], sq, ss, es)]
    lane = lax.broadcasted_iota(jnp.int32, (1, NZ), 1)
    row = jnp.zeros((1, NZ), F32)
    for i, x in enumerate(sums):
        row = jnp.where(lane == i, jnp.sum(x, axis=1, keepdims=True), row)
    dots[...] = row


def finish_kernel(got, p, w, q, e, s, x_out, r_out):
    total = jnp.sum(got[...], axis=0, keepdims=True)
    lane = lax.broadcasted_iota(jnp.int32, (1, NZ), 1)
    eq, qq, sq, ss, es = (
        jnp.broadcast_to(jnp.sum(jnp.where(lane == i, total, 0.0), axis=1, keepdims=True), (1, NZ)) for i in range(5)
    )
    rest = -eq / qq
    g = sq / qq
    k = (es - g * eq) / (ss - g * sq)
    on_p = (1.0 - rest) - k * g
    on_q = rest + k * g
    for c in range(2):
        for j in range(CY):
            at = pl.ds(j, CX, stride=CY)
            x_out.at[c][at, :] = on_p * p[c, j] + k * w[c, j]
            r_out.at[c][at, :] = e[c, j] + on_q * q[c, j] - k * s[c, j]


def call(kernel, name, outs, scratch, *args, specs=None, vmem=24 * 1024):
    outs = [o if isinstance(o, jax.ShapeDtypeStruct) else jax.ShapeDtypeStruct(o, F32) for o in outs]
    return pl.pallas_call(
        kernel,
        name=name,
        out_shape=tuple(outs),
        in_specs=specs or [VMEM] * len(args),
        out_specs=tuple(VMEM for _ in outs),
        scratch_shapes=[pltpu.VMEM(s, F32) if isinstance(s, tuple) else s for s in scratch],
        compiler_params=pltpu.CompilerParams(vmem_limit_bytes=vmem * 1024),
    )(*args)


def swapped(block, stride):
    others = [lax.ppermute(block, "gy", [(i, i ^ (k * stride)) for i in range(N_GY)]) for k in PARTNERS[1:]]
    return [block] + others


def exchange_rows(msg_a, msg_b):
    got_a = lax.ppermute(msg_a, "gx", [(i, i ^ 1) for i in range(N_GX)])
    below = lax.broadcasted_iota(jnp.int32, msg_b.shape, 0) >= 16
    tail = msg_b[16:] + got_a[16:]
    sent_b = msg_b + jnp.where(below, got_a, 0.0)
    got_d = lax.ppermute(tail, "gx", [(i, (i + 2 if i % 2 else i - 2) % N_GX) for i in range(N_GX)])
    got_b = lax.ppermute(sent_b, "gx", [(i, (i + 1 if i % 2 else i - 1) % N_GX) for i in range(N_GX)])
    got_c = lax.ppermute(tail, "gx", [(i, i ^ 4) for i in range(N_GX)])
    return got_a, sent_b, got_c, got_b, got_d


def sum_everywhere(x):
    x = x + lax.ppermute(x, "gx", [(i, i ^ 1) for i in range(N_GX)])
    others = [lax.ppermute(x, "gx", [(i, (i + 2 * k) % N_GX) for i in range(N_GX)]) for k in PARTNERS[1:]]
    x = x + others[0] + others[1] + others[2]
    x = jnp.broadcast_to(x, (N_GY, NZ))
    return lax.all_to_all(x, "gy", split_axis=0, concat_axis=0, tiled=True)


def body(right_side, accumulation, trans_x, trans_y, trans_z, perf_cell, perf_well, perf_weight, perf_count, breaks):

    def flat(a):
        return a.reshape(a.shape[0], CX * CY, NZ)

    field, block, part = (2, CY, CX, NZ), (4, CY, CX, NZ), (2, CY + 1, CX, NZ)
    half, vec, message = (20, 8, NZ), (4, CX, NZ), (24, NZ)
    order = [(4, 16, CX, NZ), (4, 4, CX, NZ)]
    two, four = (2, CX * CY, NZ), (4, CX * CY, NZ)
    sx, edge = call(
        edges_kernel, "edges", ((2, CY, NZ), (40, NZ)),
        [two, pltpu.VMEM((1, NZ), jnp.int32), pltpu.SemaphoreType.DMA((4,))],
        flat(trans_x), flat(trans_y), breaks, specs=[HBM] * 3, vmem=EDGES_VMEM,
    )
    rhs, tx, ty, tz, diag, cross = call(
        prepare_kernel, "prepare", (field,) * 6,
        [two, four, two, two, two, pltpu.SemaphoreType.DMA((5,))],
        flat(right_side), flat(accumulation), flat(trans_x), flat(trans_y), flat(trans_z),
        specs=[HBM] * 5, vmem=PREPARE_VMEM,
    )
    edges = swapped(edge, 1)
    lx = lax.ppermute(sx, "gx", [(i, i + 1) for i in range(N_GX - 1)])
    *edges, rhs, tx, ty, tz, diag, cross = lax.optimization_barrier((*edges, rhs, tx, ty, tz, diag, cross))
    relayed = swapped(relay(*edges), 4)
    slots = perf_cell.shape[3]
    live = jnp.arange(slots, dtype=jnp.int32)[None, :] < perf_count.reshape(N_GX, 1)
    weights = jnp.where(live, perf_weight.reshape(N_GX, slots), 0.0).reshape(1, SLOTS_ALL)
    owners = jnp.arange(N_GX, dtype=jnp.int32)[:, None] * 16
    wells = (perf_well.reshape(N_GX, slots) + owners).reshape(1, SLOTS_ALL)
    cells = perf_cell.reshape(1, SLOTS_ALL)
    perfs = (cells, wells, weights)

    own_a, own_b, dmat, tau, sinv, binv, ly = call(
        condense_kernel, "condense", (half, half, block, part, block, block, (2, CX, NZ)),
        [(N_GY, NZ), (4, 2 * CX, NZ), (4, 2 * CX, NZ)], diag, cross, ty, rhs, lx, *edges, *relayed,
    )
    inner, outer = [], []
    for own in (own_a, own_b):
        inner.append(swapped(own, 1))
    for near in inner:
        (group,) = call(total_half_kernel, "group_total", (half,), [(4,) + half], *near)
        outer.append(swapped(group, 4))
    inner = inner[0] + inner[1]
    outer = outer[0] + outer[1]
    solve_scratch = order + [(16, CX, NZ), (4, CX, NZ), (2, 16, NZ)]
    joined = (20, CX, NZ)
    left, right, base, from_left, from_right = call(
        make_inner_kernel(True), "inner_first", (joined, joined, field, block, block), order, *inner, sinv, tau, rhs,
    )
    owns = (own_a, own_b)
    p, ends, msg_a, msg_b = call(
        make_solve_kernel(True), "solve_first", (field, vec, message, message), solve_scratch,
        *owns, *outer, left, right, base, from_left, from_right, *perfs,
    )
    got = exchange_rows(msg_a, msg_b)
    q, e, own_v, dots = call(
        first_image_kernel, "first_image", (field, field, vec, (2, CX, NZ)), [],
        *got, p, ends, dmat, tau, sinv, binv, rhs, tx, ty, tz, lx, ly, *perfs,
    )
    inner_v = swapped(own_v, 1)
    (group_v,) = call(total_again_kernel, "group_total_again", (vec,), order, *inner, *inner_v)
    outer_v = swapped(group_v, 4)
    left, right, base = call(
        make_inner_kernel(False), "inner_second", (joined, joined, field), order, *inner, *inner_v, sinv, tau, e,
    )
    w, ends, msg_a, msg_b = call(
        make_solve_kernel(False), "solve_second", (field, vec, message, message), solve_scratch,
        *owns, *outer, own_v, *outer_v, left, right, base, from_left, from_right, *perfs,
    )
    got = exchange_rows(msg_a, msg_b)
    s, dots = call(
        second_image_kernel, "second_image", (field, (1, NZ)), [],
        *got, w, ends, dmat, tx, ty, tz, lx, ly, *perfs, q, e, dots,
    )
    dots = sum_everywhere(dots)
    x, r = call(finish_kernel, "finish", (two, two), [], dots, p, w, q, e, s)
    shape = (2, CX, CY, NZ)
    return x.reshape(shape), r.reshape(shape)


def solution(mesh):
    tile = P(None, "gx", "gy", None)
    slots = P("gx", "gy", None, None)
    return jax.shard_map(
        body,
        mesh=mesh,
        in_specs=(tile,) * 5 + (slots,) * 3 + (P("gx", "gy", None), P(("gx", "gy"), None)),
        out_specs=(tile, tile),
        check_vma=False,
    )
```

```python
import jax
import jax.numpy as jnp
from jax import lax
from jax.experimental import pallas as pl
from jax.experimental.pallas import tpu as pltpu
from jax.sharding import PartitionSpec as P

F32 = jnp.float32
BF16 = jnp.bfloat16
VMEM = pl.BlockSpec(memory_space=pltpu.VMEM)
HBM = pl.BlockSpec(memory_space=pltpu.HBM)
SMEM = pl.BlockSpec(memory_space=pltpu.SMEM)
CX, CY, NZ = 16, 8, 128
PLANE = (CX, NZ)
N_GX, N_GY = 8, 16
W_ALL = 128
PARTNERS = (0, 1, 2, 3)
PREPARE_VMEM = 54400
EDGES_VMEM = 55296
SLOTS_ALL = 256


def mm(p, q):
    return (
        p[0] * q[0] + p[1] * q[2],
        p[0] * q[1] + p[1] * q[3],
        p[2] * q[0] + p[3] * q[2],
        p[2] * q[1] + p[3] * q[3],
    )


def mv(p, v):
    return (p[0] * v[0] + p[1] * v[1], p[2] * v[0] + p[3] * v[1])


def madd(p, q):
    return tuple(a + b for a, b in zip(p, q))


def inv2(p):
    t = 1.0 / (p[0] * p[3] - p[1] * p[2])
    return (p[3] * t, -p[1] * t, -p[2] * t, p[0] * t)


def one_minus(p):
    return (1.0 - p[0], -p[1], -p[2], 1.0 - p[3])


def rows_by(t, p):
    return (t[0] * p[0], t[0] * p[1], t[1] * p[2], t[1] * p[3])


def columns_by(p, t):
    return (p[0] * t[0], p[1] * t[1], p[2] * t[0], p[3] * t[1])


def join(a, b):
    ff1, fl1, lf1, ll1, gf1, gl1 = a
    ff2, fl2, lf2, ll2, gf2, gl2 = b
    k = inv2(one_minus(mm(ll1, ff2)))
    last = mv(k, madd(gl1, mv(ll1, gf2)))
    last_b = mm(k, lf1)
    last_a = mm(k, mm(ll1, fl2))
    first = madd(gf2, mv(ff2, last))
    first_b = mm(ff2, last_b)
    first_a = madd(fl2, mm(ff2, last_a))
    return (
        madd(ff1, mm(fl1, first_b)),
        mm(fl1, first_a),
        mm(lf2, last_b),
        madd(ll2, mm(lf2, last_a)),
        madd(gf1, mv(fl1, first)),
        madd(gl2, mv(lf2, last)),
    )


def join_before(before, s):
    gm, g = before
    ff, fl, lf, ll, gf, gl = s
    k = inv2(one_minus(mm(ff, gm)))
    a = mv(k, madd(gf, mv(ff, g)))
    am = mm(k, fl)
    return (madd(ll, mm(lf, mm(gm, am))), madd(gl, mv(lf, madd(g, mv(gm, a)))))


def join_after(s, after):
    gm, g = after
    ff, fl, lf, ll, gf, gl = s
    k = inv2(one_minus(mm(ll, gm)))
    a = mv(k, madd(gl, mv(ll, g)))
    am = mm(k, lf)
    return (madd(ff, mm(fl, mm(gm, am))), madd(gf, mv(fl, madd(g, mv(gm, a)))))


def position():
    return lax.axis_index("gx"), lax.axis_index("gy")


def choose(flag, new, old):
    return tuple(tuple(jnp.where(flag, n, o) for n, o in zip(ns, os)) for ns, os in zip(new, old))


def load_segment(mat, vec, offset):
    m = [mat[i] for i in range(16)]
    v = [vec[offset + i] for i in range(4)]
    return (tuple(m[0:4]), tuple(m[4:8]), tuple(m[8:12]), tuple(m[12:16]), (v[0], v[1]), (v[2], v[3]))


def store_segment(ref, seg, whole):
    flat = [x for part in seg for x in part]
    if not whole:
        flat = flat[16:]
    for i, x in enumerate(flat):
        ref[i] = x


def lanes():
    return lax.broadcasted_iota(jnp.int32, PLANE, 1)


def rows():
    return lax.broadcasted_iota(jnp.int32, PLANE, 0)


def from_row_before(plane, edge):
    return jnp.where(rows() == 0, edge, pltpu.roll(plane, 1, 0))


def from_row_after(plane, edge):
    return jnp.where(rows() == CX - 1, edge, pltpu.roll(plane, CX - 1, 0))


def sweep_forward(sinv, tau, rhs):
    y = [rhs[0]]
    for j in range(1, CY):
        t = mv(sinv(j - 1), y[-1])
        y.append((rhs[j][0] + tau(j)[0] * t[0], rhs[j][1] + tau(j)[1] * t[1]))
    return y


def sweep_backward(binv, tau, rhs):
    z = rhs[CY - 1]
    for j in range(CY - 2, -1, -1):
        t = mv(binv(j + 1), z)
        z = (rhs[j][0] + tau(j + 1)[0] * t[0], rhs[j][1] + tau(j + 1)[1] * t[1])
    return z


def block_at(ref, j):
    return tuple(ref[i, j] for i in range(4))


def pair_at(ref, j):
    return (ref[0, j], ref[1, j])


def plane(ref, c, j):
    return ref.at[c][pl.ds(j, CX, stride=CY), :]


def edges_kernel(tx_h, ty_h, brk_h, sx, edge, ty, brk, sems):
    copies = [pltpu.make_async_copy(h, v, sems.at[i]) for i, (h, v) in enumerate(((ty_h, ty), (brk_h, brk)))]
    copies += [
        pltpu.make_async_copy(tx_h.at[c, (CX - 1) * CY : CX * CY, :], sx.at[c], sems.at[2 + c]) for c in range(2)
    ]
    for copy in copies:
        copy.start()
    for copy in copies:
        copy.wait()
    edge[2 * CX :, :] = jnp.broadcast_to(brk[...].astype(F32), (8, NZ))
    for c in range(2):
        edge[c * CX : (c + 1) * CX, :] = plane(ty, c, CY - 1)


def relay(*messages):
    z = position()[1] % 4
    row = lax.broadcasted_iota(jnp.int32, messages[0].shape, 0)
    out = jnp.zeros_like(messages[0])
    for k, ref in enumerate(messages):
        out = jnp.where(jnp.where(row < 2 * CX, z == 3 - PARTNERS[k], row == 2 * CX + k), ref, out)
    return out


def prepare_kernel(b_h, acc_h, tx_h, ty_h, tz_h, rhs, tx_o, ty_o, tz_o, diag, cross, b, acc, tx_v, ty_v, tz_v, sems):
    gx, gy = position()
    pairs = ((tx_h, tx_v), (ty_h, ty_v), (tz_h, tz_v), (acc_h, acc), (b_h, b))
    copies = [pltpu.make_async_copy(h, v, sems.at[i]) for i, (h, v) in enumerate(pairs)]
    for copy in copies:
        copy.start()
    last_x = jnp.logical_and(rows() == CX - 1, gx == N_GX - 1)
    last_z = lanes() == NZ - 1
    for copy in copies:
        copy.wait()
    for c in range(2):
        ly = 0.0
        for j in range(CY):
            tx = jnp.where(last_x, 0.0, plane(tx_v, c, j))
            tz = jnp.where(last_z, 0.0, plane(tz_v, c, j))
            ty = plane(ty_v, c, j)
            if j == CY - 1:
                ty = jnp.where(gy == N_GY - 1, 0.0, ty)
            tx_o[c, j] = tx
            tz_o[c, j] = tz
            ty_o[c, j] = ty
            faces = tx + from_row_before(tx, 0.0) + ty + ly + tz + pltpu.roll(tz, 1, 1)
            diag[c, j] = plane(acc, 3 * c, j) + faces
            cross[c, j] = plane(acc, 2 - c, j)
            rhs[c, j] = plane(b, c, j)
            ly = ty


def condense_kernel(diag, cross, ty, rhs, lx_in, *refs):
    messages, relayed = refs[:4], refs[4:8]
    seg_a, seg_b, dmat, tau_o, sinv, binv, ly_in = refs[8:15]
    brk, near, far = refs[15:]
    gy = position()[1]
    z_at, y_at = gy % 4, gy // 4
    for k in range(4):
        near[jnp.bitwise_xor(z_at, PARTNERS[k])] = messages[k][0 : 2 * CX, :]
        at = jnp.bitwise_xor(y_at, PARTNERS[k])
        far[at] = relayed[k][0 : 2 * CX, :]
        for i in range(4):
            row = relayed[k][2 * CX + i : 2 * CX + i + 1, :]
            brk[pl.ds(4 * at + jnp.bitwise_xor(z_at, PARTNERS[i]), 1), :] = row
    cuts = pltpu.roll(brk[...], (NZ - CY * gy) % NZ, 1)
    before = jnp.where(y_at > 0, far[jnp.maximum(y_at - 1, 0)], 0.0)
    before = jnp.where(z_at > 0, near[jnp.maximum(z_at - 1, 0)], before)
    for c in range(2):
        ly_in[c] = before[c * CX : (c + 1) * CX]
    for c in range(2):
        ly = ly_in[c]
        for j in range(CY):
            d = diag[c, j] + jnp.where(rows() == 0, lx_in[c, j : j + 1, :], 0.0)
            dmat[3 * c, j] = d + ly if j == 0 else d
        for j in range(CY + 1):
            keep = 1.0 - cuts[:, j : j + 1]
            tau_o[c, j] = (ty[c, j - 1] if j else ly) * keep
    for j in range(CY):
        dmat[1, j] = cross[0, j]
        dmat[2, j] = cross[1, j]

    def tau(j):
        return pair_at(tau_o, j)

    def outer(t, p):
        return tuple(x * y for x, y in zip(p, (t[0] * t[0], t[0] * t[1], t[1] * t[0], t[1] * t[1])))

    s = inv2(block_at(dmat, 0))
    e = inv2(block_at(dmat, CY - 1))
    zero = jnp.zeros(PLANE, F32)
    yf = (tau(0)[0], zero, zero, tau(0)[1])
    zl = (tau(CY)[0], zero, zero, tau(CY)[1])
    y = pair_at(rhs, 0)
    z = pair_at(rhs, CY - 1)
    for i in range(4):
        sinv[i, 0] = s[i]
        binv[i, CY - 1] = e[i]
    for j in range(1, CY):
        k = CY - 1 - j
        t, u = tau(j), tau(k + 1)
        yf = rows_by(t, mm(s, yf))
        zl = rows_by(u, mm(e, zl))
        yv, zv = mv(s, y), mv(e, z)
        y = tuple(rhs[c, j] + t[c] * yv[c] for c in range(2))
        z = tuple(rhs[c, k] + u[c] * zv[c] for c in range(2))
        s = inv2(tuple(d - x for d, x in zip(block_at(dmat, j), outer(t, s))))
        e = inv2(tuple(d - x for d, x in zip(block_at(dmat, k), outer(u, e))))
        for i in range(4):
            sinv[i, j] = s[i]
            binv[i, k] = e[i]
    whole = (columns_by(e, tau(0)), mm(e, zl), mm(s, yf), columns_by(s, tau(CY)), mv(e, z), mv(s, y))
    for half, ref in enumerate((seg_a, seg_b)):
        store_segment(ref, [[x[8 * half : 8 * half + 8] for x in part] for part in whole], True)


def gather_matrices(at_place, halves, mat_s):
    for k in range(4):
        at = jnp.bitwise_xor(at_place, PARTNERS[k])
        for half, refs in enumerate(halves):
            mat_s[at, :, 8 * half : 8 * half + 8, :] = refs[k][0:16]


def gather_vectors(at_place, vecs, vec_s):
    for k in range(4):
        vec_s[jnp.bitwise_xor(at_place, PARTNERS[k])] = vecs[k][...]


def gather_both(at_place, halves, mat_s, vec_s):
    gather_matrices(at_place, halves, mat_s)
    for k in range(4):
        at = jnp.bitwise_xor(at_place, PARTNERS[k])
        for half, refs in enumerate(halves):
            vec_s[at, :, 8 * half : 8 * half + 8, :] = refs[k][16:20]


def total_half_kernel(own, m1, m2, m3, out, segs_s):
    for k, ref in enumerate((own, m1, m2, m3)):
        segs_s[jnp.bitwise_xor(position()[1] % 4, PARTNERS[k])] = ref[...]
    segs = [load_segment(segs_s.at[m], segs_s.at[m], 16) for m in range(4)]
    store_segment(out, join(join(segs[0], segs[1]), join(segs[2], segs[3])), True)


def total_again_kernel(*refs):
    halves, vecs = (refs[0:4], refs[4:8]), refs[8:12]
    out, mat_s, vec_s = refs[12:]
    gather_matrices(position()[1] % 4, halves, mat_s)
    gather_vectors(position()[1] % 4, vecs, vec_s)
    segs = [load_segment(mat_s.at[m], vec_s.at[m], 0) for m in range(4)]
    store_segment(out, join(join(segs[0], segs[1]), join(segs[2], segs[3])), False)


def split3(x):
    hi = x.astype(BF16)
    rest = x - hi.astype(F32)
    mid = rest.astype(BF16)
    low = (rest - mid.astype(F32)).astype(BF16)
    return hi, mid, low


def slot_tables(cells, wells):
    cell = cells[...]
    row = jnp.bitwise_and(lax.shift_right_logical(cell, 7), 7) * CX + lax.shift_right_logical(cell, 10)
    shape = (NZ, SLOTS_ALL)
    up = lax.broadcasted_iota(jnp.int32, shape, 0)
    at_row = up == row
    at_layer = up == jnp.bitwise_and(cell, NZ - 1)
    at_well = up == wells[...]
    return at_row, at_layer, at_well


def ones_of(mask):
    return jnp.where(mask, 1.0, 0.0).astype(F32).astype(BF16)


NT = (((1,), (1,)), ((), ()))


def row_times(rows_in, table, dims):
    parts = [part for x in rows_in for part in split3(x)]
    n = len(rows_in)
    pad = 16 - 3 * n
    width = rows_in[0].shape[1]
    stacked = jnp.concatenate([p.astype(F32) for p in parts] + [jnp.zeros((pad, width), F32)], axis=0).astype(BF16)
    out = lax.dot_general(stacked, table, dims, preferred_element_type=F32)
    return [out[3 * i : 3 * i + 1] + out[3 * i + 1 : 3 * i + 2] + out[3 * i + 2 : 3 * i + 3] for i in range(n)]


def make_inner_kernel(whole):
    def kernel(*refs):
        halves = (refs[0:4], refs[4:8])
        vecs, rest = (None, refs[8:]) if whole else (refs[8:12], refs[12:])
        if whole:
            sinv, tau_r, rhs, left, right, base, from_left, from_right, mat_s, vec_s = rest
        else:
            sinv, tau_r, rhs, left, right, base, mat_s, vec_s = rest
        z = position()[1] % 4
        if whole:
            gather_both(z, halves, mat_s, vec_s)
        else:
            gather_matrices(z, halves, mat_s)
            gather_vectors(z, vecs, vec_s)
        segs = [load_segment(mat_s.at[m], vec_s.at[m], 0) for m in range(4)]
        pair = join(segs[0], segs[1])
        store_segment(left, choose(z == 1, segs[0], choose(z == 2, pair, join(pair, segs[2]))), True)
        pair = join(segs[2], segs[3])
        store_segment(right, choose(z == 2, segs[3], choose(z == 1, pair, join(segs[1], pair))), True)

        def tau(j):
            return pair_at(tau_r, j)

        def sv(j):
            return block_at(sinv, j)

        y = sweep_forward(sv, tau, [pair_at(rhs, j) for j in range(CY)])
        u = None
        for j in range(CY - 1, -1, -1):
            v = y[j] if u is None else tuple(y[j][c] + tau(j + 1)[c] * u[c] for c in range(2))
            u = mv(sv(j), v)
            for c in range(2):
                base[c, j] = u[c]
        if not whole:
            return
        zero = jnp.zeros(PLANE, F32)
        units = [(tau(0)[0], zero, zero, tau(0)[1])]
        for j in range(1, CY):
            units.append(rows_by(tau(j), mm(sv(j - 1), units[-1])))
        ul = ur = None
        for j in range(CY - 1, -1, -1):
            if ul is None:
                ul = mm(sv(j), units[j])
                ur = columns_by(sv(j), tau(CY))
            else:
                ul = mm(sv(j), madd(units[j], rows_by(tau(j + 1), ul)))
                ur = mm(sv(j), rows_by(tau(j + 1), ur))
            for i in range(4):
                from_left[i, j] = ul[i]
                from_right[i, j] = ur[i]

    return kernel


def make_solve_kernel(whole):
    def kernel(*refs):
        own_m, outer = refs[0:2], (refs[2:6], refs[6:10])
        own_v, outer_v, rest = (None, None, refs[10:]) if whole else (refs[10], refs[11:15], refs[15:])
        left, right, base, from_left, from_right, cells, wells, weights = rest[:8]
        p_out, ends, msg_a, msg_b = rest[8:12]
        mat_o, vec_o, mat_i, vec_i, edge = rest[12:]
        gx, gy = position()
        z_at, y_at = gy % 4, gy // 4
        for half, ref in enumerate(own_m):
            mat_i[:, 8 * half : 8 * half + 8, :] = ref[0:16]
            if whole:
                vec_i[:, 8 * half : 8 * half + 8, :] = ref[16:20]
        if whole:
            gather_both(y_at, outer, mat_o, vec_o)
        else:
            vec_i[...] = own_v[...]
            gather_matrices(y_at, outer, mat_o)
            gather_vectors(y_at, outer_v, vec_o)
        zero = jnp.zeros(PLANE, F32)
        before = ((zero,) * 4, (zero,) * 2)
        after = ((zero,) * 4, (zero,) * 2)
        for m in range(3):
            seg = load_segment(mat_o.at[m], vec_o.at[m], 0)
            before = choose(m < y_at, join_before(before, seg), before)
            m = 3 - m
            seg = load_segment(mat_o.at[m], vec_o.at[m], 0)
            after = choose(m > y_at, join_after(seg, after), after)
        before = choose(z_at > 0, join_before(before, load_segment(left, left, 16)), before)
        after = choose(z_at < 3, join_after(load_segment(right, right, 16), after), after)
        own = load_segment(mat_i, vec_i, 0)
        ff, fl, lf, ll, gf, gl = own
        up_m, up_v = join_before(before, own)
        last = mv(inv2(one_minus(mm(up_m, after[0]))), madd(up_v, mv(up_m, after[1])))
        beyond = madd(after[1], mv(after[0], last))
        k = inv2(one_minus(mm(ff, before[0])))
        first = mv(k, madd(madd(gf, mv(ff, before[1])), mv(fl, beyond)))
        behind = madd(before[1], mv(before[0], first))
        for c in range(2):
            ends[c] = behind[c]
            ends[2 + c] = beyond[c]

        for j in range(CY):
            u = madd(pair_at(base, j), madd(mv(block_at(from_left, j), behind), mv(block_at(from_right, j), beyond)))
            for c in range(2):
                p_out[c, j] = u[c]
                edge[0, c * CY + j : c * CY + j + 1, :] = u[c][0:1, :]
                edge[1, c * CY + j : c * CY + j + 1, :] = u[c][CX - 1 : CX, :]
        at_row, at_layer, at_well = slot_tables(cells, wells)
        pressure = jnp.concatenate([p_out[0, j] for j in range(CY)], axis=0)
        table = ones_of(at_layer)
        picked = sum(jnp.dot(part, table, preferred_element_type=F32) for part in split3(pressure))
        values = jnp.sum(jnp.where(at_row, picked, 0.0), axis=0, keepdims=True)
        w = weights[...]
        sums, totals = row_times([w * values, w], ones_of(at_well), NT)
        tail = jnp.concatenate([sums, totals, jnp.zeros((6, W_ALL), F32)], axis=0)
        even = gx % 2 == 0
        low, high = edge[0], edge[1]
        msg_a[0:16, :] = jnp.where(even, high, low)
        msg_b[0:16, :] = jnp.where(even, low, high)
        msg_a[16:24, :] = tail
        msg_b[16:24, :] = tail

    return kernel


def apply_operator(got, cells, wells, weights):
    gx = position()[0]
    got_a, sent_b, got_c, got_b, got_d = got
    tail = sent_b[16:24, :] + got_b[16:24, :] + got_c[...] + got_d[...]
    rates = tail[0:1] / jnp.maximum(tail[1:2], 1.0)
    at_row, at_layer, at_well = slot_tables(cells, wells)
    slot_rate = row_times([rates], ones_of(at_well), (((1,), (0,)), ((), ())))[0]
    added = jnp.where(at_layer, weights[...] * slot_rate, 0.0)
    table = ones_of(at_row)
    well_add = sum(lax.dot_general(table, part, NT, preferred_element_type=F32) for part in split3(added))
    even = gx % 2 == 0
    halo_a, halo_b = got_a[0:16, :], got_b[0:16, :]
    from_after = jnp.where(gx < N_GX - 1, jnp.where(even, halo_a, halo_b), 0.0)
    from_before = jnp.where(gx > 0, jnp.where(even, halo_b, halo_a), 0.0)
    return well_add, from_after, from_before


def operator_plane(c, j, p, ends, dmat, tx, ty, tz, lx_in, ly_in, halo, well_add):
    from_after, from_before = halo
    here = p[c, j]
    up = p[c, j + 1] if j < CY - 1 else ends[2 + c]
    down = p[c, j - 1] if j > 0 else ends[c]
    t = tx[c, j]
    at = c * CY + j
    beside = t * from_row_after(here, from_after[at : at + 1])
    beside = beside + from_row_before(t * here, lx_in[c, j : j + 1, :] * from_before[at : at + 1])
    beside = beside + ty[c, j] * up + (ty[c, j - 1] if j else ly_in[c]) * down
    tzp = tz[c, j]
    beside = beside + tzp * pltpu.roll(here, NZ - 1, 1) + pltpu.roll(tzp * here, 1, 1)
    out = dmat[2 * c, j] * p[0, j] + dmat[2 * c + 1, j] * p[1, j] - beside
    if c == 0:
        out = out + well_add[j * CX : (j + 1) * CX]
    return out


def first_image_kernel(got_a, sent_b, got_c, got_b, got_d, p, ends, dmat, tau_r, sinv, binv, rhs, tx, ty, tz, lx_in, ly_in, cells, wells, weights, q_out, e_out, vec_out, dots):
    well_add, after, before = apply_operator((got_a, sent_b, got_c, got_b, got_d), cells, wells, weights)
    eq = jnp.zeros(PLANE, F32)
    qq = jnp.zeros(PLANE, F32)
    e = []
    for j in range(CY):
        pair = []
        for c in range(2):
            q = operator_plane(c, j, p, ends, dmat, tx, ty, tz, lx_in, ly_in, (after, before), well_add)
            rest = rhs[c, j] - q
            q_out[c, j] = q
            e_out[c, j] = rest
            eq = eq + rest * q
            qq = qq + q * q
            pair.append(rest)
        e.append(tuple(pair))
    dots[0] = eq
    dots[1] = qq

    def tau(j):
        return pair_at(tau_r, j)

    y = sweep_forward(lambda j: block_at(sinv, j), tau, e)[CY - 1]
    z = sweep_backward(lambda j: block_at(binv, j), tau, e)
    first = mv(block_at(binv, 0), z)
    last = mv(block_at(sinv, CY - 1), y)
    for c in range(2):
        vec_out[c] = first[c]
        vec_out[2 + c] = last[c]


def second_image_kernel(got_a, sent_b, got_c, got_b, got_d, p, ends, dmat, tx, ty, tz, lx_in, ly_in, cells, wells, weights, q_in, e_in, dots_in, s_out, dots):
    well_add, after, before = apply_operator((got_a, sent_b, got_c, got_b, got_d), cells, wells, weights)
    sq = jnp.zeros(PLANE, F32)
    ss = jnp.zeros(PLANE, F32)
    es = jnp.zeros(PLANE, F32)
    for j in range(CY):
        for c in range(2):
            s = operator_plane(c, j, p, ends, dmat, tx, ty, tz, lx_in, ly_in, (after, before), well_add)
            s_out[c, j] = s
            sq = sq + s * q_in[c, j]
            ss = ss + s * s
            es = es + s * e_in[c, j]
    sums = [jnp.sum(x, axis=0, keepdims=True) for x in (dots_in[0], dots_in[1], sq, ss, es)]
    lane = lax.broadcasted_iota(jnp.int32, (1, NZ), 1)
    row = jnp.zeros((1, NZ), F32)
    for i, x in enumerate(sums):
        row = jnp.where(lane == i, jnp.sum(x, axis=1, keepdims=True), row)
    dots[...] = row


def finish_kernel(got, p, w, q, e, s, x_out, r_out):
    total = jnp.sum(got[...], axis=0, keepdims=True)
    lane = lax.broadcasted_iota(jnp.int32, (1, NZ), 1)
    eq, qq, sq, ss, es = (
        jnp.broadcast_to(jnp.sum(jnp.where(lane == i, total, 0.0), axis=1, keepdims=True), (1, NZ)) for i in range(5)
    )
    rest = -eq / qq
    g = sq / qq
    k = (es - g * eq) / (ss - g * sq)
    on_p = (1.0 - rest) - k * g
    on_q = rest + k * g
    for c in range(2):
        for j in range(CY):
            at = pl.ds(j, CX, stride=CY)
            x_out.at[c][at, :] = on_p * p[c, j] + k * w[c, j]
            r_out.at[c][at, :] = e[c, j] + on_q * q[c, j] - k * s[c, j]


def call(kernel, name, outs, scratch, *args, specs=None, vmem=24 * 1024):
    outs = [o if isinstance(o, jax.ShapeDtypeStruct) else jax.ShapeDtypeStruct(o, F32) for o in outs]
    return pl.pallas_call(
        kernel,
        name=name,
        out_shape=tuple(outs),
        in_specs=specs or [VMEM] * len(args),
        out_specs=tuple(VMEM for _ in outs),
        scratch_shapes=[pltpu.VMEM(s, F32) if isinstance(s, tuple) else s for s in scratch],
        compiler_params=pltpu.CompilerParams(vmem_limit_bytes=vmem * 1024),
    )(*args)


def swapped(block, stride):
    others = [lax.ppermute(block, "gy", [(i, i ^ (k * stride)) for i in range(N_GY)]) for k in PARTNERS[1:]]
    return [block] + others


def exchange_rows(msg_a, msg_b):
    got_a = lax.ppermute(msg_a, "gx", [(i, i ^ 1) for i in range(N_GX)])
    below = lax.broadcasted_iota(jnp.int32, msg_b.shape, 0) >= 16
    tail = msg_b[16:] + got_a[16:]
    sent_b = msg_b + jnp.where(below, got_a, 0.0)
    got_d = lax.ppermute(tail, "gx", [(i, (i + 2 if i % 2 else i - 2) % N_GX) for i in range(N_GX)])
    got_b = lax.ppermute(sent_b, "gx", [(i, (i + 1 if i % 2 else i - 1) % N_GX) for i in range(N_GX)])
    got_c = lax.ppermute(tail, "gx", [(i, i ^ 4) for i in range(N_GX)])
    return got_a, sent_b, got_c, got_b, got_d


def sum_everywhere(x):
    x = x + lax.ppermute(x, "gx", [(i, i ^ 1) for i in range(N_GX)])
    others = [lax.ppermute(x, "gx", [(i, (i + 2 * k) % N_GX) for i in range(N_GX)]) for k in PARTNERS[1:]]
    x = x + others[0] + others[1] + others[2]
    x = jnp.broadcast_to(x, (N_GY, NZ))
    return lax.all_to_all(x, "gy", split_axis=0, concat_axis=0, tiled=True)


def body(right_side, accumulation, trans_x, trans_y, trans_z, perf_cell, perf_well, perf_weight, perf_count, breaks):

    def flat(a):
        return a.reshape(a.shape[0], CX * CY, NZ)

    field, block, part = (2, CY, CX, NZ), (4, CY, CX, NZ), (2, CY + 1, CX, NZ)
    half, vec, message = (20, 8, NZ), (4, CX, NZ), (24, NZ)
    order = [(4, 16, CX, NZ), (4, 4, CX, NZ)]
    two, four = (2, CX * CY, NZ), (4, CX * CY, NZ)
    sx, edge = call(
        edges_kernel, "edges", ((2, CY, NZ), (40, NZ)),
        [two, pltpu.VMEM((1, NZ), jnp.int32), pltpu.SemaphoreType.DMA((4,))],
        flat(trans_x), flat(trans_y), breaks, specs=[HBM] * 3, vmem=EDGES_VMEM,
    )
    rhs, tx, ty, tz, diag, cross = call(
        prepare_kernel, "prepare", (field,) * 6,
        [two, four, two, two, two, pltpu.SemaphoreType.DMA((5,))],
        flat(right_side), flat(accumulation), flat(trans_x), flat(trans_y), flat(trans_z),
        specs=[HBM] * 5, vmem=PREPARE_VMEM,
    )
    edges = swapped(edge, 1)
    lx = lax.ppermute(sx, "gx", [(i, i + 1) for i in range(N_GX - 1)])
    *edges, lx = lax.optimization_barrier((*edges, lx))
    relayed = swapped(relay(*edges), 4)
    slots = perf_cell.shape[3]
    live = jnp.arange(slots, dtype=jnp.int32)[None, :] < perf_count.reshape(N_GX, 1)
    weights = jnp.where(live, perf_weight.reshape(N_GX, slots), 0.0).reshape(1, SLOTS_ALL)
    owners = jnp.arange(N_GX, dtype=jnp.int32)[:, None] * 16
    wells = (perf_well.reshape(N_GX, slots) + owners).reshape(1, SLOTS_ALL)
    cells = perf_cell.reshape(1, SLOTS_ALL)
    perfs = (cells, wells, weights)

    own_a, own_b, dmat, tau, sinv, binv, ly = call(
        condense_kernel, "condense", (half, half, block, part, block, block, (2, CX, NZ)),
        [(N_GY, NZ), (4, 2 * CX, NZ), (4, 2 * CX, NZ)], diag, cross, ty, rhs, lx, *edges, *relayed,
    )
    inner, outer = [], []
    for own in (own_a, own_b):
        inner.append(swapped(own, 1))
    for near in inner:
        (group,) = call(total_half_kernel, "group_total", (half,), [(4,) + half], *near)
        outer.append(swapped(group, 4))
    inner = inner[0] + inner[1]
    outer = outer[0] + outer[1]
    solve_scratch = order + [(16, CX, NZ), (4, CX, NZ), (2, 16, NZ)]
    joined = (20, CX, NZ)
    left, right, base, from_left, from_right = call(
        make_inner_kernel(True), "inner_first", (joined, joined, field, block, block), order, *inner, sinv, tau, rhs,
    )
    owns = (own_a, own_b)
    p, ends, msg_a, msg_b = call(
        make_solve_kernel(True), "solve_first", (field, vec, message, message), solve_scratch,
        *owns, *outer, left, right, base, from_left, from_right, *perfs,
    )
    got = exchange_rows(msg_a, msg_b)
    q, e, own_v, dots = call(
        first_image_kernel, "first_image", (field, field, vec, (2, CX, NZ)), [],
        *got, p, ends, dmat, tau, sinv, binv, rhs, tx, ty, tz, lx, ly, *perfs,
    )
    inner_v = swapped(own_v, 1)
    (group_v,) = call(total_again_kernel, "group_total_again", (vec,), order, *inner, *inner_v)
    outer_v = swapped(group_v, 4)
    left, right, base = call(
        make_inner_kernel(False), "inner_second", (joined, joined, field), order, *inner, *inner_v, sinv, tau, e,
    )
    w, ends, msg_a, msg_b = call(
        make_solve_kernel(False), "solve_second", (field, vec, message, message), solve_scratch,
        *owns, *outer, own_v, *outer_v, left, right, base, from_left, from_right, *perfs,
    )
    got = exchange_rows(msg_a, msg_b)
    s, dots = call(
        second_image_kernel, "second_image", (field, (1, NZ)), [],
        *got, w, ends, dmat, tx, ty, tz, lx, ly, *perfs, q, e, dots,
    )
    dots = sum_everywhere(dots)
    x, r = call(finish_kernel, "finish", (two, two), [], dots, p, w, q, e, s)
    shape = (2, CX, CY, NZ)
    return x.reshape(shape), r.reshape(shape)


def solution(mesh):
    tile = P(None, "gx", "gy", None)
    slots = P("gx", "gy", None, None)
    return jax.shard_map(
        body,
        mesh=mesh,
        in_specs=(tile,) * 5 + (slots,) * 3 + (P("gx", "gy", None), P(("gx", "gy"), None)),
        out_specs=(tile, tile),
        check_vma=False,
    )
```

```python
import jax
import jax.numpy as jnp
from jax import lax
from jax.experimental import pallas as pl
from jax.experimental.pallas import tpu as pltpu
from jax.sharding import PartitionSpec as P

F32 = jnp.float32
BF16 = jnp.bfloat16
VMEM = pl.BlockSpec(memory_space=pltpu.VMEM)
HBM = pl.BlockSpec(memory_space=pltpu.HBM)
SMEM = pl.BlockSpec(memory_space=pltpu.SMEM)
CX, CY, NZ = 16, 8, 128
PLANE = (CX, NZ)
N_GX, N_GY = 8, 16
W_ALL = 128
PARTNERS = (0, 3, 2, 1)
PREPARE_VMEM = 54400
EDGES_VMEM = 55296
SLOTS_ALL = 256


def mm(p, q):
    return (
        p[0] * q[0] + p[1] * q[2],
        p[0] * q[1] + p[1] * q[3],
        p[2] * q[0] + p[3] * q[2],
        p[2] * q[1] + p[3] * q[3],
    )


def mv(p, v):
    return (p[0] * v[0] + p[1] * v[1], p[2] * v[0] + p[3] * v[1])


def madd(p, q):
    return tuple(a + b for a, b in zip(p, q))


def inv2(p):
    t = 1.0 / (p[0] * p[3] - p[1] * p[2])
    return (p[3] * t, -p[1] * t, -p[2] * t, p[0] * t)


def one_minus(p):
    return (1.0 - p[0], -p[1], -p[2], 1.0 - p[3])


def rows_by(t, p):
    return (t[0] * p[0], t[0] * p[1], t[1] * p[2], t[1] * p[3])


def columns_by(p, t):
    return (p[0] * t[0], p[1] * t[1], p[2] * t[0], p[3] * t[1])


def join(a, b):
    ff1, fl1, lf1, ll1, gf1, gl1 = a
    ff2, fl2, lf2, ll2, gf2, gl2 = b
    k = inv2(one_minus(mm(ll1, ff2)))
    last = mv(k, madd(gl1, mv(ll1, gf2)))
    last_b = mm(k, lf1)
    last_a = mm(k, mm(ll1, fl2))
    first = madd(gf2, mv(ff2, last))
    first_b = mm(ff2, last_b)
    first_a = madd(fl2, mm(ff2, last_a))
    return (
        madd(ff1, mm(fl1, first_b)),
        mm(fl1, first_a),
        mm(lf2, last_b),
        madd(ll2, mm(lf2, last_a)),
        madd(gf1, mv(fl1, first)),
        madd(gl2, mv(lf2, last)),
    )


def join_before(before, s):
    gm, g = before
    ff, fl, lf, ll, gf, gl = s
    k = inv2(one_minus(mm(ff, gm)))
    a = mv(k, madd(gf, mv(ff, g)))
    am = mm(k, fl)
    return (madd(ll, mm(lf, mm(gm, am))), madd(gl, mv(lf, madd(g, mv(gm, a)))))


def join_after(s, after):
    gm, g = after
    ff, fl, lf, ll, gf, gl = s
    k = inv2(one_minus(mm(ll, gm)))
    a = mv(k, madd(gl, mv(ll, g)))
    am = mm(k, lf)
    return (madd(ff, mm(fl, mm(gm, am))), madd(gf, mv(fl, madd(g, mv(gm, a)))))


def position():
    return lax.axis_index("gx"), lax.axis_index("gy")


def choose(flag, new, old):
    return tuple(tuple(jnp.where(flag, n, o) for n, o in zip(ns, os)) for ns, os in zip(new, old))


def load_segment(mat, vec, offset):
    m = [mat[i] for i in range(16)]
    v = [vec[offset + i] for i in range(4)]
    return (tuple(m[0:4]), tuple(m[4:8]), tuple(m[8:12]), tuple(m[12:16]), (v[0], v[1]), (v[2], v[3]))


def store_segment(ref, seg, whole):
    flat = [x for part in seg for x in part]
    if not whole:
        flat = flat[16:]
    for i, x in enumerate(flat):
        ref[i] = x


def lanes():
    return lax.broadcasted_iota(jnp.int32, PLANE, 1)


def rows():
    return lax.broadcasted_iota(jnp.int32, PLANE, 0)


def from_row_before(plane, edge):
    return jnp.where(rows() == 0, edge, pltpu.roll(plane, 1, 0))


def from_row_after(plane, edge):
    return jnp.where(rows() == CX - 1, edge, pltpu.roll(plane, CX - 1, 0))


def sweep_forward(sinv, tau, rhs):
    y = [rhs[0]]
    for j in range(1, CY):
        t = mv(sinv(j - 1), y[-1])
        y.append((rhs[j][0] + tau(j)[0] * t[0], rhs[j][1] + tau(j)[1] * t[1]))
    return y


def sweep_backward(binv, tau, rhs):
    z = rhs[CY - 1]
    for j in range(CY - 2, -1, -1):
        t = mv(binv(j + 1), z)
        z = (rhs[j][0] + tau(j + 1)[0] * t[0], rhs[j][1] + tau(j + 1)[1] * t[1])
    return z


def block_at(ref, j):
    return tuple(ref[i, j] for i in range(4))


def pair_at(ref, j):
    return (ref[0, j], ref[1, j])


def plane(ref, c, j):
    return ref.at[c][pl.ds(j, CX, stride=CY), :]


def edges_kernel(tx_h, ty_h, brk_h, sx, edge, ty, brk, sems):
    copies = [pltpu.make_async_copy(h, v, sems.at[i]) for i, (h, v) in enumerate(((ty_h, ty), (brk_h, brk)))]
    copies += [
        pltpu.make_async_copy(tx_h.at[c, (CX - 1) * CY : CX * CY, :], sx.at[c], sems.at[2 + c]) for c in range(2)
    ]
    for copy in copies:
        copy.start()
    for copy in copies:
        copy.wait()
    edge[2 * CX :, :] = jnp.broadcast_to(brk[...].astype(F32), (8, NZ))
    for c in range(2):
        edge[c * CX : (c + 1) * CX, :] = plane(ty, c, CY - 1)


def relay(*messages):
    z = position()[1] % 4
    row = lax.broadcasted_iota(jnp.int32, messages[0].shape, 0)
    out = jnp.zeros_like(messages[0])
    for k, ref in enumerate(messages):
        out = jnp.where(jnp.where(row < 2 * CX, z == 3 - PARTNERS[k], row == 2 * CX + k), ref, out)
    return out


def prepare_kernel(b_h, acc_h, tx_h, ty_h, tz_h, rhs, tx_o, ty_o, tz_o, diag, cross, b, acc, tx_v, ty_v, tz_v, sems):
    gx, gy = position()
    pairs = ((tx_h, tx_v), (ty_h, ty_v), (tz_h, tz_v), (acc_h, acc), (b_h, b))
    copies = [pltpu.make_async_copy(h, v, sems.at[i]) for i, (h, v) in enumerate(pairs)]
    for copy in copies:
        copy.start()
    last_x = jnp.logical_and(rows() == CX - 1, gx == N_GX - 1)
    last_z = lanes() == NZ - 1
    for copy in copies:
        copy.wait()
    for c in range(2):
        ly = 0.0
        for j in range(CY):
            tx = jnp.where(last_x, 0.0, plane(tx_v, c, j))
            tz = jnp.where(last_z, 0.0, plane(tz_v, c, j))
            ty = plane(ty_v, c, j)
            if j == CY - 1:
                ty = jnp.where(gy == N_GY - 1, 0.0, ty)
            tx_o[c, j] = tx
            tz_o[c, j] = tz
            ty_o[c, j] = ty
            faces = tx + from_row_before(tx, 0.0) + ty + ly + tz + pltpu.roll(tz, 1, 1)
            diag[c, j] = plane(acc, 3 * c, j) + faces
            cross[c, j] = plane(acc, 2 - c, j)
            rhs[c, j] = plane(b, c, j)
            ly = ty


def condense_kernel(diag, cross, ty, rhs, lx_in, *refs):
    messages, relayed = refs[:4], refs[4:8]
    seg_a, seg_b, dmat, tau_o, sinv, binv, ly_in = refs[8:15]
    brk, near, far = refs[15:]
    gy = position()[1]
    z_at, y_at = gy % 4, gy // 4
    for k in range(4):
        near[jnp.bitwise_xor(z_at, PARTNERS[k])] = messages[k][0 : 2 * CX, :]
        at = jnp.bitwise_xor(y_at, PARTNERS[k])
        far[at] = relayed[k][0 : 2 * CX, :]
        for i in range(4):
            row = relayed[k][2 * CX + i : 2 * CX + i + 1, :]
            brk[pl.ds(4 * at + jnp.bitwise_xor(z_at, PARTNERS[i]), 1), :] = row
    cuts = pltpu.roll(brk[...], (NZ - CY * gy) % NZ, 1)
    before = jnp.where(y_at > 0, far[jnp.maximum(y_at - 1, 0)], 0.0)
    before = jnp.where(z_at > 0, near[jnp.maximum(z_at - 1, 0)], before)
    for c in range(2):
        ly_in[c] = before[c * CX : (c + 1) * CX]
    for c in range(2):
        ly = ly_in[c]
        for j in range(CY):
            d = diag[c, j] + jnp.where(rows() == 0, lx_in[c, j : j + 1, :], 0.0)
            dmat[3 * c, j] = d + ly if j == 0 else d
        for j in range(CY + 1):
            keep = 1.0 - cuts[:, j : j + 1]
            tau_o[c, j] = (ty[c, j - 1] if j else ly) * keep
    for j in range(CY):
        dmat[1, j] = cross[0, j]
        dmat[2, j] = cross[1, j]

    def tau(j):
        return pair_at(tau_o, j)

    def outer(t, p):
        return tuple(x * y for x, y in zip(p, (t[0] * t[0], t[0] * t[1], t[1] * t[0], t[1] * t[1])))

    s = inv2(block_at(dmat, 0))
    e = inv2(block_at(dmat, CY - 1))
    zero = jnp.zeros(PLANE, F32)
    yf = (tau(0)[0], zero, zero, tau(0)[1])
    zl = (tau(CY)[0], zero, zero, tau(CY)[1])
    y = pair_at(rhs, 0)
    z = pair_at(rhs, CY - 1)
    for i in range(4):
        sinv[i, 0] = s[i]
        binv[i, CY - 1] = e[i]
    for j in range(1, CY):
        k = CY - 1 - j
        t, u = tau(j), tau(k + 1)
        yf = rows_by(t, mm(s, yf))
        zl = rows_by(u, mm(e, zl))
        yv, zv = mv(s, y), mv(e, z)
        y = tuple(rhs[c, j] + t[c] * yv[c] for c in range(2))
        z = tuple(rhs[c, k] + u[c] * zv[c] for c in range(2))
        s = inv2(tuple(d - x for d, x in zip(block_at(dmat, j), outer(t, s))))
        e = inv2(tuple(d - x for d, x in zip(block_at(dmat, k), outer(u, e))))
        for i in range(4):
            sinv[i, j] = s[i]
            binv[i, k] = e[i]
    whole = (columns_by(e, tau(0)), mm(e, zl), mm(s, yf), columns_by(s, tau(CY)), mv(e, z), mv(s, y))
    for half, ref in enumerate((seg_a, seg_b)):
        store_segment(ref, [[x[8 * half : 8 * half + 8] for x in part] for part in whole], True)


def gather_matrices(at_place, halves, mat_s):
    for k in range(4):
        at = jnp.bitwise_xor(at_place, PARTNERS[k])
        for half, refs in enumerate(halves):
            mat_s[at, :, 8 * half : 8 * half + 8, :] = refs[k][0:16]


def gather_vectors(at_place, vecs, vec_s):
    for k in range(4):
        vec_s[jnp.bitwise_xor(at_place, PARTNERS[k])] = vecs[k][...]


def gather_both(at_place, halves, mat_s, vec_s):
    gather_matrices(at_place, halves, mat_s)
    for k in range(4):
        at = jnp.bitwise_xor(at_place, PARTNERS[k])
        for half, refs in enumerate(halves):
            vec_s[at, :, 8 * half : 8 * half + 8, :] = refs[k][16:20]


def total_half_kernel(own, m1, m2, m3, out, segs_s):
    for k, ref in enumerate((own, m1, m2, m3)):
        segs_s[jnp.bitwise_xor(position()[1] % 4, PARTNERS[k])] = ref[...]
    segs = [load_segment(segs_s.at[m], segs_s.at[m], 16) for m in range(4)]
    store_segment(out, join(join(segs[0], segs[1]), join(segs[2], segs[3])), True)


def total_again_kernel(*refs):
    halves, vecs = (refs[0:4], refs[4:8]), refs[8:12]
    out, mat_s, vec_s = refs[12:]
    gather_matrices(position()[1] % 4, halves, mat_s)
    gather_vectors(position()[1] % 4, vecs, vec_s)
    segs = [load_segment(mat_s.at[m], vec_s.at[m], 0) for m in range(4)]
    store_segment(out, join(join(segs[0], segs[1]), join(segs[2], segs[3])), False)


def split3(x):
    hi = x.astype(BF16)
    rest = x - hi.astype(F32)
    mid = rest.astype(BF16)
    low = (rest - mid.astype(F32)).astype(BF16)
    return hi, mid, low


def slot_tables(cells, wells):
    cell = cells[...]
    row = jnp.bitwise_and(lax.shift_right_logical(cell, 7), 7) * CX + lax.shift_right_logical(cell, 10)
    shape = (NZ, SLOTS_ALL)
    up = lax.broadcasted_iota(jnp.int32, shape, 0)
    at_row = up == row
    at_layer = up == jnp.bitwise_and(cell, NZ - 1)
    at_well = up == wells[...]
    return at_row, at_layer, at_well


def ones_of(mask):
    return jnp.where(mask, 1.0, 0.0).astype(F32).astype(BF16)


NT = (((1,), (1,)), ((), ()))


def row_times(rows_in, table, dims):
    parts = [part for x in rows_in for part in split3(x)]
    n = len(rows_in)
    pad = 16 - 3 * n
    width = rows_in[0].shape[1]
    stacked = jnp.concatenate([p.astype(F32) for p in parts] + [jnp.zeros((pad, width), F32)], axis=0).astype(BF16)
    out = lax.dot_general(stacked, table, dims, preferred_element_type=F32)
    return [out[3 * i : 3 * i + 1] + out[3 * i + 1 : 3 * i + 2] + out[3 * i + 2 : 3 * i + 3] for i in range(n)]


def make_inner_kernel(whole):
    def kernel(*refs):
        halves = (refs[0:4], refs[4:8])
        vecs, rest = (None, refs[8:]) if whole else (refs[8:12], refs[12:])
        if whole:
            sinv, tau_r, rhs, left, right, base, from_left, from_right, mat_s, vec_s = rest
        else:
            sinv, tau_r, rhs, left, right, base, mat_s, vec_s = rest
        z = position()[1] % 4
        if whole:
            gather_both(z, halves, mat_s, vec_s)
        else:
            gather_matrices(z, halves, mat_s)
            gather_vectors(z, vecs, vec_s)
        segs = [load_segment(mat_s.at[m], vec_s.at[m], 0) for m in range(4)]
        pair = join(segs[0], segs[1])
        store_segment(left, choose(z == 1, segs[0], choose(z == 2, pair, join(pair, segs[2]))), True)
        pair = join(segs[2], segs[3])
        store_segment(right, choose(z == 2, segs[3], choose(z == 1, pair, join(segs[1], pair))), True)

        def tau(j):
            return pair_at(tau_r, j)

        def sv(j):
            return block_at(sinv, j)

        y = sweep_forward(sv, tau, [pair_at(rhs, j) for j in range(CY)])
        u = None
        for j in range(CY - 1, -1, -1):
            v = y[j] if u is None else tuple(y[j][c] + tau(j + 1)[c] * u[c] for c in range(2))
            u = mv(sv(j), v)
            for c in range(2):
                base[c, j] = u[c]
        if not whole:
            return
        zero = jnp.zeros(PLANE, F32)
        units = [(tau(0)[0], zero, zero, tau(0)[1])]
        for j in range(1, CY):
            units.append(rows_by(tau(j), mm(sv(j - 1), units[-1])))
        ul = ur = None
        for j in range(CY - 1, -1, -1):
            if ul is None:
                ul = mm(sv(j), units[j])
                ur = columns_by(sv(j), tau(CY))
            else:
                ul = mm(sv(j), madd(units[j], rows_by(tau(j + 1), ul)))
                ur = mm(sv(j), rows_by(tau(j + 1), ur))
            for i in range(4):
                from_left[i, j] = ul[i]
                from_right[i, j] = ur[i]

    return kernel


def make_solve_kernel(whole):
    def kernel(*refs):
        own_m, outer = refs[0:2], (refs[2:6], refs[6:10])
        own_v, outer_v, rest = (None, None, refs[10:]) if whole else (refs[10], refs[11:15], refs[15:])
        left, right, base, from_left, from_right, cells, wells, weights = rest[:8]
        p_out, ends, msg_a, msg_b = rest[8:12]
        mat_o, vec_o, mat_i, vec_i, edge = rest[12:]
        gx, gy = position()
        z_at, y_at = gy % 4, gy // 4
        for half, ref in enumerate(own_m):
            mat_i[:, 8 * half : 8 * half + 8, :] = ref[0:16]
            if whole:
                vec_i[:, 8 * half : 8 * half + 8, :] = ref[16:20]
        if whole:
            gather_both(y_at, outer, mat_o, vec_o)
        else:
            vec_i[...] = own_v[...]
            gather_matrices(y_at, outer, mat_o)
            gather_vectors(y_at, outer_v, vec_o)
        zero = jnp.zeros(PLANE, F32)
        before = ((zero,) * 4, (zero,) * 2)
        after = ((zero,) * 4, (zero,) * 2)
        for m in range(3):
            seg = load_segment(mat_o.at[m], vec_o.at[m], 0)
            before = choose(m < y_at, join_before(before, seg), before)
            m = 3 - m
            seg = load_segment(mat_o.at[m], vec_o.at[m], 0)
            after = choose(m > y_at, join_after(seg, after), after)
        before = choose(z_at > 0, join_before(before, load_segment(left, left, 16)), before)
        after = choose(z_at < 3, join_after(load_segment(right, right, 16), after), after)
        own = load_segment(mat_i, vec_i, 0)
        ff, fl, lf, ll, gf, gl = own
        up_m, up_v = join_before(before, own)
        last = mv(inv2(one_minus(mm(up_m, after[0]))), madd(up_v, mv(up_m, after[1])))
        beyond = madd(after[1], mv(after[0], last))
        k = inv2(one_minus(mm(ff, before[0])))
        first = mv(k, madd(madd(gf, mv(ff, before[1])), mv(fl, beyond)))
        behind = madd(before[1], mv(before[0], first))
        for c in range(2):
            ends[c] = behind[c]
            ends[2 + c] = beyond[c]

        for j in range(CY):
            u = madd(pair_at(base, j), madd(mv(block_at(from_left, j), behind), mv(block_at(from_right, j), beyond)))
            for c in range(2):
                p_out[c, j] = u[c]
                edge[0, c * CY + j : c * CY + j + 1, :] = u[c][0:1, :]
                edge[1, c * CY + j : c * CY + j + 1, :] = u[c][CX - 1 : CX, :]
        at_row, at_layer, at_well = slot_tables(cells, wells)
        pressure = jnp.concatenate([p_out[0, j] for j in range(CY)], axis=0)
        table = ones_of(at_layer)
        picked = sum(jnp.dot(part, table, preferred_element_type=F32) for part in split3(pressure))
        values = jnp.sum(jnp.where(at_row, picked, 0.0), axis=0, keepdims=True)
        w = weights[...]
        sums, totals = row_times([w * values, w], ones_of(at_well), NT)
        tail = jnp.concatenate([sums, totals, jnp.zeros((6, W_ALL), F32)], axis=0)
        even = gx % 2 == 0
        low, high = edge[0], edge[1]
        msg_a[0:16, :] = jnp.where(even, high, low)
        msg_b[0:16, :] = jnp.where(even, low, high)
        msg_a[16:24, :] = tail
        msg_b[16:24, :] = tail

    return kernel


def apply_operator(got, cells, wells, weights):
    gx = position()[0]
    got_a, sent_b, got_c, got_b, got_d = got
    tail = sent_b[16:24, :] + got_b[16:24, :] + got_c[...] + got_d[...]
    rates = tail[0:1] / jnp.maximum(tail[1:2], 1.0)
    at_row, at_layer, at_well = slot_tables(cells, wells)
    slot_rate = row_times([rates], ones_of(at_well), (((1,), (0,)), ((), ())))[0]
    added = jnp.where(at_layer, weights[...] * slot_rate, 0.0)
    table = ones_of(at_row)
    well_add = sum(lax.dot_general(table, part, NT, preferred_element_type=F32) for part in split3(added))
    even = gx % 2 == 0
    halo_a, halo_b = got_a[0:16, :], got_b[0:16, :]
    from_after = jnp.where(gx < N_GX - 1, jnp.where(even, halo_a, halo_b), 0.0)
    from_before = jnp.where(gx > 0, jnp.where(even, halo_b, halo_a), 0.0)
    return well_add, from_after, from_before


def operator_plane(c, j, p, ends, dmat, tx, ty, tz, lx_in, ly_in, halo, well_add):
    from_after, from_before = halo
    here = p[c, j]
    up = p[c, j + 1] if j < CY - 1 else ends[2 + c]
    down = p[c, j - 1] if j > 0 else ends[c]
    t = tx[c, j]
    at = c * CY + j
    beside = t * from_row_after(here, from_after[at : at + 1])
    beside = beside + from_row_before(t * here, lx_in[c, j : j + 1, :] * from_before[at : at + 1])
    beside = beside + ty[c, j] * up + (ty[c, j - 1] if j else ly_in[c]) * down
    tzp = tz[c, j]
    beside = beside + tzp * pltpu.roll(here, NZ - 1, 1) + pltpu.roll(tzp * here, 1, 1)
    out = dmat[2 * c, j] * p[0, j] + dmat[2 * c + 1, j] * p[1, j] - beside
    if c == 0:
        out = out + well_add[j * CX : (j + 1) * CX]
    return out


def first_image_kernel(got_a, sent_b, got_c, got_b, got_d, p, ends, dmat, tau_r, sinv, binv, rhs, tx, ty, tz, lx_in, ly_in, cells, wells, weights, q_out, e_out, vec_out, dots):
    well_add, after, before = apply_operator((got_a, sent_b, got_c, got_b, got_d), cells, wells, weights)
    eq = jnp.zeros(PLANE, F32)
    qq = jnp.zeros(PLANE, F32)
    e = []
    for j in range(CY):
        pair = []
        for c in range(2):
            q = operator_plane(c, j, p, ends, dmat, tx, ty, tz, lx_in, ly_in, (after, before), well_add)
            rest = rhs[c, j] - q
            q_out[c, j] = q
            e_out[c, j] = rest
            eq = eq + rest * q
            qq = qq + q * q
            pair.append(rest)
        e.append(tuple(pair))
    dots[0] = eq
    dots[1] = qq

    def tau(j):
        return pair_at(tau_r, j)

    y = sweep_forward(lambda j: block_at(sinv, j), tau, e)[CY - 1]
    z = sweep_backward(lambda j: block_at(binv, j), tau, e)
    first = mv(block_at(binv, 0), z)
    last = mv(block_at(sinv, CY - 1), y)
    for c in range(2):
        vec_out[c] = first[c]
        vec_out[2 + c] = last[c]


def second_image_kernel(got_a, sent_b, got_c, got_b, got_d, p, ends, dmat, tx, ty, tz, lx_in, ly_in, cells, wells, weights, q_in, e_in, dots_in, s_out, dots):
    well_add, after, before = apply_operator((got_a, sent_b, got_c, got_b, got_d), cells, wells, weights)
    sq = jnp.zeros(PLANE, F32)
    ss = jnp.zeros(PLANE, F32)
    es = jnp.zeros(PLANE, F32)
    for j in range(CY):
        for c in range(2):
            s = operator_plane(c, j, p, ends, dmat, tx, ty, tz, lx_in, ly_in, (after, before), well_add)
            s_out[c, j] = s
            sq = sq + s * q_in[c, j]
            ss = ss + s * s
            es = es + s * e_in[c, j]
    sums = [jnp.sum(x, axis=0, keepdims=True) for x in (dots_in[0], dots_in[1], sq, ss, es)]
    lane = lax.broadcasted_iota(jnp.int32, (1, NZ), 1)
    row = jnp.zeros((1, NZ), F32)
    for i, x in enumerate(sums):
        row = jnp.where(lane == i, jnp.sum(x, axis=1, keepdims=True), row)
    dots[...] = row


def finish_kernel(got, p, w, q, e, s, x_out, r_out):
    total = jnp.sum(got[...], axis=0, keepdims=True)
    lane = lax.broadcasted_iota(jnp.int32, (1, NZ), 1)
    eq, qq, sq, ss, es = (
        jnp.broadcast_to(jnp.sum(jnp.where(lane == i, total, 0.0), axis=1, keepdims=True), (1, NZ)) for i in range(5)
    )
    rest = -eq / qq
    g = sq / qq
    k = (es - g * eq) / (ss - g * sq)
    on_p = (1.0 - rest) - k * g
    on_q = rest + k * g
    for c in range(2):
        for j in range(CY):
            at = pl.ds(j, CX, stride=CY)
            x_out.at[c][at, :] = on_p * p[c, j] + k * w[c, j]
            r_out.at[c][at, :] = e[c, j] + on_q * q[c, j] - k * s[c, j]


def call(kernel, name, outs, scratch, *args, specs=None, vmem=24 * 1024):
    outs = [o if isinstance(o, jax.ShapeDtypeStruct) else jax.ShapeDtypeStruct(o, F32) for o in outs]
    return pl.pallas_call(
        kernel,
        name=name,
        out_shape=tuple(outs),
        in_specs=specs or [VMEM] * len(args),
        out_specs=tuple(VMEM for _ in outs),
        scratch_shapes=[pltpu.VMEM(s, F32) if isinstance(s, tuple) else s for s in scratch],
        compiler_params=pltpu.CompilerParams(vmem_limit_bytes=vmem * 1024),
    )(*args)


def swapped(block, stride):
    others = [lax.ppermute(block, "gy", [(i, i ^ (k * stride)) for i in range(N_GY)]) for k in PARTNERS[1:]]
    return [block] + others


def exchange_rows(msg_a, msg_b):
    got_a = lax.ppermute(msg_a, "gx", [(i, i ^ 1) for i in range(N_GX)])
    below = lax.broadcasted_iota(jnp.int32, msg_b.shape, 0) >= 16
    tail = msg_b[16:] + got_a[16:]
    sent_b = msg_b + jnp.where(below, got_a, 0.0)
    got_d = lax.ppermute(tail, "gx", [(i, (i + 2 if i % 2 else i - 2) % N_GX) for i in range(N_GX)])
    got_b = lax.ppermute(sent_b, "gx", [(i, (i + 1 if i % 2 else i - 1) % N_GX) for i in range(N_GX)])
    got_c = lax.ppermute(tail, "gx", [(i, i ^ 4) for i in range(N_GX)])
    return got_a, sent_b, got_c, got_b, got_d


def sum_everywhere(x):
    x = x + lax.ppermute(x, "gx", [(i, i ^ 1) for i in range(N_GX)])
    others = [lax.ppermute(x, "gx", [(i, (i + 2 * k) % N_GX) for i in range(N_GX)]) for k in PARTNERS[1:]]
    x = x + others[0] + others[1] + others[2]
    x = jnp.broadcast_to(x, (N_GY, NZ))
    return lax.all_to_all(x, "gy", split_axis=0, concat_axis=0, tiled=True)


def body(right_side, accumulation, trans_x, trans_y, trans_z, perf_cell, perf_well, perf_weight, perf_count, breaks):

    def flat(a):
        return a.reshape(a.shape[0], CX * CY, NZ)

    field, block, part = (2, CY, CX, NZ), (4, CY, CX, NZ), (2, CY + 1, CX, NZ)
    half, vec, message = (20, 8, NZ), (4, CX, NZ), (24, NZ)
    order = [(4, 16, CX, NZ), (4, 4, CX, NZ)]
    two, four = (2, CX * CY, NZ), (4, CX * CY, NZ)
    sx, edge = call(
        edges_kernel, "edges", ((2, CY, NZ), (40, NZ)),
        [two, pltpu.VMEM((1, NZ), jnp.int32), pltpu.SemaphoreType.DMA((4,))],
        flat(trans_x), flat(trans_y), breaks, specs=[HBM] * 3, vmem=EDGES_VMEM,
    )
    rhs, tx, ty, tz, diag, cross = call(
        prepare_kernel, "prepare", (field,) * 6,
        [two, four, two, two, two, pltpu.SemaphoreType.DMA((5,))],
        flat(right_side), flat(accumulation), flat(trans_x), flat(trans_y), flat(trans_z),
        specs=[HBM] * 5, vmem=PREPARE_VMEM,
    )
    edges = swapped(edge, 1)
    lx = lax.ppermute(sx, "gx", [(i, i + 1) for i in range(N_GX - 1)])
    *edges, lx = lax.optimization_barrier((*edges, lx))
    relayed = swapped(relay(*edges), 4)
    slots = perf_cell.shape[3]
    live = jnp.arange(slots, dtype=jnp.int32)[None, :] < perf_count.reshape(N_GX, 1)
    weights = jnp.where(live, perf_weight.reshape(N_GX, slots), 0.0).reshape(1, SLOTS_ALL)
    owners = jnp.arange(N_GX, dtype=jnp.int32)[:, None] * 16
    wells = (perf_well.reshape(N_GX, slots) + owners).reshape(1, SLOTS_ALL)
    cells = perf_cell.reshape(1, SLOTS_ALL)
    perfs = (cells, wells, weights)

    own_a, own_b, dmat, tau, sinv, binv, ly = call(
        condense_kernel, "condense", (half, half, block, part, block, block, (2, CX, NZ)),
        [(N_GY, NZ), (4, 2 * CX, NZ), (4, 2 * CX, NZ)], diag, cross, ty, rhs, lx, *edges, *relayed,
    )
    inner, outer = [], []
    for own in (own_a, own_b):
        inner.append(swapped(own, 1))
    for near in inner:
        (group,) = call(total_half_kernel, "group_total", (half,), [(4,) + half], *near)
        outer.append(swapped(group, 4))
    inner = inner[0] + inner[1]
    outer = outer[0] + outer[1]
    solve_scratch = order + [(16, CX, NZ), (4, CX, NZ), (2, 16, NZ)]
    joined = (20, CX, NZ)
    left, right, base, from_left, from_right = call(
        make_inner_kernel(True), "inner_first", (joined, joined, field, block, block), order, *inner, sinv, tau, rhs,
    )
    owns = (own_a, own_b)
    p, ends, msg_a, msg_b = call(
        make_solve_kernel(True), "solve_first", (field, vec, message, message), solve_scratch,
        *owns, *outer, left, right, base, from_left, from_right, *perfs,
    )
    got = exchange_rows(msg_a, msg_b)
    q, e, own_v, dots = call(
        first_image_kernel, "first_image", (field, field, vec, (2, CX, NZ)), [],
        *got, p, ends, dmat, tau, sinv, binv, rhs, tx, ty, tz, lx, ly, *perfs,
    )
    inner_v = swapped(own_v, 1)
    (group_v,) = call(total_again_kernel, "group_total_again", (vec,), order, *inner, *inner_v)
    outer_v = swapped(group_v, 4)
    left, right, base = call(
        make_inner_kernel(False), "inner_second", (joined, joined, field), order, *inner, *inner_v, sinv, tau, e,
    )
    w, ends, msg_a, msg_b = call(
        make_solve_kernel(False), "solve_second", (field, vec, message, message), solve_scratch,
        *owns, *outer, own_v, *outer_v, left, right, base, from_left, from_right, *perfs,
    )
    got = exchange_rows(msg_a, msg_b)
    s, dots = call(
        second_image_kernel, "second_image", (field, (1, NZ)), [],
        *got, w, ends, dmat, tx, ty, tz, lx, ly, *perfs, q, e, dots,
    )
    dots = sum_everywhere(dots)
    x, r = call(finish_kernel, "finish", (two, two), [], dots, p, w, q, e, s)
    shape = (2, CX, CY, NZ)
    return x.reshape(shape), r.reshape(shape)


def solution(mesh):
    tile = P(None, "gx", "gy", None)
    slots = P("gx", "gy", None, None)
    return jax.shard_map(
        body,
        mesh=mesh,
        in_specs=(tile,) * 5 + (slots,) * 3 + (P("gx", "gy", None), P(("gx", "gy"), None)),
        out_specs=(tile, tile),
        check_vma=False,
    )
```

```python
import jax
import jax.numpy as jnp
from jax import lax
from jax.experimental import pallas as pl
from jax.experimental.pallas import tpu as pltpu
from jax.sharding import PartitionSpec as P

F32 = jnp.float32
BF16 = jnp.bfloat16
VMEM = pl.BlockSpec(memory_space=pltpu.VMEM)
HBM = pl.BlockSpec(memory_space=pltpu.HBM)
SMEM = pl.BlockSpec(memory_space=pltpu.SMEM)
CX, CY, NZ = 16, 8, 128
PLANE = (CX, NZ)
N_GX, N_GY = 8, 16
W_ALL = 128
PARTNERS = (0, 3, 2, 1)
PREPARE_VMEM = 54400
EDGES_VMEM = 55296
SLOTS_ALL = 256


def mm(p, q):
    return (
        p[0] * q[0] + p[1] * q[2],
        p[0] * q[1] + p[1] * q[3],
        p[2] * q[0] + p[3] * q[2],
        p[2] * q[1] + p[3] * q[3],
    )


def mv(p, v):
    return (p[0] * v[0] + p[1] * v[1], p[2] * v[0] + p[3] * v[1])


def madd(p, q):
    return tuple(a + b for a, b in zip(p, q))


def inv2(p):
    t = 1.0 / (p[0] * p[3] - p[1] * p[2])
    return (p[3] * t, -p[1] * t, -p[2] * t, p[0] * t)


def one_minus(p):
    return (1.0 - p[0], -p[1], -p[2], 1.0 - p[3])


def rows_by(t, p):
    return (t[0] * p[0], t[0] * p[1], t[1] * p[2], t[1] * p[3])


def columns_by(p, t):
    return (p[0] * t[0], p[1] * t[1], p[2] * t[0], p[3] * t[1])


def join(a, b):
    ff1, fl1, lf1, ll1, gf1, gl1 = a
    ff2, fl2, lf2, ll2, gf2, gl2 = b
    k = inv2(one_minus(mm(ll1, ff2)))
    last = mv(k, madd(gl1, mv(ll1, gf2)))
    last_b = mm(k, lf1)
    last_a = mm(k, mm(ll1, fl2))
    first = madd(gf2, mv(ff2, last))
    first_b = mm(ff2, last_b)
    first_a = madd(fl2, mm(ff2, last_a))
    return (
        madd(ff1, mm(fl1, first_b)),
        mm(fl1, first_a),
        mm(lf2, last_b),
        madd(ll2, mm(lf2, last_a)),
        madd(gf1, mv(fl1, first)),
        madd(gl2, mv(lf2, last)),
    )


def join_before(before, s):
    gm, g = before
    ff, fl, lf, ll, gf, gl = s
    k = inv2(one_minus(mm(ff, gm)))
    a = mv(k, madd(gf, mv(ff, g)))
    am = mm(k, fl)
    return (madd(ll, mm(lf, mm(gm, am))), madd(gl, mv(lf, madd(g, mv(gm, a)))))


def join_after(s, after):
    gm, g = after
    ff, fl, lf, ll, gf, gl = s
    k = inv2(one_minus(mm(ll, gm)))
    a = mv(k, madd(gl, mv(ll, g)))
    am = mm(k, lf)
    return (madd(ff, mm(fl, mm(gm, am))), madd(gf, mv(fl, madd(g, mv(gm, a)))))


def position():
    return lax.axis_index("gx"), lax.axis_index("gy")


def choose(flag, new, old):
    return tuple(tuple(jnp.where(flag, n, o) for n, o in zip(ns, os)) for ns, os in zip(new, old))


def load_segment(mat, vec, offset):
    m = [mat[i] for i in range(16)]
    v = [vec[offset + i] for i in range(4)]
    return (tuple(m[0:4]), tuple(m[4:8]), tuple(m[8:12]), tuple(m[12:16]), (v[0], v[1]), (v[2], v[3]))


def store_segment(ref, seg, whole):
    flat = [x for part in seg for x in part]
    if not whole:
        flat = flat[16:]
    for i, x in enumerate(flat):
        ref[i] = x


def lanes():
    return lax.broadcasted_iota(jnp.int32, PLANE, 1)


def rows():
    return lax.broadcasted_iota(jnp.int32, PLANE, 0)


def from_row_before(plane, edge):
    return jnp.where(rows() == 0, edge, pltpu.roll(plane, 1, 0))


def from_row_after(plane, edge):
    return jnp.where(rows() == CX - 1, edge, pltpu.roll(plane, CX - 1, 0))


def sweep_forward(sinv, tau, rhs):
    y = [rhs[0]]
    for j in range(1, CY):
        t = mv(sinv(j - 1), y[-1])
        y.append((rhs[j][0] + tau(j)[0] * t[0], rhs[j][1] + tau(j)[1] * t[1]))
    return y


def sweep_backward(binv, tau, rhs):
    z = rhs[CY - 1]
    for j in range(CY - 2, -1, -1):
        t = mv(binv(j + 1), z)
        z = (rhs[j][0] + tau(j + 1)[0] * t[0], rhs[j][1] + tau(j + 1)[1] * t[1])
    return z


def block_at(ref, j):
    return tuple(ref[i, j] for i in range(4))


def pair_at(ref, j):
    return (ref[0, j], ref[1, j])


def plane(ref, c, j):
    return ref.at[c][pl.ds(j, CX, stride=CY), :]


def edges_kernel(tx_h, ty_h, brk_h, sx, edge, ty, brk, sems):
    copies = [pltpu.make_async_copy(h, v, sems.at[i]) for i, (h, v) in enumerate(((ty_h, ty), (brk_h, brk)))]
    copies += [
        pltpu.make_async_copy(tx_h.at[c, (CX - 1) * CY : CX * CY, :], sx.at[c], sems.at[2 + c]) for c in range(2)
    ]
    for copy in copies:
        copy.start()
    for copy in copies:
        copy.wait()
    edge[2 * CX :, :] = jnp.broadcast_to(brk[...].astype(F32), (8, NZ))
    for c in range(2):
        edge[c * CX : (c + 1) * CX, :] = plane(ty, c, CY - 1)


def relay(*messages):
    z = position()[1] % 4
    row = lax.broadcasted_iota(jnp.int32, messages[0].shape, 0)
    out = jnp.zeros_like(messages[0])
    for k, ref in enumerate(messages):
        out = jnp.where(jnp.where(row < 2 * CX, z == 3 - PARTNERS[k], row == 2 * CX + k), ref, out)
    return out


def prepare_kernel(b_h, acc_h, tx_h, ty_h, tz_h, rhs, tx_o, ty_o, tz_o, diag, cross, b, acc, tx_v, ty_v, tz_v, sems):
    gx, gy = position()
    pairs = ((tx_h, tx_v), (ty_h, ty_v), (tz_h, tz_v), (acc_h, acc), (b_h, b))
    copies = [pltpu.make_async_copy(h, v, sems.at[i]) for i, (h, v) in enumerate(pairs)]
    for copy in copies:
        copy.start()
    last_x = jnp.logical_and(rows() == CX - 1, gx == N_GX - 1)
    last_z = lanes() == NZ - 1
    for copy in copies:
        copy.wait()
    for c in range(2):
        ly = 0.0
        for j in range(CY):
            tx = jnp.where(last_x, 0.0, plane(tx_v, c, j))
            tz = jnp.where(last_z, 0.0, plane(tz_v, c, j))
            ty = plane(ty_v, c, j)
            if j == CY - 1:
                ty = jnp.where(gy == N_GY - 1, 0.0, ty)
            tx_o[c, j] = tx
            tz_o[c, j] = tz
            ty_o[c, j] = ty
            faces = tx + from_row_before(tx, 0.0) + ty + ly + tz + pltpu.roll(tz, 1, 1)
            diag[c, j] = plane(acc, 3 * c, j) + faces
            cross[c, j] = plane(acc, 2 - c, j)
            rhs[c, j] = plane(b, c, j)
            ly = ty


def condense_kernel(diag, cross, ty, rhs, lx_in, *refs):
    messages, relayed = refs[:4], refs[4:8]
    seg_a, seg_b, dmat, tau_o, sinv, binv, ly_in = refs[8:15]
    brk, near, far = refs[15:]
    gy = position()[1]
    z_at, y_at = gy % 4, gy // 4
    for k in range(4):
        near[jnp.bitwise_xor(z_at, PARTNERS[k])] = messages[k][0 : 2 * CX, :]
        at = jnp.bitwise_xor(y_at, PARTNERS[k])
        far[at] = relayed[k][0 : 2 * CX, :]
        for i in range(4):
            row = relayed[k][2 * CX + i : 2 * CX + i + 1, :]
            brk[pl.ds(4 * at + jnp.bitwise_xor(z_at, PARTNERS[i]), 1), :] = row
    cuts = pltpu.roll(brk[...], (NZ - CY * gy) % NZ, 1)
    before = jnp.where(y_at > 0, far[jnp.maximum(y_at - 1, 0)], 0.0)
    before = jnp.where(z_at > 0, near[jnp.maximum(z_at - 1, 0)], before)
    for c in range(2):
        ly_in[c] = before[c * CX : (c + 1) * CX]
    for c in range(2):
        ly = ly_in[c]
        for j in range(CY):
            d = diag[c, j] + jnp.where(rows() == 0, lx_in[c, j : j + 1, :], 0.0)
            dmat[3 * c, j] = d + ly if j == 0 else d
        for j in range(CY + 1):
            keep = 1.0 - cuts[:, j : j + 1]
            tau_o[c, j] = (ty[c, j - 1] if j else ly) * keep
    for j in range(CY):
        dmat[1, j] = cross[0, j]
        dmat[2, j] = cross[1, j]

    def tau(j):
        return pair_at(tau_o, j)

    def outer(t, p):
        return tuple(x * y for x, y in zip(p, (t[0] * t[0], t[0] * t[1], t[1] * t[0], t[1] * t[1])))

    s = inv2(block_at(dmat, 0))
    e = inv2(block_at(dmat, CY - 1))
    zero = jnp.zeros(PLANE, F32)
    yf = (tau(0)[0], zero, zero, tau(0)[1])
    zl = (tau(CY)[0], zero, zero, tau(CY)[1])
    y = pair_at(rhs, 0)
    z = pair_at(rhs, CY - 1)
    for i in range(4):
        sinv[i, 0] = s[i]
        binv[i, CY - 1] = e[i]
    for j in range(1, CY):
        k = CY - 1 - j
        t, u = tau(j), tau(k + 1)
        yf = rows_by(t, mm(s, yf))
        zl = rows_by(u, mm(e, zl))
        yv, zv = mv(s, y), mv(e, z)
        y = tuple(rhs[c, j] + t[c] * yv[c] for c in range(2))
        z = tuple(rhs[c, k] + u[c] * zv[c] for c in range(2))
        s = inv2(tuple(d - x for d, x in zip(block_at(dmat, j), outer(t, s))))
        e = inv2(tuple(d - x for d, x in zip(block_at(dmat, k), outer(u, e))))
        for i in range(4):
            sinv[i, j] = s[i]
            binv[i, k] = e[i]
    whole = (columns_by(e, tau(0)), mm(e, zl), mm(s, yf), columns_by(s, tau(CY)), mv(e, z), mv(s, y))
    for half, ref in enumerate((seg_a, seg_b)):
        store_segment(ref, [[x[8 * half : 8 * half + 8] for x in part] for part in whole], True)


def gather_matrices(at_place, halves, mat_s):
    for k in range(4):
        at = jnp.bitwise_xor(at_place, PARTNERS[k])
        for half, refs in enumerate(halves):
            mat_s[at, :, 8 * half : 8 * half + 8, :] = refs[k][0:16]


def gather_vectors(at_place, vecs, vec_s):
    for k in range(4):
        vec_s[jnp.bitwise_xor(at_place, PARTNERS[k])] = vecs[k][...]


def gather_both(at_place, halves, mat_s, vec_s):
    gather_matrices(at_place, halves, mat_s)
    for k in range(4):
        at = jnp.bitwise_xor(at_place, PARTNERS[k])
        for half, refs in enumerate(halves):
            vec_s[at, :, 8 * half : 8 * half + 8, :] = refs[k][16:20]


def total_half_kernel(own, m1, m2, m3, out, segs_s):
    for k, ref in enumerate((own, m1, m2, m3)):
        segs_s[jnp.bitwise_xor(position()[1] % 4, PARTNERS[k])] = ref[...]
    segs = [load_segment(segs_s.at[m], segs_s.at[m], 16) for m in range(4)]
    store_segment(out, join(join(segs[0], segs[1]), join(segs[2], segs[3])), True)


def total_again_kernel(*refs):
    halves, vecs = (refs[0:4], refs[4:8]), refs[8:12]
    out, mat_s, vec_s = refs[12:]
    gather_matrices(position()[1] % 4, halves, mat_s)
    gather_vectors(position()[1] % 4, vecs, vec_s)
    segs = [load_segment(mat_s.at[m], vec_s.at[m], 0) for m in range(4)]
    store_segment(out, join(join(segs[0], segs[1]), join(segs[2], segs[3])), False)


def split3(x):
    hi = x.astype(BF16)
    rest = x - hi.astype(F32)
    mid = rest.astype(BF16)
    low = (rest - mid.astype(F32)).astype(BF16)
    return hi, mid, low


def slot_tables(cells, wells):
    cell = cells[...]
    row = jnp.bitwise_and(lax.shift_right_logical(cell, 7), 7) * CX + lax.shift_right_logical(cell, 10)
    shape = (NZ, SLOTS_ALL)
    up = lax.broadcasted_iota(jnp.int32, shape, 0)
    at_row = up == row
    at_layer = up == jnp.bitwise_and(cell, NZ - 1)
    at_well = up == wells[...]
    return at_row, at_layer, at_well


def ones_of(mask):
    return jnp.where(mask, 1.0, 0.0).astype(F32).astype(BF16)


NT = (((1,), (1,)), ((), ()))


def row_times(rows_in, table, dims):
    parts = [part for x in rows_in for part in split3(x)]
    n = len(rows_in)
    pad = 16 - 3 * n
    width = rows_in[0].shape[1]
    stacked = jnp.concatenate([p.astype(F32) for p in parts] + [jnp.zeros((pad, width), F32)], axis=0).astype(BF16)
    out = lax.dot_general(stacked, table, dims, preferred_element_type=F32)
    return [out[3 * i : 3 * i + 1] + out[3 * i + 1 : 3 * i + 2] + out[3 * i + 2 : 3 * i + 3] for i in range(n)]


def make_inner_kernel(whole):
    def kernel(*refs):
        halves = (refs[0:4], refs[4:8])
        vecs, rest = (None, refs[8:]) if whole else (refs[8:12], refs[12:])
        if whole:
            sinv, tau_r, rhs, left, right, base, from_left, from_right, mat_s, vec_s = rest
        else:
            sinv, tau_r, rhs, left, right, base, mat_s, vec_s = rest
        z = position()[1] % 4
        if whole:
            gather_both(z, halves, mat_s, vec_s)
        else:
            gather_matrices(z, halves, mat_s)
            gather_vectors(z, vecs, vec_s)
        segs = [load_segment(mat_s.at[m], vec_s.at[m], 0) for m in range(4)]
        pair = join(segs[0], segs[1])
        store_segment(left, choose(z == 1, segs[0], choose(z == 2, pair, join(pair, segs[2]))), True)
        pair = join(segs[2], segs[3])
        store_segment(right, choose(z == 2, segs[3], choose(z == 1, pair, join(segs[1], pair))), True)

        def tau(j):
            return pair_at(tau_r, j)

        def sv(j):
            return block_at(sinv, j)

        y = sweep_forward(sv, tau, [pair_at(rhs, j) for j in range(CY)])
        u = None
        for j in range(CY - 1, -1, -1):
            v = y[j] if u is None else tuple(y[j][c] + tau(j + 1)[c] * u[c] for c in range(2))
            u = mv(sv(j), v)
            for c in range(2):
                base[c, j] = u[c]
        if not whole:
            return
        zero = jnp.zeros(PLANE, F32)
        units = [(tau(0)[0], zero, zero, tau(0)[1])]
        for j in range(1, CY):
            units.append(rows_by(tau(j), mm(sv(j - 1), units[-1])))
        ul = ur = None
        for j in range(CY - 1, -1, -1):
            if ul is None:
                ul = mm(sv(j), units[j])
                ur = columns_by(sv(j), tau(CY))
            else:
                ul = mm(sv(j), madd(units[j], rows_by(tau(j + 1), ul)))
                ur = mm(sv(j), rows_by(tau(j + 1), ur))
            for i in range(4):
                from_left[i, j] = ul[i]
                from_right[i, j] = ur[i]

    return kernel


def make_solve_kernel(whole):
    def kernel(*refs):
        own_m, outer = refs[0:2], (refs[2:6], refs[6:10])
        own_v, outer_v, rest = (None, None, refs[10:]) if whole else (refs[10], refs[11:15], refs[15:])
        left, right, base, from_left, from_right, cells, wells, weights = rest[:8]
        p_out, ends, msg_a, msg_b = rest[8:12]
        mat_o, vec_o, mat_i, vec_i, edge = rest[12:]
        gx, gy = position()
        z_at, y_at = gy % 4, gy // 4
        for half, ref in enumerate(own_m):
            mat_i[:, 8 * half : 8 * half + 8, :] = ref[0:16]
            if whole:
                vec_i[:, 8 * half : 8 * half + 8, :] = ref[16:20]
        if whole:
            gather_both(y_at, outer, mat_o, vec_o)
        else:
            vec_i[...] = own_v[...]
            gather_matrices(y_at, outer, mat_o)
            gather_vectors(y_at, outer_v, vec_o)
        zero = jnp.zeros(PLANE, F32)
        before = ((zero,) * 4, (zero,) * 2)
        after = ((zero,) * 4, (zero,) * 2)
        for m in range(3):
            seg = load_segment(mat_o.at[m], vec_o.at[m], 0)
            before = choose(m < y_at, join_before(before, seg), before)
            m = 3 - m
            seg = load_segment(mat_o.at[m], vec_o.at[m], 0)
            after = choose(m > y_at, join_after(seg, after), after)
        before = choose(z_at > 0, join_before(before, load_segment(left, left, 16)), before)
        after = choose(z_at < 3, join_after(load_segment(right, right, 16), after), after)
        own = load_segment(mat_i, vec_i, 0)
        ff, fl, lf, ll, gf, gl = own
        up_m, up_v = join_before(before, own)
        last = mv(inv2(one_minus(mm(up_m, after[0]))), madd(up_v, mv(up_m, after[1])))
        beyond = madd(after[1], mv(after[0], last))
        k = inv2(one_minus(mm(ff, before[0])))
        first = mv(k, madd(madd(gf, mv(ff, before[1])), mv(fl, beyond)))
        behind = madd(before[1], mv(before[0], first))
        for c in range(2):
            ends[c] = behind[c]
            ends[2 + c] = beyond[c]

        for j in range(CY):
            u = madd(pair_at(base, j), madd(mv(block_at(from_left, j), behind), mv(block_at(from_right, j), beyond)))
            for c in range(2):
                p_out[c, j] = u[c]
                edge[0, c * CY + j : c * CY + j + 1, :] = u[c][0:1, :]
                edge[1, c * CY + j : c * CY + j + 1, :] = u[c][CX - 1 : CX, :]
        at_row, at_layer, at_well = slot_tables(cells, wells)
        pressure = jnp.concatenate([p_out[0, j] for j in range(CY)], axis=0)
        table = ones_of(at_layer)
        picked = sum(jnp.dot(part, table, preferred_element_type=F32) for part in split3(pressure))
        values = jnp.sum(jnp.where(at_row, picked, 0.0), axis=0, keepdims=True)
        w = weights[...]
        sums, totals = row_times([w * values, w], ones_of(at_well), NT)
        tail = jnp.concatenate([sums, totals, jnp.zeros((6, W_ALL), F32)], axis=0)
        even = gx % 2 == 0
        low, high = edge[0], edge[1]
        msg_a[0:16, :] = jnp.where(even, high, low)
        msg_b[0:16, :] = jnp.where(even, low, high)
        msg_a[16:24, :] = tail
        msg_b[16:24, :] = tail

    return kernel


def apply_operator(got, cells, wells, weights):
    gx = position()[0]
    got_a, sent_b, got_c, got_b, got_d = got
    tail = sent_b[16:24, :] + got_b[16:24, :] + got_c[...] + got_d[...]
    rates = tail[0:1] / jnp.maximum(tail[1:2], 1.0)
    at_row, at_layer, at_well = slot_tables(cells, wells)
    slot_rate = row_times([rates], ones_of(at_well), (((1,), (0,)), ((), ())))[0]
    added = jnp.where(at_layer, weights[...] * slot_rate, 0.0)
    table = ones_of(at_row)
    well_add = sum(lax.dot_general(table, part, NT, preferred_element_type=F32) for part in split3(added))
    even = gx % 2 == 0
    halo_a, halo_b = got_a[0:16, :], got_b[0:16, :]
    from_after = jnp.where(gx < N_GX - 1, jnp.where(even, halo_a, halo_b), 0.0)
    from_before = jnp.where(gx > 0, jnp.where(even, halo_b, halo_a), 0.0)
    return well_add, from_after, from_before


def operator_plane(c, j, p, ends, dmat, tx, ty, tz, lx_in, ly_in, halo, well_add):
    from_after, from_before = halo
    here = p[c, j]
    up = p[c, j + 1] if j < CY - 1 else ends[2 + c]
    down = p[c, j - 1] if j > 0 else ends[c]
    t = tx[c, j]
    at = c * CY + j
    beside = t * from_row_after(here, from_after[at : at + 1])
    beside = beside + from_row_before(t * here, lx_in[c, j : j + 1, :] * from_before[at : at + 1])
    beside = beside + ty[c, j] * up + (ty[c, j - 1] if j else ly_in[c]) * down
    tzp = tz[c, j]
    beside = beside + tzp * pltpu.roll(here, NZ - 1, 1) + pltpu.roll(tzp * here, 1, 1)
    out = dmat[2 * c, j] * p[0, j] + dmat[2 * c + 1, j] * p[1, j] - beside
    if c == 0:
        out = out + well_add[j * CX : (j + 1) * CX]
    return out


def first_image_kernel(got_a, sent_b, got_c, got_b, got_d, p, ends, dmat, tau_r, sinv, binv, rhs, tx, ty, tz, lx_in, ly_in, cells, wells, weights, q_out, e_out, vec_out, dots):
    well_add, after, before = apply_operator((got_a, sent_b, got_c, got_b, got_d), cells, wells, weights)
    eq = jnp.zeros(PLANE, F32)
    qq = jnp.zeros(PLANE, F32)
    e = []
    for j in range(CY):
        pair = []
        for c in range(2):
            q = operator_plane(c, j, p, ends, dmat, tx, ty, tz, lx_in, ly_in, (after, before), well_add)
            rest = rhs[c, j] - q
            q_out[c, j] = q
            e_out[c, j] = rest
            eq = eq + rest * q
            qq = qq + q * q
            pair.append(rest)
        e.append(tuple(pair))
    dots[0] = eq
    dots[1] = qq

    def tau(j):
        return pair_at(tau_r, j)

    y = sweep_forward(lambda j: block_at(sinv, j), tau, e)[CY - 1]
    z = sweep_backward(lambda j: block_at(binv, j), tau, e)
    first = mv(block_at(binv, 0), z)
    last = mv(block_at(sinv, CY - 1), y)
    for c in range(2):
        vec_out[c] = first[c]
        vec_out[2 + c] = last[c]


def second_image_kernel(got_a, sent_b, got_c, got_b, got_d, p, ends, dmat, tx, ty, tz, lx_in, ly_in, cells, wells, weights, q_in, e_in, dots_in, s_out, dots):
    well_add, after, before = apply_operator((got_a, sent_b, got_c, got_b, got_d), cells, wells, weights)
    sq = jnp.zeros(PLANE, F32)
    ss = jnp.zeros(PLANE, F32)
    es = jnp.zeros(PLANE, F32)
    for j in range(CY):
        for c in range(2):
            s = operator_plane(c, j, p, ends, dmat, tx, ty, tz, lx_in, ly_in, (after, before), well_add)
            s_out[c, j] = s
            sq = sq + s * q_in[c, j]
            ss = ss + s * s
            es = es + s * e_in[c, j]
    sums = [jnp.sum(x, axis=0, keepdims=True) for x in (dots_in[0], dots_in[1], sq, ss, es)]
    lane = lax.broadcasted_iota(jnp.int32, (1, NZ), 1)
    row = jnp.zeros((1, NZ), F32)
    for i, x in enumerate(sums):
        row = jnp.where(lane == i, jnp.sum(x, axis=1, keepdims=True), row)
    dots[...] = row


def finish_kernel(got, p, w, q, e, s, x_out, r_out):
    total = jnp.sum(got[...], axis=0, keepdims=True)
    lane = lax.broadcasted_iota(jnp.int32, (1, NZ), 1)
    eq, qq, sq, ss, es = (
        jnp.broadcast_to(jnp.sum(jnp.where(lane == i, total, 0.0), axis=1, keepdims=True), (1, NZ)) for i in range(5)
    )
    rest = -eq / qq
    g = sq / qq
    k = (es - g * eq) / (ss - g * sq)
    on_p = (1.0 - rest) - k * g
    on_q = rest + k * g
    for c in range(2):
        for j in range(CY):
            at = pl.ds(j, CX, stride=CY)
            x_out.at[c][at, :] = on_p * p[c, j] + k * w[c, j]
            r_out.at[c][at, :] = e[c, j] + on_q * q[c, j] - k * s[c, j]


def call(kernel, name, outs, scratch, *args, specs=None, vmem=24 * 1024):
    outs = [o if isinstance(o, jax.ShapeDtypeStruct) else jax.ShapeDtypeStruct(o, F32) for o in outs]
    return pl.pallas_call(
        kernel,
        name=name,
        out_shape=tuple(outs),
        in_specs=specs or [VMEM] * len(args),
        out_specs=tuple(VMEM for _ in outs),
        scratch_shapes=[pltpu.VMEM(s, F32) if isinstance(s, tuple) else s for s in scratch],
        compiler_params=pltpu.CompilerParams(vmem_limit_bytes=vmem * 1024),
    )(*args)


def swapped(block, stride):
    others = [lax.ppermute(block, "gy", [(i, i ^ (k * stride)) for i in range(N_GY)]) for k in PARTNERS[1:]]
    return [block] + others


def exchange_rows(msg_a, msg_b):
    got_a = lax.ppermute(msg_a, "gx", [(i, i ^ 1) for i in range(N_GX)])
    below = lax.broadcasted_iota(jnp.int32, msg_b.shape, 0) >= 16
    tail = msg_b[16:] + got_a[16:]
    sent_b = msg_b + jnp.where(below, got_a, 0.0)
    got_d = lax.ppermute(tail, "gx", [(i, (i + 2 if i % 2 else i - 2) % N_GX) for i in range(N_GX)])
    got_b = lax.ppermute(sent_b, "gx", [(i, (i + 1 if i % 2 else i - 1) % N_GX) for i in range(N_GX)])
    got_c = lax.ppermute(tail, "gx", [(i, i ^ 4) for i in range(N_GX)])
    return got_a, sent_b, got_c, got_b, got_d


def sum_everywhere(x):
    x = x + lax.ppermute(x, "gx", [(i, i ^ 1) for i in range(N_GX)])
    others = [lax.ppermute(x, "gx", [(i, (i + 2 * k) % N_GX) for i in range(N_GX)]) for k in PARTNERS[1:]]
    x = x + others[0] + others[1] + others[2]
    for stride in (1, 4):
        x, *others = swapped(x, stride)
        x = x + others[0] + others[1] + others[2]
    return x


def body(right_side, accumulation, trans_x, trans_y, trans_z, perf_cell, perf_well, perf_weight, perf_count, breaks):

    def flat(a):
        return a.reshape(a.shape[0], CX * CY, NZ)

    field, block, part = (2, CY, CX, NZ), (4, CY, CX, NZ), (2, CY + 1, CX, NZ)
    half, vec, message = (20, 8, NZ), (4, CX, NZ), (24, NZ)
    order = [(4, 16, CX, NZ), (4, 4, CX, NZ)]
    two, four = (2, CX * CY, NZ), (4, CX * CY, NZ)
    sx, edge = call(
        edges_kernel, "edges", ((2, CY, NZ), (40, NZ)),
        [two, pltpu.VMEM((1, NZ), jnp.int32), pltpu.SemaphoreType.DMA((4,))],
        flat(trans_x), flat(trans_y), breaks, specs=[HBM] * 3, vmem=EDGES_VMEM,
    )
    rhs, tx, ty, tz, diag, cross = call(
        prepare_kernel, "prepare", (field,) * 6,
        [two, four, two, two, two, pltpu.SemaphoreType.DMA((5,))],
        flat(right_side), flat(accumulation), flat(trans_x), flat(trans_y), flat(trans_z),
        specs=[HBM] * 5, vmem=PREPARE_VMEM,
    )
    edges = swapped(edge, 1)
    lx = lax.ppermute(sx, "gx", [(i, i + 1) for i in range(N_GX - 1)])
    *edges, lx = lax.optimization_barrier((*edges, lx))
    relayed = swapped(relay(*edges), 4)
    slots = perf_cell.shape[3]
    live = jnp.arange(slots, dtype=jnp.int32)[None, :] < perf_count.reshape(N_GX, 1)
    weights = jnp.where(live, perf_weight.reshape(N_GX, slots), 0.0).reshape(1, SLOTS_ALL)
    owners = jnp.arange(N_GX, dtype=jnp.int32)[:, None] * 16
    wells = (perf_well.reshape(N_GX, slots) + owners).reshape(1, SLOTS_ALL)
    cells = perf_cell.reshape(1, SLOTS_ALL)
    perfs = (cells, wells, weights)

    own_a, own_b, dmat, tau, sinv, binv, ly = call(
        condense_kernel, "condense", (half, half, block, part, block, block, (2, CX, NZ)),
        [(N_GY, NZ), (4, 2 * CX, NZ), (4, 2 * CX, NZ)], diag, cross, ty, rhs, lx, *edges, *relayed,
    )
    inner, outer = [], []
    for own in (own_a, own_b):
        inner.append(swapped(own, 1))
    for near in inner:
        (group,) = call(total_half_kernel, "group_total", (half,), [(4,) + half], *near)
        outer.append(swapped(group, 4))
    inner = inner[0] + inner[1]
    outer = outer[0] + outer[1]
    solve_scratch = order + [(16, CX, NZ), (4, CX, NZ), (2, 16, NZ)]
    joined = (20, CX, NZ)
    left, right, base, from_left, from_right = call(
        make_inner_kernel(True), "inner_first", (joined, joined, field, block, block), order, *inner, sinv, tau, rhs,
    )
    owns = (own_a, own_b)
    p, ends, msg_a, msg_b = call(
        make_solve_kernel(True), "solve_first", (field, vec, message, message), solve_scratch,
        *owns, *outer, left, right, base, from_left, from_right, *perfs,
    )
    got = exchange_rows(msg_a, msg_b)
    q, e, own_v, dots = call(
        first_image_kernel, "first_image", (field, field, vec, (2, CX, NZ)), [],
        *got, p, ends, dmat, tau, sinv, binv, rhs, tx, ty, tz, lx, ly, *perfs,
    )
    inner_v = swapped(own_v, 1)
    (group_v,) = call(total_again_kernel, "group_total_again", (vec,), order, *inner, *inner_v)
    outer_v = swapped(group_v, 4)
    left, right, base = call(
        make_inner_kernel(False), "inner_second", (joined, joined, field), order, *inner, *inner_v, sinv, tau, e,
    )
    w, ends, msg_a, msg_b = call(
        make_solve_kernel(False), "solve_second", (field, vec, message, message), solve_scratch,
        *owns, *outer, own_v, *outer_v, left, right, base, from_left, from_right, *perfs,
    )
    got = exchange_rows(msg_a, msg_b)
    s, dots = call(
        second_image_kernel, "second_image", (field, (1, NZ)), [],
        *got, w, ends, dmat, tx, ty, tz, lx, ly, *perfs, q, e, dots,
    )
    dots = sum_everywhere(dots)
    x, r = call(finish_kernel, "finish", (two, two), [], dots, p, w, q, e, s)
    shape = (2, CX, CY, NZ)
    return x.reshape(shape), r.reshape(shape)


def solution(mesh):
    tile = P(None, "gx", "gy", None)
    slots = P("gx", "gy", None, None)
    return jax.shard_map(
        body,
        mesh=mesh,
        in_specs=(tile,) * 5 + (slots,) * 3 + (P("gx", "gy", None), P(("gx", "gy"), None)),
        out_specs=(tile, tile),
        check_vma=False,
    )
```

```python
import jax
import jax.numpy as jnp
from jax import lax
from jax.experimental import pallas as pl
from jax.experimental.pallas import tpu as pltpu
from jax.sharding import PartitionSpec as P

F32 = jnp.float32
BF16 = jnp.bfloat16
VMEM = pl.BlockSpec(memory_space=pltpu.VMEM)
HBM = pl.BlockSpec(memory_space=pltpu.HBM)
SMEM = pl.BlockSpec(memory_space=pltpu.SMEM)
CX, CY, NZ = 16, 8, 128
PLANE = (CX, NZ)
N_GX, N_GY = 8, 16
W_ALL = 128
PARTNERS = (0, 3, 2, 1)
PREPARE_VMEM = 54400
EDGES_VMEM = 55296
SLOTS_ALL = 256


def mm(p, q):
    return (
        p[0] * q[0] + p[1] * q[2],
        p[0] * q[1] + p[1] * q[3],
        p[2] * q[0] + p[3] * q[2],
        p[2] * q[1] + p[3] * q[3],
    )


def mv(p, v):
    return (p[0] * v[0] + p[1] * v[1], p[2] * v[0] + p[3] * v[1])


def madd(p, q):
    return tuple(a + b for a, b in zip(p, q))


def inv2(p):
    t = 1.0 / (p[0] * p[3] - p[1] * p[2])
    return (p[3] * t, -p[1] * t, -p[2] * t, p[0] * t)


def one_minus(p):
    return (1.0 - p[0], -p[1], -p[2], 1.0 - p[3])


def rows_by(t, p):
    return (t[0] * p[0], t[0] * p[1], t[1] * p[2], t[1] * p[3])


def columns_by(p, t):
    return (p[0] * t[0], p[1] * t[1], p[2] * t[0], p[3] * t[1])


def join(a, b):
    ff1, fl1, lf1, ll1, gf1, gl1 = a
    ff2, fl2, lf2, ll2, gf2, gl2 = b
    k = inv2(one_minus(mm(ll1, ff2)))
    last = mv(k, madd(gl1, mv(ll1, gf2)))
    last_b = mm(k, lf1)
    last_a = mm(k, mm(ll1, fl2))
    first = madd(gf2, mv(ff2, last))
    first_b = mm(ff2, last_b)
    first_a = madd(fl2, mm(ff2, last_a))
    return (
        madd(ff1, mm(fl1, first_b)),
        mm(fl1, first_a),
        mm(lf2, last_b),
        madd(ll2, mm(lf2, last_a)),
        madd(gf1, mv(fl1, first)),
        madd(gl2, mv(lf2, last)),
    )


def join_before(before, s):
    gm, g = before
    ff, fl, lf, ll, gf, gl = s
    k = inv2(one_minus(mm(ff, gm)))
    a = mv(k, madd(gf, mv(ff, g)))
    am = mm(k, fl)
    return (madd(ll, mm(lf, mm(gm, am))), madd(gl, mv(lf, madd(g, mv(gm, a)))))


def join_after(s, after):
    gm, g = after
    ff, fl, lf, ll, gf, gl = s
    k = inv2(one_minus(mm(ll, gm)))
    a = mv(k, madd(gl, mv(ll, g)))
    am = mm(k, lf)
    return (madd(ff, mm(fl, mm(gm, am))), madd(gf, mv(fl, madd(g, mv(gm, a)))))


def position():
    return lax.axis_index("gx"), lax.axis_index("gy")


def choose(flag, new, old):
    return tuple(tuple(jnp.where(flag, n, o) for n, o in zip(ns, os)) for ns, os in zip(new, old))


def load_segment(mat, vec, offset):
    m = [mat[i] for i in range(16)]
    v = [vec[offset + i] for i in range(4)]
    return (tuple(m[0:4]), tuple(m[4:8]), tuple(m[8:12]), tuple(m[12:16]), (v[0], v[1]), (v[2], v[3]))


def store_segment(ref, seg, whole):
    flat = [x for part in seg for x in part]
    if not whole:
        flat = flat[16:]
    for i, x in enumerate(flat):
        ref[i] = x


def lanes():
    return lax.broadcasted_iota(jnp.int32, PLANE, 1)


def rows():
    return lax.broadcasted_iota(jnp.int32, PLANE, 0)


def from_row_before(plane, edge):
    return jnp.where(rows() == 0, edge, pltpu.roll(plane, 1, 0))


def from_row_after(plane, edge):
    return jnp.where(rows() == CX - 1, edge, pltpu.roll(plane, CX - 1, 0))


def sweep_forward(sinv, tau, rhs):
    y = [rhs[0]]
    for j in range(1, CY):
        t = mv(sinv(j - 1), y[-1])
        y.append((rhs[j][0] + tau(j)[0] * t[0], rhs[j][1] + tau(j)[1] * t[1]))
    return y


def sweep_backward(binv, tau, rhs):
    z = rhs[CY - 1]
    for j in range(CY - 2, -1, -1):
        t = mv(binv(j + 1), z)
        z = (rhs[j][0] + tau(j + 1)[0] * t[0], rhs[j][1] + tau(j + 1)[1] * t[1])
    return z


def block_at(ref, j):
    return tuple(ref[i, j] for i in range(4))


def pair_at(ref, j):
    return (ref[0, j], ref[1, j])


def plane(ref, c, j):
    return ref.at[c][pl.ds(j, CX, stride=CY), :]


def edges_kernel(tx_h, ty_h, brk_h, sx, edge, ty, brk, sems):
    copies = [pltpu.make_async_copy(h, v, sems.at[i]) for i, (h, v) in enumerate(((ty_h, ty), (brk_h, brk)))]
    copies += [
        pltpu.make_async_copy(tx_h.at[c, (CX - 1) * CY : CX * CY, :], sx.at[c], sems.at[2 + c]) for c in range(2)
    ]
    for copy in copies:
        copy.start()
    for copy in copies:
        copy.wait()
    edge[2 * CX :, :] = jnp.broadcast_to(brk[...].astype(F32), (8, NZ))
    for c in range(2):
        edge[c * CX : (c + 1) * CX, :] = plane(ty, c, CY - 1)


def relay(*messages):
    z = position()[1] % 4
    row = lax.broadcasted_iota(jnp.int32, messages[0].shape, 0)
    out = jnp.zeros_like(messages[0])
    for k, ref in enumerate(messages):
        out = jnp.where(jnp.where(row < 2 * CX, z == 3 - PARTNERS[k], row == 2 * CX + k), ref, out)
    return out


def prepare_kernel(b_h, acc_h, tx_h, ty_h, tz_h, rhs, tx_o, ty_o, tz_o, diag, cross, b, acc, tx_v, ty_v, tz_v, sems):
    gx, gy = position()
    pairs = ((tx_h, tx_v), (ty_h, ty_v), (tz_h, tz_v), (acc_h, acc), (b_h, b))
    copies = [pltpu.make_async_copy(h, v, sems.at[i]) for i, (h, v) in enumerate(pairs)]
    for copy in copies:
        copy.start()
    last_x = jnp.logical_and(rows() == CX - 1, gx == N_GX - 1)
    last_z = lanes() == NZ - 1
    for copy in copies:
        copy.wait()
    for c in range(2):
        ly = 0.0
        for j in range(CY):
            tx = jnp.where(last_x, 0.0, plane(tx_v, c, j))
            tz = jnp.where(last_z, 0.0, plane(tz_v, c, j))
            ty = plane(ty_v, c, j)
            if j == CY - 1:
                ty = jnp.where(gy == N_GY - 1, 0.0, ty)
            tx_o[c, j] = tx
            tz_o[c, j] = tz
            ty_o[c, j] = ty
            faces = tx + from_row_before(tx, 0.0) + ty + ly + tz + pltpu.roll(tz, 1, 1)
            diag[c, j] = plane(acc, 3 * c, j) + faces
            cross[c, j] = plane(acc, 2 - c, j)
            rhs[c, j] = plane(b, c, j)
            ly = ty


def condense_kernel(diag, cross, ty, rhs, lx_in, *refs):
    messages, relayed = refs[:4], refs[4:8]
    seg_a, seg_b, dmat, tau_o, sinv, binv, ly_in = refs[8:15]
    brk, near, far = refs[15:]
    gy = position()[1]
    z_at, y_at = gy % 4, gy // 4
    for k in range(4):
        near[jnp.bitwise_xor(z_at, PARTNERS[k])] = messages[k][0 : 2 * CX, :]
        at = jnp.bitwise_xor(y_at, PARTNERS[k])
        far[at] = relayed[k][0 : 2 * CX, :]
        for i in range(4):
            row = relayed[k][2 * CX + i : 2 * CX + i + 1, :]
            brk[pl.ds(4 * at + jnp.bitwise_xor(z_at, PARTNERS[i]), 1), :] = row
    cuts = pltpu.roll(brk[...], (NZ - CY * gy) % NZ, 1)
    before = jnp.where(y_at > 0, far[jnp.maximum(y_at - 1, 0)], 0.0)
    before = jnp.where(z_at > 0, near[jnp.maximum(z_at - 1, 0)], before)
    for c in range(2):
        ly_in[c] = before[c * CX : (c + 1) * CX]
    for c in range(2):
        ly = ly_in[c]
        for j in range(CY):
            d = diag[c, j] + jnp.where(rows() == 0, lx_in[c, j : j + 1, :], 0.0)
            dmat[3 * c, j] = d + ly if j == 0 else d
        for j in range(CY + 1):
            keep = 1.0 - cuts[:, j : j + 1]
            tau_o[c, j] = (ty[c, j - 1] if j else ly) * keep
    for j in range(CY):
        dmat[1, j] = cross[0, j]
        dmat[2, j] = cross[1, j]

    def tau(j):
        return pair_at(tau_o, j)

    def outer(t, p):
        return tuple(x * y for x, y in zip(p, (t[0] * t[0], t[0] * t[1], t[1] * t[0], t[1] * t[1])))

    s = inv2(block_at(dmat, 0))
    e = inv2(block_at(dmat, CY - 1))
    zero = jnp.zeros(PLANE, F32)
    yf = (tau(0)[0], zero, zero, tau(0)[1])
    zl = (tau(CY)[0], zero, zero, tau(CY)[1])
    y = pair_at(rhs, 0)
    z = pair_at(rhs, CY - 1)
    for i in range(4):
        sinv[i, 0] = s[i]
        binv[i, CY - 1] = e[i]
    for j in range(1, CY):
        k = CY - 1 - j
        t, u = tau(j), tau(k + 1)
        yf = rows_by(t, mm(s, yf))
        zl = rows_by(u, mm(e, zl))
        yv, zv = mv(s, y), mv(e, z)
        y = tuple(rhs[c, j] + t[c] * yv[c] for c in range(2))
        z = tuple(rhs[c, k] + u[c] * zv[c] for c in range(2))
        s = inv2(tuple(d - x for d, x in zip(block_at(dmat, j), outer(t, s))))
        e = inv2(tuple(d - x for d, x in zip(block_at(dmat, k), outer(u, e))))
        for i in range(4):
            sinv[i, j] = s[i]
            binv[i, k] = e[i]
    whole = (columns_by(e, tau(0)), mm(e, zl), mm(s, yf), columns_by(s, tau(CY)), mv(e, z), mv(s, y))
    for half, ref in enumerate((seg_a, seg_b)):
        store_segment(ref, [[x[8 * half : 8 * half + 8] for x in part] for part in whole], True)


def gather_matrices(at_place, halves, mat_s):
    for k in range(4):
        at = jnp.bitwise_xor(at_place, PARTNERS[k])
        for half, refs in enumerate(halves):
            mat_s[at, :, 8 * half : 8 * half + 8, :] = refs[k][0:16]


def gather_vectors(at_place, vecs, vec_s):
    for k in range(4):
        vec_s[jnp.bitwise_xor(at_place, PARTNERS[k])] = vecs[k][...]


def gather_both(at_place, halves, mat_s, vec_s):
    gather_matrices(at_place, halves, mat_s)
    for k in range(4):
        at = jnp.bitwise_xor(at_place, PARTNERS[k])
        for half, refs in enumerate(halves):
            vec_s[at, :, 8 * half : 8 * half + 8, :] = refs[k][16:20]


def total_half_kernel(own, m1, m2, m3, out, segs_s):
    for k, ref in enumerate((own, m1, m2, m3)):
        segs_s[jnp.bitwise_xor(position()[1] % 4, PARTNERS[k])] = ref[...]
    segs = [load_segment(segs_s.at[m], segs_s.at[m], 16) for m in range(4)]
    store_segment(out, join(join(segs[0], segs[1]), join(segs[2], segs[3])), True)


def total_again_kernel(*refs):
    halves, vecs = (refs[0:4], refs[4:8]), refs[8:12]
    out, mat_s, vec_s = refs[12:]
    gather_matrices(position()[1] % 4, halves, mat_s)
    gather_vectors(position()[1] % 4, vecs, vec_s)
    segs = [load_segment(mat_s.at[m], vec_s.at[m], 0) for m in range(4)]
    store_segment(out, join(join(segs[0], segs[1]), join(segs[2], segs[3])), False)


def split3(x):
    hi = x.astype(BF16)
    rest = x - hi.astype(F32)
    mid = rest.astype(BF16)
    low = (rest - mid.astype(F32)).astype(BF16)
    return hi, mid, low


def slot_tables(cells, wells):
    cell = cells[...]
    row = jnp.bitwise_and(lax.shift_right_logical(cell, 7), 7) * CX + lax.shift_right_logical(cell, 10)
    shape = (NZ, SLOTS_ALL)
    up = lax.broadcasted_iota(jnp.int32, shape, 0)
    at_row = up == row
    at_layer = up == jnp.bitwise_and(cell, NZ - 1)
    at_well = up == wells[...]
    return at_row, at_layer, at_well


def ones_of(mask):
    return jnp.where(mask, 1.0, 0.0).astype(F32).astype(BF16)


NT = (((1,), (1,)), ((), ()))


def row_times(rows_in, table, dims):
    parts = [part for x in rows_in for part in split3(x)]
    n = len(rows_in)
    pad = 16 - 3 * n
    width = rows_in[0].shape[1]
    stacked = jnp.concatenate([p.astype(F32) for p in parts] + [jnp.zeros((pad, width), F32)], axis=0).astype(BF16)
    out = lax.dot_general(stacked, table, dims, preferred_element_type=F32)
    return [out[3 * i : 3 * i + 1] + out[3 * i + 1 : 3 * i + 2] + out[3 * i + 2 : 3 * i + 3] for i in range(n)]


def make_inner_kernel(whole):
    def kernel(*refs):
        halves = (refs[0:4], refs[4:8])
        vecs, rest = (None, refs[8:]) if whole else (refs[8:12], refs[12:])
        if whole:
            sinv, tau_r, rhs, left, right, base, from_left, from_right, mat_s, vec_s = rest
        else:
            sinv, tau_r, rhs, left, right, base, mat_s, vec_s = rest
        z = position()[1] % 4
        if whole:
            gather_both(z, halves, mat_s, vec_s)
        else:
            gather_matrices(z, halves, mat_s)
            gather_vectors(z, vecs, vec_s)
        segs = [load_segment(mat_s.at[m], vec_s.at[m], 0) for m in range(4)]
        pair = join(segs[0], segs[1])
        store_segment(left, choose(z == 1, segs[0], choose(z == 2, pair, join(pair, segs[2]))), True)
        pair = join(segs[2], segs[3])
        store_segment(right, choose(z == 2, segs[3], choose(z == 1, pair, join(segs[1], pair))), True)

        def tau(j):
            return pair_at(tau_r, j)

        def sv(j):
            return block_at(sinv, j)

        y = sweep_forward(sv, tau, [pair_at(rhs, j) for j in range(CY)])
        u = None
        for j in range(CY - 1, -1, -1):
            v = y[j] if u is None else tuple(y[j][c] + tau(j + 1)[c] * u[c] for c in range(2))
            u = mv(sv(j), v)
            for c in range(2):
                base[c, j] = u[c]
        if not whole:
            return
        zero = jnp.zeros(PLANE, F32)
        units = [(tau(0)[0], zero, zero, tau(0)[1])]
        for j in range(1, CY):
            units.append(rows_by(tau(j), mm(sv(j - 1), units[-1])))
        ul = ur = None
        for j in range(CY - 1, -1, -1):
            if ul is None:
                ul = mm(sv(j), units[j])
                ur = columns_by(sv(j), tau(CY))
            else:
                ul = mm(sv(j), madd(units[j], rows_by(tau(j + 1), ul)))
                ur = mm(sv(j), rows_by(tau(j + 1), ur))
            for i in range(4):
                from_left[i, j] = ul[i]
                from_right[i, j] = ur[i]

    return kernel


def make_solve_kernel(whole):
    def kernel(*refs):
        own_m, outer = refs[0:2], (refs[2:6], refs[6:10])
        own_v, outer_v, rest = (None, None, refs[10:]) if whole else (refs[10], refs[11:15], refs[15:])
        left, right, base, from_left, from_right, cells, wells, weights = rest[:8]
        p_out, ends, msg_a, msg_b = rest[8:12]
        mat_o, vec_o, mat_i, vec_i, edge = rest[12:]
        gx, gy = position()
        z_at, y_at = gy % 4, gy // 4
        for half, ref in enumerate(own_m):
            mat_i[:, 8 * half : 8 * half + 8, :] = ref[0:16]
            if whole:
                vec_i[:, 8 * half : 8 * half + 8, :] = ref[16:20]
        if whole:
            gather_both(y_at, outer, mat_o, vec_o)
        else:
            vec_i[...] = own_v[...]
            gather_matrices(y_at, outer, mat_o)
            gather_vectors(y_at, outer_v, vec_o)
        zero = jnp.zeros(PLANE, F32)
        before = ((zero,) * 4, (zero,) * 2)
        after = ((zero,) * 4, (zero,) * 2)
        for m in range(3):
            seg = load_segment(mat_o.at[m], vec_o.at[m], 0)
            before = choose(m < y_at, join_before(before, seg), before)
            m = 3 - m
            seg = load_segment(mat_o.at[m], vec_o.at[m], 0)
            after = choose(m > y_at, join_after(seg, after), after)
        before = choose(z_at > 0, join_before(before, load_segment(left, left, 16)), before)
        after = choose(z_at < 3, join_after(load_segment(right, right, 16), after), after)
        own = load_segment(mat_i, vec_i, 0)
        ff, fl, lf, ll, gf, gl = own
        up_m, up_v = join_before(before, own)
        last = mv(inv2(one_minus(mm(up_m, after[0]))), madd(up_v, mv(up_m, after[1])))
        beyond = madd(after[1], mv(after[0], last))
        k = inv2(one_minus(mm(ff, before[0])))
        first = mv(k, madd(madd(gf, mv(ff, before[1])), mv(fl, beyond)))
        behind = madd(before[1], mv(before[0], first))
        for c in range(2):
            ends[c] = behind[c]
            ends[2 + c] = beyond[c]

        for j in range(CY):
            u = madd(pair_at(base, j), madd(mv(block_at(from_left, j), behind), mv(block_at(from_right, j), beyond)))
            for c in range(2):
                p_out[c, j] = u[c]
                edge[0, c * CY + j : c * CY + j + 1, :] = u[c][0:1, :]
                edge[1, c * CY + j : c * CY + j + 1, :] = u[c][CX - 1 : CX, :]
        at_row, at_layer, at_well = slot_tables(cells, wells)
        pressure = jnp.concatenate([p_out[0, j] for j in range(CY)], axis=0)
        table = ones_of(at_layer)
        picked = sum(jnp.dot(part, table, preferred_element_type=F32) for part in split3(pressure))
        values = jnp.sum(jnp.where(at_row, picked, 0.0), axis=0, keepdims=True)
        w = weights[...]
        sums, totals = row_times([w * values, w], ones_of(at_well), NT)
        tail = jnp.concatenate([sums, totals, jnp.zeros((6, W_ALL), F32)], axis=0)
        even = gx % 2 == 0
        low, high = edge[0], edge[1]
        msg_a[0:16, :] = jnp.where(even, high, low)
        msg_b[0:16, :] = jnp.where(even, low, high)
        msg_a[16:24, :] = tail
        msg_b[16:24, :] = tail

    return kernel


def apply_operator(got, cells, wells, weights):
    gx = position()[0]
    got_a, sent_b, got_c, got_b, got_d = got
    tail = sent_b[16:24, :] + got_b[16:24, :] + got_c[...] + got_d[...]
    rates = tail[0:1] / jnp.maximum(tail[1:2], 1.0)
    at_row, at_layer, at_well = slot_tables(cells, wells)
    slot_rate = row_times([rates], ones_of(at_well), (((1,), (0,)), ((), ())))[0]
    added = jnp.where(at_layer, weights[...] * slot_rate, 0.0)
    table = ones_of(at_row)
    well_add = sum(lax.dot_general(table, part, NT, preferred_element_type=F32) for part in split3(added))
    even = gx % 2 == 0
    halo_a, halo_b = got_a[0:16, :], got_b[0:16, :]
    from_after = jnp.where(gx < N_GX - 1, jnp.where(even, halo_a, halo_b), 0.0)
    from_before = jnp.where(gx > 0, jnp.where(even, halo_b, halo_a), 0.0)
    return well_add, from_after, from_before


def operator_plane(c, j, p, ends, dmat, tx, ty, tz, lx_in, ly_in, halo, well_add):
    from_after, from_before = halo
    here = p[c, j]
    up = p[c, j + 1] if j < CY - 1 else ends[2 + c]
    down = p[c, j - 1] if j > 0 else ends[c]
    t = tx[c, j]
    at = c * CY + j
    beside = t * from_row_after(here, from_after[at : at + 1])
    beside = beside + from_row_before(t * here, lx_in[c, j : j + 1, :] * from_before[at : at + 1])
    beside = beside + ty[c, j] * up + (ty[c, j - 1] if j else ly_in[c]) * down
    tzp = tz[c, j]
    beside = beside + tzp * pltpu.roll(here, NZ - 1, 1) + pltpu.roll(tzp * here, 1, 1)
    out = dmat[2 * c, j] * p[0, j] + dmat[2 * c + 1, j] * p[1, j] - beside
    if c == 0:
        out = out + well_add[j * CX : (j + 1) * CX]
    return out


def first_image_kernel(got_a, sent_b, got_c, got_b, got_d, p, ends, dmat, tau_r, sinv, binv, rhs, tx, ty, tz, lx_in, ly_in, cells, wells, weights, q_out, e_out, vec_out, dots):
    well_add, after, before = apply_operator((got_a, sent_b, got_c, got_b, got_d), cells, wells, weights)
    eq = jnp.zeros(PLANE, F32)
    qq = jnp.zeros(PLANE, F32)
    e = []
    for j in range(CY):
        pair = []
        for c in range(2):
            q = operator_plane(c, j, p, ends, dmat, tx, ty, tz, lx_in, ly_in, (after, before), well_add)
            rest = rhs[c, j] - q
            q_out[c, j] = q
            e_out[c, j] = rest
            eq = eq + rest * q
            qq = qq + q * q
            pair.append(rest)
        e.append(tuple(pair))
    dots[0] = eq
    dots[1] = qq

    def tau(j):
        return pair_at(tau_r, j)

    y = sweep_forward(lambda j: block_at(sinv, j), tau, e)[CY - 1]
    z = sweep_backward(lambda j: block_at(binv, j), tau, e)
    first = mv(block_at(binv, 0), z)
    last = mv(block_at(sinv, CY - 1), y)
    for c in range(2):
        vec_out[c] = first[c]
        vec_out[2 + c] = last[c]


def second_image_kernel(got_a, sent_b, got_c, got_b, got_d, p, ends, dmat, tx, ty, tz, lx_in, ly_in, cells, wells, weights, q_in, e_in, dots_in, s_out, dots):
    well_add, after, before = apply_operator((got_a, sent_b, got_c, got_b, got_d), cells, wells, weights)
    sq = jnp.zeros(PLANE, F32)
    ss = jnp.zeros(PLANE, F32)
    es = jnp.zeros(PLANE, F32)
    for j in range(CY):
        for c in range(2):
            s = operator_plane(c, j, p, ends, dmat, tx, ty, tz, lx_in, ly_in, (after, before), well_add)
            s_out[c, j] = s
            sq = sq + s * q_in[c, j]
            ss = ss + s * s
            es = es + s * e_in[c, j]
    sums = [jnp.sum(x, axis=0, keepdims=True) for x in (dots_in[0], dots_in[1], sq, ss, es)]
    lane = lax.broadcasted_iota(jnp.int32, (1, NZ), 1)
    row = jnp.zeros((1, NZ), F32)
    for i, x in enumerate(sums):
        row = jnp.where(lane == i, jnp.sum(x, axis=1, keepdims=True), row)
    dots[...] = row


def finish_kernel(got, p, w, q, e, s, x_out, r_out):
    total = jnp.sum(got[...], axis=0, keepdims=True)
    lane = lax.broadcasted_iota(jnp.int32, (1, NZ), 1)
    eq, qq, sq, ss, es = (
        jnp.broadcast_to(jnp.sum(jnp.where(lane == i, total, 0.0), axis=1, keepdims=True), (1, NZ)) for i in range(5)
    )
    rest = -eq / qq
    g = sq / qq
    k = (es - g * eq) / (ss - g * sq)
    on_p = (1.0 - rest) - k * g
    on_q = rest + k * g
    for c in range(2):
        for j in range(CY):
            at = pl.ds(j, CX, stride=CY)
            x_out.at[c][at, :] = on_p * p[c, j] + k * w[c, j]
            r_out.at[c][at, :] = e[c, j] + on_q * q[c, j] - k * s[c, j]


def call(kernel, name, outs, scratch, *args, specs=None, vmem=24 * 1024):
    outs = [o if isinstance(o, jax.ShapeDtypeStruct) else jax.ShapeDtypeStruct(o, F32) for o in outs]
    return pl.pallas_call(
        kernel,
        name=name,
        out_shape=tuple(outs),
        in_specs=specs or [VMEM] * len(args),
        out_specs=tuple(VMEM for _ in outs),
        scratch_shapes=[pltpu.VMEM(s, F32) if isinstance(s, tuple) else s for s in scratch],
        compiler_params=pltpu.CompilerParams(vmem_limit_bytes=vmem * 1024),
    )(*args)


def swapped(block, stride):
    others = [lax.ppermute(block, "gy", [(i, i ^ (k * stride)) for i in range(N_GY)]) for k in PARTNERS[1:]]
    return [block] + others


def chips(step):
    return [(i, (i + step if i % 2 else i - step) % N_GX) for i in range(N_GX)]


def exchange_rows(msg_a, msg_b):
    got_a = lax.ppermute(msg_a, "gx", [(i, i ^ 1) for i in range(N_GX)])
    below = lax.broadcasted_iota(jnp.int32, msg_b.shape, 0) >= 16
    tail = msg_b[16:] + got_a[16:]
    sent_b = msg_b + jnp.where(below, got_a, 0.0)
    got_d = lax.ppermute(tail, "gx", chips(-3))
    got_b = lax.ppermute(sent_b, "gx", chips(1))
    got_c = lax.ppermute(tail, "gx", chips(4))
    return got_a, sent_b, got_c, got_b, got_d


def sum_everywhere(x):
    x = x + lax.ppermute(x, "gx", [(i, i ^ 1) for i in range(N_GX)])
    others = [lax.ppermute(x, "gx", chips(step)) for step in (-3, 4, 1)]
    x = x + others[0] + others[1] + others[2]
    x = jnp.broadcast_to(x, (N_GY, NZ))
    return lax.all_to_all(x, "gy", split_axis=0, concat_axis=0, tiled=True)


def body(right_side, accumulation, trans_x, trans_y, trans_z, perf_cell, perf_well, perf_weight, perf_count, breaks):

    def flat(a):
        return a.reshape(a.shape[0], CX * CY, NZ)

    field, block, part = (2, CY, CX, NZ), (4, CY, CX, NZ), (2, CY + 1, CX, NZ)
    half, vec, message = (20, 8, NZ), (4, CX, NZ), (24, NZ)
    order = [(4, 16, CX, NZ), (4, 4, CX, NZ)]
    two, four = (2, CX * CY, NZ), (4, CX * CY, NZ)
    sx, edge = call(
        edges_kernel, "edges", ((2, CY, NZ), (40, NZ)),
        [two, pltpu.VMEM((1, NZ), jnp.int32), pltpu.SemaphoreType.DMA((4,))],
        flat(trans_x), flat(trans_y), breaks, specs=[HBM] * 3, vmem=EDGES_VMEM,
    )
    rhs, tx, ty, tz, diag, cross = call(
        prepare_kernel, "prepare", (field,) * 6,
        [two, four, two, two, two, pltpu.SemaphoreType.DMA((5,))],
        flat(right_side), flat(accumulation), flat(trans_x), flat(trans_y), flat(trans_z),
        specs=[HBM] * 5, vmem=PREPARE_VMEM,
    )
    edges = swapped(edge, 1)
    lx = lax.ppermute(sx, "gx", [(i, i + 1) for i in range(N_GX - 1)])
    *edges, lx = lax.optimization_barrier((*edges, lx))
    relayed = swapped(relay(*edges), 4)
    slots = perf_cell.shape[3]
    live = jnp.arange(slots, dtype=jnp.int32)[None, :] < perf_count.reshape(N_GX, 1)
    weights = jnp.where(live, perf_weight.reshape(N_GX, slots), 0.0).reshape(1, SLOTS_ALL)
    owners = jnp.arange(N_GX, dtype=jnp.int32)[:, None] * 16
    wells = (perf_well.reshape(N_GX, slots) + owners).reshape(1, SLOTS_ALL)
    cells = perf_cell.reshape(1, SLOTS_ALL)
    perfs = (cells, wells, weights)

    own_a, own_b, dmat, tau, sinv, binv, ly = call(
        condense_kernel, "condense", (half, half, block, part, block, block, (2, CX, NZ)),
        [(N_GY, NZ), (4, 2 * CX, NZ), (4, 2 * CX, NZ)], diag, cross, ty, rhs, lx, *edges, *relayed,
    )
    inner, outer = [], []
    for own in (own_a, own_b):
        inner.append(swapped(own, 1))
    for near in inner:
        (group,) = call(total_half_kernel, "group_total", (half,), [(4,) + half], *near)
        outer.append(swapped(group, 4))
    inner = inner[0] + inner[1]
    outer = outer[0] + outer[1]
    solve_scratch = order + [(16, CX, NZ), (4, CX, NZ), (2, 16, NZ)]
    joined = (20, CX, NZ)
    left, right, base, from_left, from_right = call(
        make_inner_kernel(True), "inner_first", (joined, joined, field, block, block), order, *inner, sinv, tau, rhs,
    )
    owns = (own_a, own_b)
    p, ends, msg_a, msg_b = call(
        make_solve_kernel(True), "solve_first", (field, vec, message, message), solve_scratch,
        *owns, *outer, left, right, base, from_left, from_right, *perfs,
    )
    got = exchange_rows(msg_a, msg_b)
    q, e, own_v, dots = call(
        first_image_kernel, "first_image", (field, field, vec, (2, CX, NZ)), [],
        *got, p, ends, dmat, tau, sinv, binv, rhs, tx, ty, tz, lx, ly, *perfs,
    )
    inner_v = swapped(own_v, 1)
    (group_v,) = call(total_again_kernel, "group_total_again", (vec,), order, *inner, *inner_v)
    outer_v = swapped(group_v, 4)
    left, right, base = call(
        make_inner_kernel(False), "inner_second", (joined, joined, field), order, *inner, *inner_v, sinv, tau, e,
    )
    w, ends, msg_a, msg_b = call(
        make_solve_kernel(False), "solve_second", (field, vec, message, message), solve_scratch,
        *owns, *outer, own_v, *outer_v, left, right, base, from_left, from_right, *perfs,
    )
    got = exchange_rows(msg_a, msg_b)
    s, dots = call(
        second_image_kernel, "second_image", (field, (1, NZ)), [],
        *got, w, ends, dmat, tx, ty, tz, lx, ly, *perfs, q, e, dots,
    )
    dots = sum_everywhere(dots)
    x, r = call(finish_kernel, "finish", (two, two), [], dots, p, w, q, e, s)
    shape = (2, CX, CY, NZ)
    return x.reshape(shape), r.reshape(shape)


def solution(mesh):
    tile = P(None, "gx", "gy", None)
    slots = P("gx", "gy", None, None)
    return jax.shard_map(
        body,
        mesh=mesh,
        in_specs=(tile,) * 5 + (slots,) * 3 + (P("gx", "gy", None), P(("gx", "gy"), None)),
        out_specs=(tile, tile),
        check_vma=False,
    )
```
